256 devices in a mesh: event: 32 (over x, z), feat: 8 (over y, core).
Axes of the slice: x: 4, y: 4, z: 8, core: 2. Of those that a mesh axis runs over, the one named last changes fastest.
Arguments:
- events: bfloat16 [40960, 32768], P('event', 'feat')
- labels: int32 [40960], P('event'), may hold values 0 or 1
- weights: float32 [32768], P('feat'), may hold values from -6 to 6
- contexts: int32 [63], replicated, may hold values from 0 to 40959
Outputs:
- new_weights: float32 [32768], P('feat')
- widths: float32 [63], replicated
The draws below stay inside these ranges and needn't reach their ends.
All inputs are finite; a program needn't handle non-finite values. No bound on the sum of `labels` on one device may be relied on, other than what follows from the above.
Results may differ from the reference program's by a relative error of at most 0.0022.
Values may be sent and summed in bfloat16 or wider, within the bound.
No kernel may reach another device: no remote copies, remote signals or barrier semaphores. Data moves between devices by JAX's collectives and lax.ppermute only.
A program may use at most 64 MiB of HBM per device.

```python
import math
import jax
import jax.numpy as jnp
from jax import lax

F = 32768
NCAND = 63
ITERS = 2
RHS = 64
EVENTS = 40960


def draw_events(key, part):
    key = jax.random.fold_in(key, 11)
    key_rows = jax.random.fold_in(key, 0)
    key_cols = jax.random.fold_in(key, 1)
    key_base = jax.random.fold_in(key, 2)
    key_gain = jax.random.fold_in(key, 4)
    key_amp = jax.random.fold_in(key, 5)
    key_pattern = jax.random.fold_in(key, 6)
    row_scale = jnp.exp(jax.random.uniform(key_rows, (EVENTS, 1), jnp.float32, -1.15, 1.15))
    col_scale = jnp.exp(jax.random.uniform(key_cols, (1, F), jnp.float32, -1.15, 1.15))
    groups = max(1, EVENTS * 3 // 80)
    group_of = jnp.arange(F, dtype=jnp.int32) * groups // F
    gain = jax.random.uniform(key_gain, (EVENTS, 1), jnp.float32, 0.0, 1.5)
    pattern = jax.random.normal(key_pattern, (1, F), jnp.float32)
    base = jax.random.normal(key_base, (EVENTS, F), jnp.float32)
    amplitude = jax.random.normal(key_amp, (EVENTS, groups), jnp.float32)
    shared = jnp.take(amplitude, group_of, axis=1) * pattern
    values = (base + gain * shared) * row_scale * col_scale / (2.146 * math.sqrt(F))
    return values.astype(jnp.bfloat16)


def place_ends(drawn, rng, smallest, high):
    dims = drawn.shape
    place = [jax.random.randint(jax.random.fold_in(rng, axis), (), 0, dims[axis]) for axis in range(len(dims))]
    drawn = drawn.at[tuple(place)].set(smallest)
    longest = dims.index(max(dims))
    place[longest] = (place[longest] + 1) % dims[longest]
    return drawn.at[tuple(place)].set(high)


def level_of(rng, extent, pieces, least, top_value):
    level, own = 1.0, jax.random.fold_in(rng, 6)
    for position, shards_of in pieces:
        heights = jnp.exp(jax.random.uniform(jax.random.fold_in(own, position), (shards_of,), jnp.float32, least / len(pieces), top_value / len(pieces)))
        level = level * jnp.repeat(heights, extent[position] // shards_of).reshape([-1 if axis == position else 1 for axis in range(len(extent))])
    return level


def gaussian(stream_key, shape, spread, reach, pieces=(), kind=jnp.bfloat16):
    entries = jax.random.normal(stream_key, shape, jnp.float32) * spread
    if len(pieces) > 0:
        entries = level_of(stream_key, shape, pieces, -0.22, 0.18) * entries
    return jnp.clip(entries, min=-reach, max=reach).astype(kind)


def setup_inputs(seed: int = 0) -> dict:
    key_of = jax.random.split(jax.random.key(seed), 5)
    return {
        "events": draw_events(jax.random.fold_in(key_of[4], 71), 0),
        "labels": place_ends((jax.random.randint(key_of[1], (EVENTS,), 0, 2) < 1).astype(jnp.int32), jax.random.fold_in(key_of[1], 1), 0, 1),
        "weights": gaussian(key_of[2], (F,), 1.0, 6.0, ((0, 8),), jnp.float32),
        "contexts": place_ends(jax.random.randint(key_of[3], (NCAND,), 0, EVENTS), jax.random.fold_in(key_of[3], 1), 0, EVENTS - 1).astype(jnp.int32),
    }


LAMBDA = 0.5


def split_pair(values):
    leading = values.astype(jnp.bfloat16)
    rest = values - lax.optimization_barrier(leading).astype(jnp.float32)
    return leading, rest.astype(jnp.bfloat16)


def reference(events, labels, weights, contexts):
    block_rows = math.gcd(EVENTS, 2048)
    block_count = EVENTS // block_rows
    tiled_events = events.reshape(block_count, block_rows, F)
    tiled_labels = labels.reshape(block_count, block_rows)
    weight_half = weights.astype(jnp.bfloat16)

    def gradient_block(summed, packed):
        tile_rows, tile_labels = packed
        margin = jnp.dot(tile_rows, weight_half, preferred_element_type=jnp.float32)
        chance = jax.nn.sigmoid(margin)
        errors = chance - tile_labels.astype(jnp.float32)
        err_lead, err_rest = split_pair(errors)
        summed = summed + jnp.dot(err_lead, tile_rows, preferred_element_type=jnp.float32)
        summed = summed + jnp.dot(err_rest, tile_rows, preferred_element_type=jnp.float32)
        return summed, chance * (1.0 - chance)

    gradient, curvature_rate = lax.scan(gradient_block, jnp.zeros((F,), jnp.float32), (tiled_events, tiled_labels))
    gradient = gradient + LAMBDA * weights
    picked = jnp.take(events, contexts, axis=0).astype(jnp.float32)
    right_side = jnp.concatenate([gradient[None, :], picked], axis=0)
    solution = jnp.zeros_like(right_side)
    residual = right_side
    direction = right_side
    norm_now = jnp.sum(residual * residual, axis=1)
    for iteration in range(ITERS):
        dir_lead, dir_rest = split_pair(direction)
        dir_pair = jnp.concatenate([dir_lead, dir_rest], axis=0)

        def hessian_block(summed, packed):
            tile_rows, tile_curv = packed
            both = lax.dot_general(dir_pair, tile_rows, (((1,), (1,)), ((), ())), preferred_element_type=jnp.float32)
            scores = both[:RHS] + both[RHS:]
            weighted = tile_curv[None, :] * scores
            q_lead, q_rest = split_pair(weighted)
            hess_part = jnp.dot(q_lead, tile_rows, preferred_element_type=jnp.float32)
            hess_part = hess_part + jnp.dot(q_rest, tile_rows, preferred_element_type=jnp.float32)
            terms = jnp.sum(weighted * scores, axis=1)
            return (summed[0] + hess_part, summed[1] + terms), None

        start_pair = (jnp.zeros((RHS, F), jnp.float32), jnp.zeros((RHS,), jnp.float32))
        (hess_sum, event_terms), _ = lax.scan(hessian_block, start_pair, (tiled_events, curvature_rate))
        hess_vec = hess_sum + LAMBDA * direction
        curvature = event_terms + LAMBDA * jnp.sum(direction * direction, axis=1)
        step_size = norm_now / curvature
        solution = solution + step_size[:, None] * direction
        residual = residual - step_size[:, None] * hess_vec
        norm_next = jnp.sum(residual * residual, axis=1)
        direction = residual + (norm_next / norm_now)[:, None] * direction
        norm_now = norm_next
    new_weights = weights - solution[0]
    widths = jnp.sum(right_side[1:] * solution[1:], axis=1)
    return new_weights, widths
```

```python
import jax
import jax.numpy as jnp
from jax import lax
from jax.sharding import PartitionSpec as P

LAMBDA = 0.5
XN, ZN, YN, CN = 4, 8, 4, 2
F32, BF16 = jnp.float32, jnp.bfloat16


def rounded(v):
    return lax.optimization_barrier(v.astype(BF16))


def pair_of(v):
    lead = rounded(v)
    return lead, rounded(v - lead.astype(F32))


def triple_of(v):
    lead, rest = rounded(v), None
    rest = v - lead.astype(F32)
    mid = rounded(rest)
    return lead, mid, rounded(rest - mid.astype(F32))


def x_move(v, k):
    return lax.ppermute(v, "event", [(i, (i + k * ZN) % (XN * ZN)) for i in range(XN * ZN)])


def y_move(v, k):
    return lax.ppermute(v, "feat", [(i, (i + k * CN) % (YN * CN)) for i in range(YN * CN)])


def core_move(v):
    return lax.ppermute(v, "feat", [(i, i ^ 1) for i in range(YN * CN)])


def z_exchange(v):
    groups = [[x * ZN + z for z in range(ZN)] for x in range(XN)]
    return lax.all_to_all(v, "event", 0, 0, axis_index_groups=groups)


def z_spread(v):
    return z_exchange(jnp.broadcast_to(v[None], (ZN,) + v.shape))


def four(own, moved):
    return (own + moved[1]) + (moved[0] + moved[2])


def y_total(v):
    return four(v, [y_move(v, k) for k in (1, 2, 3)])


def x_total(v):
    return four(v, [x_move(v, k) for k in (1, 2, 3)])


def event_total_small(v):
    return jnp.sum(z_spread(x_total(v)), axis=0)


def feat_total_small(v):
    return y_total(v + core_move(v))


def x_scatter(v, x):
    width = v.shape[1] // XN
    quarter = lambda k: lax.dynamic_slice_in_dim(v, lax.rem(x + k, XN) * width, width, axis=1)
    moved = [x_move(quarter(k), k) for k in (1, 2, 3)]
    return four(quarter(0).astype(F32), [m.astype(F32) for m in moved])


def z_scatter(v):
    rows, width = v.shape
    cut = v.reshape(rows, ZN, width // ZN).transpose(1, 0, 2)
    return jnp.sum(z_exchange(cut).astype(F32), axis=0)


def event_gather(v, x):
    rows = v.shape[0]
    quarter = z_spread(v).transpose(1, 0, 2).reshape(rows, -1)
    parts = [quarter] + [x_move(quarter, k) for k in (1, 2, 3)]
    ordered = jnp.stack([parts[0], parts[3], parts[2], parts[1]], axis=1)
    twice = jnp.concatenate([ordered, ordered], axis=1)
    return lax.dynamic_slice_in_dim(twice, lax.rem(XN - x, XN), XN, axis=1).reshape(rows, -1)


def feat_total(v):
    rows, width = v.shape
    half = width // 2
    core = lax.rem(lax.axis_index("feat"), CN)
    own = lax.dynamic_slice_in_dim(v, core * half, half, axis=1)
    other = lax.dynamic_slice_in_dim(v, (1 - core) * half, half, axis=1)
    total = y_total(own + core_move(other))
    return total


def both_halves(total):
    core = lax.rem(lax.axis_index("feat"), CN)
    theirs = core_move(total)
    first = jnp.where(core == 0, total, theirs)
    second = jnp.where(core == 0, theirs, total)
    return jnp.concatenate([first, second], axis=1)


def on_device(events, labels, weights, contexts):
    count = events.shape[0]
    place = lax.axis_index("event")
    x, z = place // ZN, lax.rem(place, ZN)
    weight_half = weights.astype(BF16)

    positions = place * count + jnp.arange(count, dtype=jnp.int32)
    selector = (contexts[:, None] == positions[None, :]).astype(BF16)
    picked = jnp.dot(selector, events, preferred_element_type=F32).astype(BF16)
    cand = event_gather(z_scatter(x_scatter(picked, x).astype(BF16)).astype(BF16), x)

    margin = feat_total_small(jnp.dot(events, weight_half, preferred_element_type=F32))
    chance = jax.nn.sigmoid(margin)
    rate = chance * (1.0 - chance)
    errors = chance - labels.astype(F32)
    err_pair = jnp.stack(pair_of(errors), axis=0)
    grad = jnp.sum(jnp.dot(err_pair, events, preferred_element_type=F32), axis=0)
    grad = event_total_small(grad) + LAMBDA * weights

    grad_lead, grad_rest = pair_of(grad)
    right_side = jnp.concatenate([grad[None], cand.astype(F32)], axis=0)
    rhs_rows = jnp.concatenate([grad_lead[None], cand, grad_rest[None]], axis=0)
    last = (((1,), (1,)), ((), ()))
    raw = lax.dot_general(rhs_rows, events, last, preferred_element_type=F32)
    scores = jnp.concatenate([raw[:1] + raw[64:], raw[1:64]], axis=0)
    norm_part = jnp.sum(right_side * right_side, axis=1)
    row = jnp.pad(norm_part, (0, count // 2 - 64))[None]
    row = jnp.concatenate([row, row], axis=1)
    core = lax.rem(lax.axis_index("feat"), CN)
    total = both_halves(feat_total(jnp.concatenate([scores, row], axis=0)))
    scores, norm_now = total[:64], total[64, :64]

    weighted = rate[None] * scores
    curv_part = jnp.sum(weighted * scores, axis=1)
    q_lead, q_rest = pair_of(weighted)
    raw = jnp.dot(jnp.concatenate([q_lead, q_rest[:1]], axis=0), events, preferred_element_type=F32)
    hess = jnp.concatenate([raw[:1] + raw[64:], raw[1:64]], axis=0)

    def packed(values, scalars):
        lead = rounded(values)
        rest = rounded(values[:1] - lead[:1].astype(F32))
        width = values.shape[1] // scalars.shape[0]
        line = jnp.stack(triple_of(scalars), axis=1).reshape(scalars.shape[0], -1)
        line = jnp.pad(line, ((0, 0), (0, width - line.shape[1]))).reshape(1, -1)
        return jnp.concatenate([lead, rest, line], axis=0)

    def unpacked(total, pieces):
        line = jnp.sum(total[65].reshape(pieces, -1)[:, :192].reshape(pieces, 3, 64), axis=1)
        values = jnp.concatenate([total[:1] + total[64:65], total[1:64]], axis=0)
        return values, line

    quarter = x_scatter(packed(hess, jnp.broadcast_to(curv_part[None], (XN, 64))), x)
    hess_q, curv = unpacked(quarter, 1)
    curv = curv[0]
    lead = rounded(hess_q)
    rest = rounded(hess_q[:1] - lead[:1].astype(F32))
    c_lead, c_mid, c_low = triple_of(curv)
    zero = jnp.zeros_like(c_lead)
    lines = jnp.stack([jnp.concatenate([c_lead, c_mid]), jnp.concatenate([c_low, zero])], axis=0)
    lines = jnp.tile(lines, (1, ZN))
    eighth = z_scatter(jnp.concatenate([lead, rest, lines], axis=0))
    hess_shard = jnp.concatenate([eighth[:1] + eighth[64:65], eighth[1:64]], axis=0)
    curv = (eighth[65, :64] + eighth[65, 64:]) + eighth[66, :64]

    norm_b = norm_now
    step_one = norm_b / (curv + LAMBDA * norm_b)
    b_shard = lax.dynamic_slice_in_dim(right_side, place * 128, 128, axis=1)
    res_shard = b_shard - step_one[:, None] * (hess_shard + LAMBDA * b_shard)
    res_lead = rounded(res_shard)
    res_rest = rounded(res_shard[:1] - res_lead[:1].astype(F32))
    res_rows = event_gather(jnp.concatenate([res_lead, res_rest], axis=0), x)

    raw = lax.dot_general(res_rows, events, last, preferred_element_type=F32)
    res_scores = jnp.concatenate([raw[:1] + raw[64:], raw[1:64]], axis=0)
    res = res_rows.astype(F32)
    res = jnp.concatenate([res[:1] + res[64:], res[1:64]], axis=0)
    line = jnp.concatenate([jnp.sum(res * res, axis=1), jnp.sum(res * right_side, axis=1)])
    line = jnp.pad(line, (0, count // 2 - 128))[None]
    line = jnp.concatenate([line, line], axis=1)
    half = feat_total(jnp.concatenate([res_scores, line], axis=0))
    norm_next, cross = half[64, :64], half[64, 64:128]
    res_scores = half[:64]
    own = lax.dynamic_slice_in_dim(weighted, core * (count // 2), count // 2, axis=1)
    own_rate = lax.dynamic_slice_in_dim(rate, core * (count // 2), count // 2, axis=0)
    mixed = jnp.sum(own * res_scores, axis=1)
    square = jnp.sum(own_rate[None] * res_scores * res_scores, axis=1)
    tail = jnp.concatenate([mixed, square])
    tail = tail + core_move(tail)
    tail = jnp.sum(lax.all_to_all(jnp.broadcast_to(tail[None], (XN * ZN, 128)), "event", 0, 0), axis=0)
    mixed, square = tail[:64], tail[64:]

    ratio = norm_next / norm_b
    curvature = square + 2.0 * ratio * mixed + ratio * ratio * curv
    curvature = curvature + LAMBDA * (norm_next + 2.0 * ratio * cross + ratio * ratio * norm_b)
    step_two = norm_next / curvature
    widths = step_one * norm_b + step_two * (cross + ratio * norm_b)
    step_full = step_one[0] * grad + step_two[0] * (res[0] + ratio[0] * grad)
    return (weights - step_full, widths[1:])


def solution(mesh):
    in_specs = (P("event", "feat"), P("event"), P("feat"), P())
    out_specs = (P("feat"), P())
    return jax.shard_map(on_device, mesh=mesh, in_specs=in_specs, out_specs=out_specs, check_vma=False)
```

```python
import jax
import jax.numpy as jnp
from jax import lax
from jax.experimental import pallas as pl
from jax.experimental.pallas import tpu as pltpu
from jax.sharding import PartitionSpec as P

LAMBDA = 0.5
XN, ZN, YN, CN = 4, 8, 4, 2
F32, BF16 = jnp.float32, jnp.bfloat16


def rounded(v):
    return lax.optimization_barrier(v.astype(BF16))


def pair_of(v):
    lead = rounded(v)
    return lead, rounded(v - lead.astype(F32))


def triple_of(v):
    lead, rest = rounded(v), None
    rest = v - lead.astype(F32)
    mid = rounded(rest)
    return lead, mid, rounded(rest - mid.astype(F32))


def x_move(v, k):
    return lax.ppermute(v, "event", [(i, (i + k * ZN) % (XN * ZN)) for i in range(XN * ZN)])


def y_move(v, k):
    return lax.ppermute(v, "feat", [(i, (i + k * CN) % (YN * CN)) for i in range(YN * CN)])


def core_move(v):
    return lax.ppermute(v, "feat", [(i, i ^ 1) for i in range(YN * CN)])


def z_exchange(v):
    groups = [[x * ZN + z for z in range(ZN)] for x in range(XN)]
    return lax.all_to_all(v, "event", 0, 0, axis_index_groups=groups)


def z_spread(v):
    return z_exchange(jnp.broadcast_to(v[None], (ZN,) + v.shape))


def four(own, moved):
    return (own + moved[1]) + (moved[0] + moved[2])


def y_total(v):
    return four(v, [y_move(v, k) for k in (1, 2, 3)])


def x_total(v):
    return four(v, [x_move(v, k) for k in (1, 2, 3)])


def feat_total_small(v):
    return y_total(v + core_move(v))


def x_scatter(v, x):
    width = v.shape[1] // XN
    quarter = lambda k: lax.dynamic_slice_in_dim(v, lax.rem(x + k, XN) * width, width, axis=1)
    moved = [x_move(quarter(k), k) for k in (1, 2, 3)]
    return four(quarter(0).astype(F32), [m.astype(F32) for m in moved])


def z_scatter(v):
    rows, width = v.shape
    cut = v.reshape(rows, ZN, width // ZN).transpose(1, 0, 2)
    return jnp.sum(z_exchange(cut).astype(F32), axis=0)


def event_gather(v, x):
    rows = v.shape[0]
    quarter = z_spread(v).transpose(1, 0, 2).reshape(rows, -1)
    parts = [quarter] + [x_move(quarter, k) for k in (1, 2, 3)]
    ordered = jnp.stack([parts[0], parts[3], parts[2], parts[1]], axis=1)
    twice = jnp.concatenate([ordered, ordered], axis=1)
    return lax.dynamic_slice_in_dim(twice, lax.rem(XN - x, XN), XN, axis=1).reshape(rows, -1)


def half_sums(v):
    half = v.shape[1] // 2
    core = lax.rem(lax.axis_index("feat"), CN)
    own = lax.dynamic_slice_in_dim(v, core * half, half, axis=1)
    other = lax.dynamic_slice_in_dim(v, (1 - core) * half, half, axis=1)
    return own + core_move(other)


def y_sums(scores, lines):
    lead = rounded(scores)
    rest = rounded(scores[:1] - lead[:1].astype(F32))
    line = jnp.stack(triple_of(lines), axis=1).reshape(1, -1)
    line = jnp.pad(line, ((0, 0), (0, scores.shape[1] - line.shape[1])))
    total = jnp.concatenate([lead, rest, line], axis=0)
    total = four(total.astype(F32), [y_move(total, k).astype(F32) for k in (1, 2, 3)])
    line = jnp.sum(total[65, : lines.shape[0] * 192].reshape(-1, 3, 64), axis=1)
    return jnp.concatenate([total[:1] + total[64:65], total[1:64]], axis=0), line


def pick_kernel(local_ref, events_ref, out_ref, blocks, rows, sems):
    count = events_ref.shape[0]
    wanted = local_ref.shape[0]

    def fetch(j):
        r = local_ref[j]
        start = pl.multiple_of(lax.div(r, 16) * 16, 16)
        return pltpu.make_async_copy(events_ref.at[pl.ds(start, 16), :], blocks.at[j], sems.at[j])

    def owned(j):
        return jnp.logical_and(local_ref[j] >= 0, local_ref[j] < count)

    @pl.loop(0, wanted)
    def _(j):
        @pl.when(owned(j))
        def _():
            fetch(j).start()

    rows[...] = jnp.zeros_like(rows)

    @pl.loop(0, wanted)
    def _(j):
        @pl.when(owned(j))
        def _():
            fetch(j).wait()
            line = lax.broadcasted_iota(jnp.int32, blocks.shape[1:], 0) == lax.rem(local_ref[j], 16)
            found = jnp.where(line, blocks[j].astype(F32), 0.0)
            rows[pl.ds(j, 1), :] = jnp.sum(found, axis=0, keepdims=True)

    for t in range(out_ref.shape[0]):
        out_ref[t] = rows[:, t * 128 : (t + 1) * 128].astype(BF16)


def pick(local, events):
    width = events.shape[1]
    return pl.pallas_call(
        pick_kernel,
        out_shape=jax.ShapeDtypeStruct((width // 128, 64, 128), BF16),
        in_specs=[pl.BlockSpec(memory_space=pltpu.SMEM), pl.BlockSpec(memory_space=pl.ANY)],
        out_specs=pl.BlockSpec(memory_space=pltpu.VMEM),
        scratch_shapes=[
            pltpu.VMEM((63, 16, width), BF16),
            pltpu.VMEM((64, width), F32),
            pltpu.SemaphoreType.DMA((63,)),
        ],
        compiler_params=pltpu.CompilerParams(vmem_limit_bytes=24 << 20),
        cost_estimate=pl.CostEstimate(flops=0, bytes_accessed=2 << 20, transcendentals=0),
    )(local, events)


def both_halves(total):
    core = lax.rem(lax.axis_index("feat"), CN)
    theirs = core_move(total)
    first = jnp.where(core == 0, total, theirs)
    second = jnp.where(core == 0, theirs, total)
    return jnp.concatenate([first, second], axis=1)


def on_device(events, labels, weights, contexts):
    count = events.shape[0]
    place = lax.axis_index("event")
    x, z = place // ZN, lax.rem(place, ZN)
    weight_half = weights.astype(BF16)

    chunks = lax.all_to_all(pick(contexts - place * count, events), "event", 0, 0)
    cand_shard = jnp.sum(chunks.astype(F32), axis=0).astype(BF16)

    margin = feat_total_small(jnp.dot(events, weight_half, preferred_element_type=F32))
    chance = jax.nn.sigmoid(margin)
    rate = chance * (1.0 - chance)
    errors = chance - labels.astype(F32)
    err_pair = jnp.stack(pair_of(errors), axis=0)
    grad = jnp.sum(jnp.dot(err_pair, events, preferred_element_type=F32), axis=0).reshape(-1, 128)
    message = z_spread(jnp.concatenate([cand_shard, *pair_of(grad)], axis=0))
    grad = jnp.sum(message[:, 64:96].astype(F32) + message[:, 96:].astype(F32), axis=0)
    own = jnp.concatenate([message[:, :64].reshape(-1, 128), *pair_of(grad)], axis=0)
    parts = [own] + [x_move(own, k) for k in (1, 2, 3)]
    grads = [p[512:544].astype(F32) + p[544:].astype(F32) for p in parts]
    grad = four(grads[0], grads[1:]).reshape(-1) + LAMBDA * weights
    ordered = jnp.stack([parts[0][:512], parts[3][:512], parts[2][:512], parts[1][:512]], axis=0)
    ordered = jnp.concatenate([ordered, ordered], axis=0)
    ordered = lax.dynamic_slice_in_dim(ordered, lax.rem(XN - x, XN), XN, axis=0)
    cand = ordered.reshape(32, 64, 128).transpose(1, 0, 2).reshape(64, -1)[:63]

    grad_lead, grad_rest = pair_of(grad)
    right_side = jnp.concatenate([grad[None], cand.astype(F32)], axis=0)
    rhs_rows = jnp.concatenate([grad_lead[None], cand, grad_rest[None]], axis=0)
    last = (((1,), (1,)), ((), ()))
    raw = lax.dot_general(rhs_rows, events, last, preferred_element_type=F32)
    scores = jnp.concatenate([raw[:1] + raw[64:], raw[1:64]], axis=0)
    norm_part = jnp.sum(right_side * right_side, axis=1)
    row = jnp.pad(norm_part, (0, count // 2 - 64))[None]
    half = half_sums(jnp.concatenate([scores, jnp.concatenate([row, row], axis=1)], axis=0))
    half, line = y_sums(half[:64], half[64:, :64])
    scores, norm_now = both_halves(half), line[0]
    core = lax.rem(lax.axis_index("feat"), CN)

    weighted = rate[None] * scores
    curv_part = jnp.sum(weighted * scores, axis=1)
    q_lead, q_rest = pair_of(weighted)
    raw = jnp.dot(jnp.concatenate([q_lead, q_rest[:1]], axis=0), events, preferred_element_type=F32)
    hess = jnp.concatenate([raw[:1] + raw[64:], raw[1:64]], axis=0)

    def packed(values, scalars):
        lead = rounded(values)
        rest = rounded(values[:1] - lead[:1].astype(F32))
        width = values.shape[1] // scalars.shape[0]
        line = jnp.stack(triple_of(scalars), axis=1).reshape(scalars.shape[0], -1)
        line = jnp.pad(line, ((0, 0), (0, width - line.shape[1]))).reshape(1, -1)
        return jnp.concatenate([lead, rest, line], axis=0)

    def unpacked(total, pieces):
        line = jnp.sum(total[65].reshape(pieces, -1)[:, :192].reshape(pieces, 3, 64), axis=1)
        values = jnp.concatenate([total[:1] + total[64:65], total[1:64]], axis=0)
        return values, line

    quarter = x_scatter(packed(hess, jnp.broadcast_to(curv_part[None], (XN, 64))), x)
    hess_q, curv = unpacked(quarter, 1)
    curv = curv[0]
    lead = rounded(hess_q)
    rest = rounded(hess_q[:1] - lead[:1].astype(F32))
    c_lead, c_mid, c_low = triple_of(curv)
    zero = jnp.zeros_like(c_lead)
    lines = jnp.stack([jnp.concatenate([c_lead, c_mid]), jnp.concatenate([c_low, zero])], axis=0)
    lines = jnp.tile(lines, (1, ZN))
    eighth = z_scatter(jnp.concatenate([lead, rest, lines], axis=0))
    hess_shard = jnp.concatenate([eighth[:1] + eighth[64:65], eighth[1:64]], axis=0)
    curv = (eighth[65, :64] + eighth[65, 64:]) + eighth[66, :64]

    norm_b = norm_now
    step_one = norm_b / (curv + LAMBDA * norm_b)
    b_shard = lax.dynamic_slice_in_dim(right_side, place * 128, 128, axis=1)
    res_shard = b_shard - step_one[:, None] * (hess_shard + LAMBDA * b_shard)
    res_lead = rounded(res_shard)
    res_rest = rounded(res_shard[:1] - res_lead[:1].astype(F32))
    res_rows = event_gather(jnp.concatenate([res_lead, res_rest], axis=0), x)

    raw = lax.dot_general(res_rows, events, last, preferred_element_type=F32)
    res_scores = jnp.concatenate([raw[:1] + raw[64:], raw[1:64]], axis=0)
    res = res_rows.astype(F32)
    res = jnp.concatenate([res[:1] + res[64:], res[1:64]], axis=0)
    line = jnp.concatenate([jnp.sum(res * res, axis=1), jnp.sum(res * right_side, axis=1)])
    line = jnp.pad(line, (0, count // 2 - 128))[None]
    line = jnp.concatenate([line, line], axis=1)
    half = half_sums(jnp.concatenate([res_scores, line], axis=0))
    res_scores, line = y_sums(half[:64], half[64, :128].reshape(2, 64))
    norm_next, cross = line[0], line[1]
    own = lax.dynamic_slice_in_dim(weighted, core * (count // 2), count // 2, axis=1)
    own_rate = lax.dynamic_slice_in_dim(rate, core * (count // 2), count // 2, axis=0)
    mixed = jnp.sum(own * res_scores, axis=1)
    square = jnp.sum(own_rate[None] * res_scores * res_scores, axis=1)
    tail = jnp.concatenate([mixed, square])
    tail = tail + core_move(tail)
    tail = jnp.sum(lax.all_to_all(jnp.broadcast_to(tail[None], (XN * ZN, 128)), "event", 0, 0), axis=0)
    mixed, square = tail[:64], tail[64:]

    ratio = norm_next / norm_b
    curvature = square + 2.0 * ratio * mixed + ratio * ratio * curv
    curvature = curvature + LAMBDA * (norm_next + 2.0 * ratio * cross + ratio * ratio * norm_b)
    step_two = norm_next / curvature
    widths = step_one * norm_b + step_two * (cross + ratio * norm_b)
    step_full = step_one[0] * grad + step_two[0] * (res[0] + ratio[0] * grad)
    return (weights - step_full, widths[1:])


def solution(mesh):
    in_specs = (P("event", "feat"), P("event"), P("feat"), P())
    out_specs = (P("feat"), P())
    return jax.shard_map(on_device, mesh=mesh, in_specs=in_specs, out_specs=out_specs, check_vma=False)
```

```python
import jax
import jax.numpy as jnp
from jax import lax
from jax.experimental import pallas as pl
from jax.experimental.pallas import tpu as pltpu
from jax.sharding import PartitionSpec as P

LAMBDA = 0.5
XN, ZN, YN, CN = 4, 8, 4, 2
EN = XN * ZN
ROWS = 64
TILES = 32
QUARTER = TILES // XN
COUNT = 1280
HALF = COUNT // 2
F32, BF16 = jnp.float32, jnp.bfloat16
VMEM = pl.BlockSpec(memory_space=pltpu.VMEM)
SMEM = pl.BlockSpec(memory_space=pltpu.SMEM)
HBM = pl.BlockSpec(memory_space=pltpu.HBM)
ACROSS = (((1,), (1,)), ((), ()))


def shaped(*shape, dtype=F32):
    return jax.ShapeDtypeStruct(shape, dtype)


def kernel_call(body, ins, outs, args, scratch=(), micros=0.5):
    return pl.pallas_call(
        body,
        out_shape=outs,
        in_specs=ins,
        out_specs=[VMEM] * len(outs),
        scratch_shapes=list(scratch),
        compiler_params=pltpu.CompilerParams(vmem_limit_bytes=28 << 20),
        cost_estimate=pl.CostEstimate(flops=0, bytes_accessed=int(micros * 3.6e6), transcendentals=0),
    )(*args)


def x_moves(v):
    n = XN * ZN
    return [lax.ppermute(v, "event", [(i, (i + k * ZN) % n) for i in range(n)]) for k in (1, 2, 3)]


def y_moves(v):
    n = YN * CN
    return [lax.ppermute(v, "feat", [(i, (i + k * CN) % n) for i in range(n)]) for k in (1, 2, 3)]


def core_move(v):
    return lax.ppermute(v, "feat", [(i, i ^ 1) for i in range(YN * CN)])


def z_exchange(v):
    groups = [[x * ZN + z for z in range(ZN)] for x in range(XN)]
    return lax.all_to_all(v, "event", 0, 0, axis_index_groups=groups)


def four(own, one, two, three):
    return (own + two) + (one + three)


def pair_of(v):
    lead = v.astype(BF16)
    return lead, (v - lead.astype(F32)).astype(BF16)


def triple_of(v):
    lead, rest = v.astype(BF16), v
    rest = v - lead.astype(F32)
    mid = rest.astype(BF16)
    return lead, mid, (rest - mid.astype(F32)).astype(BF16)


def row_is(shape, i):
    return lax.broadcasted_iota(jnp.int32, shape, 0) == i


def stacked(lines, rows):
    out = jnp.zeros((rows, lines[0].shape[1]), F32)
    for i, line in enumerate(lines):
        out = jnp.where(row_is(out.shape, i), line.astype(F32), out)
    return out


def joined(v):
    top = v[:ROWS]
    return top + jnp.where(row_is(top.shape, ROWS - 1), v[ROWS : ROWS + 1], 0.0)


def line_sums(top, bottom):
    return jnp.sum(jnp.transpose(jnp.concatenate([top, bottom], axis=0)), axis=0, keepdims=True)


def tile_sums(v):
    total = v[:, :128]
    for t in range(1, v.shape[1] // 128):
        total = total + v[:, t * 128 : (t + 1) * 128]
    return total


def first_kernel(local_ref, w_ref, events_ref, held_ref, margin_ref, out_ref, rows, sems):
    piece = COUNT // 5
    copies = [
        pltpu.make_async_copy(
            events_ref.at[pl.ds(c * piece, piece), :], held_ref.at[pl.ds(c * piece, piece), :], sems.at[c]
        )
        for c in range(5)
    ]
    for copy in copies:
        copy.start()
    rows[...] = jnp.zeros_like(rows)
    w = jnp.broadcast_to(w_ref[...], (16, TILES * 128)).astype(BF16)
    for c, copy in enumerate(copies):
        copy.wait()
        part = lax.dot_general(w, held_ref[c * piece : (c + 1) * piece, :], ACROSS, preferred_element_type=F32)
        margin_ref[2 * c : 2 * c + 1, :] = part[:1, :128]
        margin_ref[2 * c + 1 : 2 * c + 2, :] = part[:1, 128:]

    @pl.loop(0, ROWS - 1)
    def _(j):
        r = local_ref[j]

        @pl.when(jnp.logical_and(r >= 0, r < COUNT))
        def _():
            start = pl.multiple_of(lax.div(r, 16) * 16, 16)
            block = held_ref[pl.ds(start, 16), :].astype(F32)
            found = jnp.where(row_is(block.shape, lax.rem(r, 16)), block, 0.0)
            rows[pl.ds(j, 1), :] = jnp.sum(found, axis=0, keepdims=True)

    for t in range(TILES):
        out_ref[t] = rows[:, t * 128 : (t + 1) * 128].astype(BF16)


def gradient_kernel(held_ref, own, one, two, three, labels_ref, rate_ref, grad_ref, errs):
    margin = four(own[...], one[...], two[...], three[...])
    chance = jax.nn.sigmoid(margin)
    rate = chance * (1.0 - chance)
    errors = chance - labels_ref[...].astype(F32)
    lead, rest = pair_of(errors)
    lead, rest = lead.astype(F32), rest.astype(F32)
    for i in range(COUNT // 128):
        at = slice(i * 128, (i + 1) * 128)
        rate_ref[:, at] = rate[i : i + 1]
        errs[:, at] = stacked([lead[i : i + 1], rest[i : i + 1]], 16).astype(BF16)
    for n in range(0, TILES, 4):
        part = jnp.dot(errs[...], held_ref[:, n * 128 : (n + 4) * 128], preferred_element_type=F32)
        line = part[:1] + part[1:2]
        for u in range(4):
            grad_ref[n + u : n + u + 1, :] = line[:, u * 128 : (u + 1) * 128]


def spread_kernel(chunks_ref, grad_ref, out_ref):
    total = chunks_ref[0].astype(F32)
    for e in range(1, EN):
        total = total + chunks_ref[e].astype(F32)
    lead, rest = pair_of(grad_ref[...])
    for z in range(ZN):
        out_ref[z, :ROWS, :] = total.astype(BF16)
        out_ref[z, ROWS : ROWS + TILES, :] = lead
        out_ref[z, ROWS + TILES :, :] = rest


def collect_kernel(in_ref, out_ref):
    grad = jnp.zeros((TILES, 128), F32)
    for z in range(ZN):
        out_ref[z * ROWS : (z + 1) * ROWS, :] = in_ref[z, :ROWS, :]
        grad = grad + (in_ref[z, ROWS : ROWS + TILES, :].astype(F32) + in_ref[z, ROWS + TILES :, :].astype(F32))
    lead, rest = pair_of(grad)
    out_ref[QUARTER * ROWS : QUARTER * ROWS + TILES, :] = lead
    out_ref[QUARTER * ROWS + TILES :, :] = rest


def put_scores(held_ref, rhs, core, other_ref, own_ref, lines):
    for half, out_ref in ((1 - core, other_ref), (core, own_ref)):
        start = pl.multiple_of(half * HALF, HALF)
        part = lax.dot_general(held_ref[pl.ds(start, HALF), :], rhs[...], ACROSS, preferred_element_type=F32)
        for t in range(HALF // 128):
            out_ref[:ROWS, t * 128 : (t + 1) * 128] = joined(jnp.transpose(part[t * 128 : (t + 1) * 128]))
            out_ref[ROWS:, t * 128 : (t + 1) * 128] = lines if t == 0 else jnp.zeros_like(lines)


def scores_kernel(idx_ref, held_ref, w_ref, own, one, two, three, rhs_ref, grad_ref, other_ref, mine_ref):
    x, core = idx_ref[0], idx_ref[2]
    top = QUARTER * ROWS
    grads = [p[top : top + TILES, :].astype(F32) + p[top + TILES :, :].astype(F32) for p in (own, one, two, three)]
    grad_ref[...] = four(*grads) + LAMBDA * w_ref[...]
    norm = jnp.zeros((ROWS, 128), F32)
    rhs_ref[ROWS:, :] = jnp.zeros((128 - ROWS, TILES * 128), BF16)
    for k, part in enumerate((own, one, two, three)):
        quarter = lax.rem(x + XN - k, XN)
        for t in range(QUARTER):
            tile = quarter * QUARTER + t
            grad = grad_ref[pl.ds(tile, 1), :]
            lead, rest = pair_of(grad)
            values = part[t * ROWS : (t + 1) * ROWS, :].astype(F32)
            last = row_is(values.shape, ROWS - 1)
            exact = jnp.where(last, grad, values)
            norm = norm + exact * exact
            at = pl.ds(pl.multiple_of(tile * 128, 128), 128)
            rhs_ref[:ROWS, at] = jnp.where(last, lead.astype(F32), values).astype(BF16)
            rhs_ref[ROWS : ROWS + 16, at] = stacked([rest], 16).astype(BF16)
    line = line_sums(norm, jnp.zeros_like(norm))
    put_scores(held_ref, rhs_ref, core, other_ref, mine_ref, stacked([line], 8))


def pack_kernel(own, other, out_ref):
    total = own[...] + other[...]
    scores, lines = total[:ROWS], total[ROWS:]
    lead = scores.astype(BF16)
    rest = scores[ROWS - 1 :] - lead[ROWS - 1 :].astype(F32)
    out_ref[:ROWS, :] = lead
    out_ref[ROWS:, :] = stacked([rest, *triple_of(lines[:1]), *triple_of(lines[1:2])], 16).astype(BF16)


def unpacked(own, one, two, three):
    total = four(*(p[...].astype(F32) for p in (own, one, two, three)))
    first = total[65:66] + total[66:67] + total[67:68]
    second = total[68:69] + total[69:70] + total[70:71]
    return joined(total), first[:, :128], second[:, :128]


def unpack_kernel(own, one, two, three, scores_ref, norm_ref):
    scores, norm, _ = unpacked(own, one, two, three)
    scores_ref[...] = scores
    norm_ref[...] = stacked([norm], 8)


def hessian_kernel(idx_ref, held_ref, mine_ref, theirs_ref, rate_ref, own_ref, curv_ref, one_ref, two_ref, three_ref, q):
    x, core = idx_ref[0], idx_ref[2]
    curv = jnp.zeros((ROWS, 128), F32)
    for half in range(2):
        scores = jnp.where(core == half, mine_ref[...], theirs_ref[...])
        at = slice(half * HALF, (half + 1) * HALF)
        weighted = rate_ref[:, at] * scores
        curv = curv + tile_sums(weighted * scores)
        lead = weighted.astype(BF16)
        q[:ROWS, at] = lead
        q[ROWS:, at] = stacked([weighted[ROWS - 1 :] - lead[ROWS - 1 :].astype(F32)], 16).astype(BF16)
    triple = [v.astype(F32) for v in triple_of(line_sums(curv, jnp.zeros_like(curv)))]
    curv_ref[...] = stacked(triple, 8)
    for k, out_ref in ((2, two_ref), (1, one_ref), (3, three_ref), (0, own_ref)):
        quarter = lax.rem(x + k, XN)
        columns = pl.ds(pl.multiple_of(quarter * QUARTER * 128, 128), QUARTER * 128)
        total = joined(jnp.dot(q[...], held_ref[:, columns], preferred_element_type=F32))
        rests = []
        for t in range(QUARTER):
            values = total[:, t * 128 : (t + 1) * 128]
            out_ref[t * ROWS : (t + 1) * ROWS, :] = values.astype(out_ref.dtype)
            rests.append(values[ROWS - 1 :] - values[ROWS - 1 :].astype(BF16).astype(F32))
        if k:
            out_ref[QUARTER * ROWS :, :] = stacked(rests + triple, 16).astype(BF16)


def cut_kernel(own, curv_ref, one, two, three, out_ref):
    top = QUARTER * ROWS
    tails = [p[top:, :].astype(F32) for p in (one, two, three)]
    curvs = [curv_ref[0:1] + curv_ref[1:2] + curv_ref[2:3]]
    curvs += [v[QUARTER : QUARTER + 1] + v[QUARTER + 1 : QUARTER + 2] + v[QUARTER + 2 : QUARTER + 3] for v in tails]
    curv = triple_of(four(*curvs))
    for t in range(QUARTER):
        at = slice(t * ROWS, (t + 1) * ROWS)
        total = four(own[at, :], one[at, :].astype(F32), two[at, :].astype(F32), three[at, :].astype(F32))
        rest = tails[0][t : t + 1] + tails[1][t : t + 1] + tails[2][t : t + 1]
        total = total + jnp.where(row_is(total.shape, ROWS - 1), rest, 0.0)
        lead = total.astype(BF16)
        rest = total[ROWS - 1 :] - lead[ROWS - 1 :].astype(F32)
        out_ref[t, :ROWS, :] = lead
        out_ref[t, ROWS:, :] = stacked([rest, *curv], 8).astype(BF16)


def residual_kernel(idx_ref, in_ref, norm_ref, rhs_ref, grad_ref, out_ref, scalars_ref):
    tile = idx_ref[0] * QUARTER + idx_ref[1]
    total = in_ref[0].astype(F32)
    for z in range(1, ZN):
        total = total + in_ref[z].astype(F32)
    curv = total[65:66] + total[66:67] + total[67:68]
    norm = norm_ref[:1]
    step = norm / (curv + LAMBDA * norm)
    square = (ROWS, 128)
    eye = lax.broadcasted_iota(jnp.int32, square, 0) == lax.broadcasted_iota(jnp.int32, square, 1)
    column = jnp.sum(jnp.where(eye, step, 0.0), axis=1, keepdims=True)
    right = rhs_ref[:ROWS, pl.ds(pl.multiple_of(tile * 128, 128), 128)].astype(F32)
    right = jnp.where(row_is(square, ROWS - 1), grad_ref[pl.ds(tile, 1), :], right)
    residual = right - column * (joined(total) + LAMBDA * right)
    lead = residual.astype(BF16)
    rest = stacked([residual[ROWS - 1 :] - lead[ROWS - 1 :].astype(F32)], 8).astype(BF16)
    for z in range(ZN):
        out_ref[z, :ROWS, :] = lead
        out_ref[z, ROWS:, :] = rest
    scalars_ref[...] = stacked([step, curv, norm], 8)


def second_kernel(idx_ref, held_ref, rhs_ref, grad_ref, own, one, two, three, other_ref, mine_ref, first_ref, res):
    x, core = idx_ref[0], idx_ref[2]
    norm = jnp.zeros((ROWS, 128), F32)
    cross = jnp.zeros((ROWS, 128), F32)
    res[ROWS:, :] = jnp.zeros((128 - ROWS, TILES * 128), BF16)
    for k, part in enumerate((own, one, two, three)):
        quarter = lax.rem(x + XN - k, XN)
        for t in range(QUARTER):
            tile = quarter * QUARTER + t
            at = pl.ds(pl.multiple_of(tile * 128, 128), 128)
            rows = part[t]
            values = joined(rows.astype(F32))
            right = rhs_ref[:ROWS, at].astype(F32)
            right = jnp.where(row_is(right.shape, ROWS - 1), grad_ref[pl.ds(tile, 1), :], right)
            norm = norm + values * values
            cross = cross + values * right
            first_ref[pl.ds(tile, 1), :] = values[ROWS - 1 :]
            res[:ROWS, at] = rows[:ROWS]
            res[ROWS : ROWS + 16, at] = stacked([rows[ROWS:].astype(F32)[:1]], 16).astype(BF16)
    line = line_sums(norm, cross)
    lines = stacked([line, pltpu.roll(line, ROWS, 1)], 8)
    put_scores(held_ref, res, core, other_ref, mine_ref, lines)


def tail_kernel(idx_ref, own, one, two, three, scores_ref, rate_ref, tail_ref, lines_ref):
    scores, norm, cross = unpacked(own, one, two, three)
    rate = jnp.where(idx_ref[2] == 0, rate_ref[:, :HALF], rate_ref[:, HALF:])
    weighted = rate * scores
    tail_ref[...] = line_sums(tile_sums(weighted * scores_ref[...]), tile_sums(weighted * scores))
    lines_ref[...] = stacked([norm, cross], 8)


def end_kernel(tails_ref, scalars_ref, lines_ref, w_ref, grad_ref, first_ref, weights_ref, widths_ref):
    tail = tails_ref[0]
    for e in range(1, EN):
        tail = tail + tails_ref[e]
    mixed, square = tail, pltpu.roll(tail, ROWS, 1)
    step_one, curv, norm = scalars_ref[0:1], scalars_ref[1:2], scalars_ref[2:3]
    norm_next, cross = lines_ref[0:1], lines_ref[1:2]
    ratio = norm_next / norm
    curvature = square + 2.0 * ratio * mixed + ratio * ratio * curv
    curvature = curvature + LAMBDA * (norm_next + 2.0 * ratio * cross + ratio * ratio * norm)
    step_two = norm_next / curvature
    widths_ref[...] = step_one * norm + step_two * (cross + ratio * norm)
    at = slice(ROWS - 1, ROWS)
    grad = grad_ref[...]
    step = step_one[:, at] * grad + step_two[:, at] * (first_ref[...] + ratio[:, at] * grad)
    weights_ref[...] = w_ref[...] - step


def on_device(events, labels, weights, contexts):
    place = lax.axis_index("event")
    core = lax.rem(lax.axis_index("feat"), CN)
    idx = jnp.stack([place // ZN, lax.rem(place, ZN), core]).astype(jnp.int32)
    features = TILES * 128
    tiled = weights.reshape(TILES, 128)

    held, margin, picked = kernel_call(
        first_kernel,
        [SMEM, VMEM, HBM],
        [shaped(COUNT, features, dtype=BF16), shaped(COUNT // 128, 128), shaped(TILES, ROWS, 128, dtype=BF16)],
        (contexts - place * COUNT, weights.reshape(1, features), events),
        [pltpu.VMEM((ROWS, features), F32), pltpu.SemaphoreType.DMA((5,))],
        micros=4,
    )
    chunks = lax.all_to_all(picked, "event", 0, 0)

    margin = margin + core_move(margin)
    rate, grad = kernel_call(
        gradient_kernel,
        [VMEM] * 6,
        [shaped(1, COUNT), shaped(TILES, 128)],
        (held, margin, *y_moves(margin), labels.reshape(COUNT // 128, 128)),
        [pltpu.VMEM((16, COUNT), BF16)],
        micros=3,
    )
    (message,) = kernel_call(
        spread_kernel, [VMEM] * 2, [shaped(ZN, ROWS + 2 * TILES, 128, dtype=BF16)], (chunks, grad)
    )
    message = z_exchange(message)
    (message,) = kernel_call(
        collect_kernel, [VMEM], [shaped(QUARTER * ROWS + 2 * TILES, 128, dtype=BF16)], (message,)
    )

    half = [shaped(ROWS + 8, HALF), shaped(ROWS + 8, HALF)]
    rhs, grad, other, mine = kernel_call(
        scores_kernel,
        [SMEM] + [VMEM] * 6,
        [shaped(128, features, dtype=BF16), shaped(TILES, 128)] + half,
        (idx, held, tiled, message, *x_moves(message)),
        micros=3,
    )
    packed = [shaped(ROWS + 16, HALF, dtype=BF16)]
    (message,) = kernel_call(pack_kernel, [VMEM] * 2, packed, (mine, core_move(other)))
    scores, norm = kernel_call(
        unpack_kernel, [VMEM] * 4, [shaped(ROWS, HALF), shaped(8, 128)], (message, *y_moves(message))
    )

    part = shaped(QUARTER * ROWS + 16, 128, dtype=BF16)
    own, curv, one, two, three = kernel_call(
        hessian_kernel,
        [SMEM] + [VMEM] * 4,
        [shaped(QUARTER * ROWS, 128), shaped(8, 128), part, part, part],
        (idx, held, scores, core_move(scores), rate),
        [pltpu.VMEM((ROWS + 16, COUNT), BF16)],
        micros=3,
    )
    moved = [
        lax.ppermute(v, "event", [(i, (i + k * ZN) % EN) for i in range(EN)])
        for k, v in ((1, one), (2, two), (3, three))
    ]
    shard = [shaped(ZN, ROWS + 8, 128, dtype=BF16)]
    (message,) = kernel_call(cut_kernel, [VMEM] * 5, shard, (own, curv, *moved))
    message, scalars = kernel_call(
        residual_kernel,
        [SMEM] + [VMEM] * 4,
        shard + [shaped(8, 128)],
        (idx, z_exchange(message), norm, rhs, grad),
    )
    message = z_exchange(message)

    other, mine, first = kernel_call(
        second_kernel,
        [SMEM] + [VMEM] * 7,
        half + [shaped(TILES, 128)],
        (idx, held, rhs, grad, message, *x_moves(message)),
        [pltpu.VMEM((128, features), BF16)],
        micros=3,
    )
    (message,) = kernel_call(pack_kernel, [VMEM] * 2, packed, (mine, core_move(other)))
    tail, lines = kernel_call(
        tail_kernel,
        [SMEM] + [VMEM] * 6,
        [shaped(1, 128), shaped(8, 128)],
        (idx, message, *y_moves(message), scores, rate),
    )
    tail = tail + core_move(tail)
    tails = lax.all_to_all(jnp.broadcast_to(tail[None], (EN, 1, 128)), "event", 0, 0)
    updated, widths = kernel_call(
        end_kernel, [VMEM] * 6, [shaped(TILES, 128), shaped(1, 128)], (tails, scalars, lines, tiled, grad, first)
    )
    return updated.reshape(features), widths[0, : ROWS - 1]


def solution(mesh):
    in_specs = (P("event", "feat"), P("event"), P("feat"), P())
    out_specs = (P("feat"), P())
    return jax.shard_map(on_device, mesh=mesh, in_specs=in_specs, out_specs=out_specs, check_vma=False)
```

```python
import jax
import jax.numpy as jnp
from jax import lax
from jax.experimental import pallas as pl
from jax.experimental.pallas import tpu as pltpu
from jax.sharding import PartitionSpec as P

LAMBDA = 0.5
XN, ZN, YN, CN = 4, 8, 4, 2
EN = XN * ZN
ROWS = 64
TILES = 32
QUARTER = TILES // XN
COUNT = 1280
HALF = COUNT // 2
ROOM = 48
F32, BF16 = jnp.float32, jnp.bfloat16
VMEM = pl.BlockSpec(memory_space=pltpu.VMEM)
SMEM = pl.BlockSpec(memory_space=pltpu.SMEM)
HBM = pl.BlockSpec(memory_space=pltpu.HBM)
ACROSS = (((1,), (1,)), ((), ()))


def shaped(*shape, dtype=F32):
    return jax.ShapeDtypeStruct(shape, dtype)


def kernel_call(body, ins, outs, args, scratch=(), micros=0.5, room=8):
    return pl.pallas_call(
        body,
        out_shape=outs,
        in_specs=ins,
        out_specs=[VMEM] * len(outs),
        scratch_shapes=list(scratch),
        compiler_params=pltpu.CompilerParams(vmem_limit_bytes=room << 20),
        cost_estimate=pl.CostEstimate(flops=0, bytes_accessed=int(micros * 3.6e6), transcendentals=0),
    )(*args)


def x_moves(v):
    n = XN * ZN
    return [lax.ppermute(v, "event", [(i, (i + k * ZN) % n) for i in range(n)]) for k in (1, 2, 3)]


def y_moves(v):
    n = YN * CN
    return [lax.ppermute(v, "feat", [(i, (i + k * CN) % n) for i in range(n)]) for k in (1, 2, 3)]


def core_move(v):
    return lax.ppermute(v, "feat", [(i, i ^ 1) for i in range(YN * CN)])


def z_exchange(v):
    groups = [[x * ZN + z for z in range(ZN)] for x in range(XN)]
    return lax.all_to_all(v, "event", 0, 0, axis_index_groups=groups)


def four(own, one, two, three):
    return (own + two) + (one + three)


def pair_of(v):
    lead = v.astype(BF16)
    return lead, (v - lead.astype(F32)).astype(BF16)


def triple_of(v):
    lead, rest = v.astype(BF16), v
    rest = v - lead.astype(F32)
    mid = rest.astype(BF16)
    return lead, mid, (rest - mid.astype(F32)).astype(BF16)


def row_is(shape, i):
    return lax.broadcasted_iota(jnp.int32, shape, 0) == i


def stacked(lines, rows):
    out = jnp.zeros((rows, lines[0].shape[1]), F32)
    for i, line in enumerate(lines):
        out = jnp.where(row_is(out.shape, i), line.astype(F32), out)
    return out


def joined(v):
    top = v[:ROWS]
    return top + jnp.where(row_is(top.shape, ROWS - 1), v[ROWS : ROWS + 1], 0.0)


def line_sums(top, bottom):
    return jnp.sum(jnp.transpose(jnp.concatenate([top, bottom], axis=0)), axis=0, keepdims=True)


def tile_sums(v):
    total = v[:, :128]
    for t in range(1, v.shape[1] // 128):
        total = total + v[:, t * 128 : (t + 1) * 128]
    return total


def stream(events_ref, held, sems, starts, size, axis):
    copies = []
    for i, start in enumerate(starts):
        start = pl.multiple_of(start, 128)
        at = (pl.ds(start, size), slice(None)) if axis == 0 else (slice(None), pl.ds(start, size))
        copies.append((pltpu.make_async_copy(events_ref.at[at], held.at[i], sems.at[i]), i))
    for copy, _ in copies:
        copy.start()
    return copies


def pick_kernel(local_ref, events_ref, out_ref, blocks, rows, sems):
    def owned(j):
        return jnp.logical_and(local_ref[j] >= 0, local_ref[j] < COUNT)

    def fetch(j):
        start = pl.multiple_of(lax.div(local_ref[j], 16) * 16, 16)
        return pltpu.make_async_copy(events_ref.at[pl.ds(start, 16), :], blocks.at[j], sems.at[j])

    @pl.loop(0, ROWS - 1)
    def _(j):
        @pl.when(owned(j))
        def _():
            fetch(j).start()

    rows[...] = jnp.zeros_like(rows)

    @pl.loop(0, ROWS - 1)
    def _(j):
        @pl.when(owned(j))
        def _():
            fetch(j).wait()
            block = blocks[j].astype(F32)
            found = jnp.where(row_is(block.shape, lax.rem(local_ref[j], 16)), block, 0.0)
            rows[pl.ds(j, 1), :] = jnp.sum(found, axis=0, keepdims=True)

    for t in range(TILES):
        out_ref[t] = rows[:, t * 128 : (t + 1) * 128].astype(BF16)


def margin_kernel(w_ref, events_ref, _after, margin_ref, held, sems):
    copies = stream(events_ref, held, sems, [c * 256 for c in range(5)], 256, 0)
    w = jnp.broadcast_to(w_ref[...], (16, TILES * 128)).astype(BF16)
    for copy, c in copies:
        copy.wait()
        part = lax.dot_general(w, held[c], ACROSS, preferred_element_type=F32)
        margin_ref[2 * c : 2 * c + 1, :] = part[:1, :128]
        margin_ref[2 * c + 1 : 2 * c + 2, :] = part[:1, 128:]


def gradient_kernel(events_ref, own, one, two, three, labels_ref, rate_ref, grad_ref, errs, held, sems):
    copies = stream(events_ref, held, sems, [c * 1024 for c in range(4)], 1024, 1)
    margin = four(own[...], one[...], two[...], three[...])
    chance = jax.nn.sigmoid(margin)
    rate = chance * (1.0 - chance)
    errors = chance - labels_ref[...].astype(F32)
    lead, rest = pair_of(errors)
    lead, rest = lead.astype(F32), rest.astype(F32)
    for i in range(COUNT // 128):
        at = slice(i * 128, (i + 1) * 128)
        rate_ref[:, at] = rate[i : i + 1]
        errs[:, at] = stacked([lead[i : i + 1], rest[i : i + 1]], 16).astype(BF16)
    for copy, c in copies:
        copy.wait()
        part = jnp.dot(errs[...], held[c], preferred_element_type=F32)
        line = part[:1] + part[1:2]
        for u in range(QUARTER):
            at = c * QUARTER + u
            grad_ref[at : at + 1, :] = line[:, u * 128 : (u + 1) * 128]


def spread_kernel(chunks_ref, grad_ref, out_ref):
    total = chunks_ref[0].astype(F32)
    for e in range(1, EN):
        total = total + chunks_ref[e].astype(F32)
    lead, rest = pair_of(grad_ref[...])
    for z in range(ZN):
        out_ref[z, :ROWS, :] = total.astype(BF16)
        out_ref[z, ROWS : ROWS + TILES, :] = lead
        out_ref[z, ROWS + TILES :, :] = rest


def collect_kernel(in_ref, out_ref):
    grad = jnp.zeros((TILES, 128), F32)
    for z in range(ZN):
        out_ref[z * ROWS : (z + 1) * ROWS, :] = in_ref[z, :ROWS, :]
        grad = grad + (in_ref[z, ROWS : ROWS + TILES, :].astype(F32) + in_ref[z, ROWS + TILES :, :].astype(F32))
    lead, rest = pair_of(grad)
    out_ref[QUARTER * ROWS : QUARTER * ROWS + TILES, :] = lead
    out_ref[QUARTER * ROWS + TILES :, :] = rest


def half_starts(core):
    return [(half * HALF + first, size) for half in (1 - core, core) for first, size in ((0, 256), (256, 384))]


def stream_halves(events_ref, held, sems, core):
    copies = []
    at = 0
    for i, (start, size) in enumerate(half_starts(core)):
        source = events_ref.at[pl.ds(pl.multiple_of(start, 128), size), :]
        copies.append((pltpu.make_async_copy(source, held.at[pl.ds(at, size), :], sems.at[i]), at, size))
        at += size
    for copy, _, _ in copies:
        copy.start()
    return copies


def put_scores(copies, held, rhs, other_ref, own_ref, lines):
    for copy, at, size in copies:
        copy.wait()
        part = lax.dot_general(held[at : at + size, :], rhs[...], ACROSS, preferred_element_type=F32)
        out_ref = other_ref if at < HALF else own_ref
        for t in range(size // 128):
            columns = slice(at % HALF + t * 128, at % HALF + (t + 1) * 128)
            out_ref[:ROWS, columns] = joined(jnp.transpose(part[t * 128 : (t + 1) * 128]))
            out_ref[ROWS:, columns] = lines if at % HALF + t == 0 else jnp.zeros_like(lines)


def scores_kernel(
    idx_ref, events_ref, w_ref, own, one, two, three, rhs_ref, grad_ref, other_ref, mine_ref, held, sems
):
    x, core = idx_ref[0], idx_ref[2]
    copies = stream_halves(events_ref, held, sems, core)
    top = QUARTER * ROWS
    grads = [p[top : top + TILES, :].astype(F32) + p[top + TILES :, :].astype(F32) for p in (own, one, two, three)]
    grad_ref[...] = four(*grads) + LAMBDA * w_ref[...]
    norm = jnp.zeros((ROWS, 128), F32)
    rhs_ref[ROWS:, :] = jnp.zeros((128 - ROWS, TILES * 128), BF16)
    for k, part in enumerate((own, one, two, three)):
        quarter = lax.rem(x + XN - k, XN)
        for t in range(QUARTER):
            tile = quarter * QUARTER + t
            grad = grad_ref[pl.ds(tile, 1), :]
            lead, rest = pair_of(grad)
            values = part[t * ROWS : (t + 1) * ROWS, :].astype(F32)
            last = row_is(values.shape, ROWS - 1)
            exact = jnp.where(last, grad, values)
            norm = norm + exact * exact
            at = pl.ds(pl.multiple_of(tile * 128, 128), 128)
            rhs_ref[:ROWS, at] = jnp.where(last, lead.astype(F32), values).astype(BF16)
            rhs_ref[ROWS : ROWS + 16, at] = stacked([rest], 16).astype(BF16)
    line = line_sums(norm, jnp.zeros_like(norm))
    put_scores(copies, held, rhs_ref, other_ref, mine_ref, stacked([line], 8))


def pack_kernel(own, other, out_ref):
    total = own[...] + other[...]
    scores, lines = total[:ROWS], total[ROWS:]
    lead = scores.astype(BF16)
    rest = scores[ROWS - 1 :] - lead[ROWS - 1 :].astype(F32)
    out_ref[:ROWS, :] = lead
    out_ref[ROWS:, :] = stacked([rest, *triple_of(lines[:1]), *triple_of(lines[1:2])], 16).astype(BF16)


def unpacked(own, one, two, three):
    total = four(*(p[...].astype(F32) for p in (own, one, two, three)))
    first = total[65:66] + total[66:67] + total[67:68]
    second = total[68:69] + total[69:70] + total[70:71]
    return joined(total), first[:, :128], second[:, :128]


def unpack_kernel(own, one, two, three, scores_ref, norm_ref):
    scores, norm, _ = unpacked(own, one, two, three)
    scores_ref[...] = scores
    norm_ref[...] = stacked([norm], 8)


def hessian_kernel(
    idx_ref, events_ref, mine_ref, theirs_ref, rate_ref, own_ref, curv_ref, one_ref, two_ref, three_ref, q, held, sems
):
    x, core = idx_ref[0], idx_ref[2]
    outs = ((2, two_ref), (1, one_ref), (3, three_ref), (0, own_ref))
    width = QUARTER * 128
    copies = stream(events_ref, held, sems, [lax.rem(x + k, XN) * width for k, _ in outs], width, 1)
    curv = jnp.zeros((ROWS, 128), F32)
    for half in range(2):
        scores = jnp.where(core == half, mine_ref[...], theirs_ref[...])
        at = slice(half * HALF, (half + 1) * HALF)
        weighted = rate_ref[:, at] * scores
        curv = curv + tile_sums(weighted * scores)
        lead = weighted.astype(BF16)
        q[:ROWS, at] = lead
        q[ROWS:, at] = stacked([weighted[ROWS - 1 :] - lead[ROWS - 1 :].astype(F32)], 16).astype(BF16)
    triple = [v.astype(F32) for v in triple_of(line_sums(curv, jnp.zeros_like(curv)))]
    curv_ref[...] = stacked(triple, 8)
    for (copy, c), (k, out_ref) in zip(copies, outs, strict=True):
        copy.wait()
        total = joined(jnp.dot(q[...], held[c], preferred_element_type=F32))
        rests = []
        for t in range(QUARTER):
            values = total[:, t * 128 : (t + 1) * 128]
            out_ref[t * ROWS : (t + 1) * ROWS, :] = values.astype(out_ref.dtype)
            rests.append(values[ROWS - 1 :] - values[ROWS - 1 :].astype(BF16).astype(F32))
        if k:
            out_ref[QUARTER * ROWS :, :] = stacked(rests + triple, 16).astype(BF16)


def cut_kernel(own, curv_ref, one, two, three, out_ref):
    top = QUARTER * ROWS
    tails = [p[top:, :].astype(F32) for p in (one, two, three)]
    curvs = [curv_ref[0:1] + curv_ref[1:2] + curv_ref[2:3]]
    curvs += [v[QUARTER : QUARTER + 1] + v[QUARTER + 1 : QUARTER + 2] + v[QUARTER + 2 : QUARTER + 3] for v in tails]
    curv = triple_of(four(*curvs))
    for t in range(QUARTER):
        at = slice(t * ROWS, (t + 1) * ROWS)
        total = four(own[at, :], one[at, :].astype(F32), two[at, :].astype(F32), three[at, :].astype(F32))
        rest = tails[0][t : t + 1] + tails[1][t : t + 1] + tails[2][t : t + 1]
        total = total + jnp.where(row_is(total.shape, ROWS - 1), rest, 0.0)
        lead = total.astype(BF16)
        rest = total[ROWS - 1 :] - lead[ROWS - 1 :].astype(F32)
        out_ref[t, :ROWS, :] = lead
        out_ref[t, ROWS:, :] = stacked([rest, *curv], 8).astype(BF16)


def residual_kernel(idx_ref, in_ref, norm_ref, rhs_ref, grad_ref, out_ref, scalars_ref):
    tile = idx_ref[0] * QUARTER + idx_ref[1]
    total = in_ref[0].astype(F32)
    for z in range(1, ZN):
        total = total + in_ref[z].astype(F32)
    curv = total[65:66] + total[66:67] + total[67:68]
    norm = norm_ref[:1]
    step = norm / (curv + LAMBDA * norm)
    square = (ROWS, 128)
    eye = lax.broadcasted_iota(jnp.int32, square, 0) == lax.broadcasted_iota(jnp.int32, square, 1)
    column = jnp.sum(jnp.where(eye, step, 0.0), axis=1, keepdims=True)
    right = rhs_ref[:ROWS, pl.ds(pl.multiple_of(tile * 128, 128), 128)].astype(F32)
    right = jnp.where(row_is(square, ROWS - 1), grad_ref[pl.ds(tile, 1), :], right)
    residual = right - column * (joined(total) + LAMBDA * right)
    lead = residual.astype(BF16)
    rest = stacked([residual[ROWS - 1 :] - lead[ROWS - 1 :].astype(F32)], 8).astype(BF16)
    for z in range(ZN):
        out_ref[z, :ROWS, :] = lead
        out_ref[z, ROWS:, :] = rest
    scalars_ref[...] = stacked([step, curv, norm], 8)


def second_kernel(
    idx_ref, events_ref, rhs_ref, grad_ref, own, one, two, three, other_ref, mine_ref, first_ref, res, held, sems
):
    x, core = idx_ref[0], idx_ref[2]
    copies = stream_halves(events_ref, held, sems, core)
    norm = jnp.zeros((ROWS, 128), F32)
    cross = jnp.zeros((ROWS, 128), F32)
    res[ROWS:, :] = jnp.zeros((128 - ROWS, TILES * 128), BF16)
    for k, part in enumerate((own, one, two, three)):
        quarter = lax.rem(x + XN - k, XN)
        for t in range(QUARTER):
            tile = quarter * QUARTER + t
            at = pl.ds(pl.multiple_of(tile * 128, 128), 128)
            rows = part[t]
            values = joined(rows.astype(F32))
            right = rhs_ref[:ROWS, at].astype(F32)
            right = jnp.where(row_is(right.shape, ROWS - 1), grad_ref[pl.ds(tile, 1), :], right)
            norm = norm + values * values
            cross = cross + values * right
            first_ref[pl.ds(tile, 1), :] = values[ROWS - 1 :]
            res[:ROWS, at] = rows[:ROWS]
            res[ROWS : ROWS + 16, at] = stacked([rows[ROWS:].astype(F32)[:1]], 16).astype(BF16)
    line = line_sums(norm, cross)
    lines = stacked([line, pltpu.roll(line, ROWS, 1)], 8)
    put_scores(copies, held, res, other_ref, mine_ref, lines)


def tail_kernel(idx_ref, own, one, two, three, scores_ref, rate_ref, tail_ref, lines_ref):
    scores, norm, cross = unpacked(own, one, two, three)
    rate = jnp.where(idx_ref[2] == 0, rate_ref[:, :HALF], rate_ref[:, HALF:])
    weighted = rate * scores
    tail_ref[...] = line_sums(tile_sums(weighted * scores_ref[...]), tile_sums(weighted * scores))
    lines_ref[...] = stacked([norm, cross], 8)


def end_kernel(tails_ref, scalars_ref, lines_ref, w_ref, grad_ref, first_ref, weights_ref, widths_ref):
    tail = tails_ref[0]
    for e in range(1, EN):
        tail = tail + tails_ref[e]
    mixed, square = tail, pltpu.roll(tail, ROWS, 1)
    step_one, curv, norm = scalars_ref[0:1], scalars_ref[1:2], scalars_ref[2:3]
    norm_next, cross = lines_ref[0:1], lines_ref[1:2]
    ratio = norm_next / norm
    curvature = square + 2.0 * ratio * mixed + ratio * ratio * curv
    curvature = curvature + LAMBDA * (norm_next + 2.0 * ratio * cross + ratio * ratio * norm)
    step_two = norm_next / curvature
    widths_ref[...] = step_one * norm + step_two * (cross + ratio * norm)
    at = slice(ROWS - 1, ROWS)
    grad = grad_ref[...]
    step = step_one[:, at] * grad + step_two[:, at] * (first_ref[...] + ratio[:, at] * grad)
    weights_ref[...] = w_ref[...] - step


def on_device(events, labels, weights, contexts):
    place = lax.axis_index("event")
    core = lax.rem(lax.axis_index("feat"), CN)
    idx = jnp.stack([place // ZN, lax.rem(place, ZN), core]).astype(jnp.int32)
    features = TILES * 128
    tiled = weights.reshape(TILES, 128)

    (picked,) = kernel_call(
        pick_kernel,
        [SMEM, HBM],
        [shaped(TILES, ROWS, 128, dtype=BF16)],
        (contexts - place * COUNT, events),
        [
            pltpu.VMEM((ROWS - 1, 16, features), BF16),
            pltpu.VMEM((ROWS, features), F32),
            pltpu.SemaphoreType.DMA((ROWS - 1,)),
        ],
        micros=2,
        room=ROOM,
    )
    chunks = lax.all_to_all(picked, "event", 0, 0)
    (margin,) = kernel_call(
        margin_kernel,
        [VMEM, HBM, HBM],
        [shaped(COUNT // 128, 128)],
        (weights.reshape(1, features), events, picked),
        [pltpu.VMEM((5, 256, features), BF16), pltpu.SemaphoreType.DMA((5,))],
        micros=4,
        room=ROOM,
    )

    margin = margin + core_move(margin)
    rate, grad = kernel_call(
        gradient_kernel,
        [HBM] + [VMEM] * 5,
        [shaped(1, COUNT), shaped(TILES, 128)],
        (events, margin, *y_moves(margin), labels.reshape(COUNT // 128, 128)),
        [pltpu.VMEM((16, COUNT), BF16), pltpu.VMEM((4, COUNT, 1024), BF16), pltpu.SemaphoreType.DMA((4,))],
        micros=4,
        room=ROOM,
    )
    (message,) = kernel_call(
        spread_kernel, [VMEM] * 2, [shaped(ZN, ROWS + 2 * TILES, 128, dtype=BF16)], (chunks, grad)
    )
    message = z_exchange(message)
    (message,) = kernel_call(
        collect_kernel, [VMEM], [shaped(QUARTER * ROWS + 2 * TILES, 128, dtype=BF16)], (message,)
    )

    half = [shaped(ROWS + 8, HALF), shaped(ROWS + 8, HALF)]
    rhs, grad, other, mine = kernel_call(
        scores_kernel,
        [SMEM, HBM] + [VMEM] * 5,
        [shaped(128, features, dtype=BF16), shaped(TILES, 128)] + half,
        (idx, events, tiled, message, *x_moves(message)),
        [pltpu.VMEM((COUNT, features), BF16), pltpu.SemaphoreType.DMA((4,))],
        micros=4,
        room=ROOM,
    )
    packed = [shaped(ROWS + 16, HALF, dtype=BF16)]
    (message,) = kernel_call(pack_kernel, [VMEM] * 2, packed, (mine, core_move(other)))
    scores, norm = kernel_call(
        unpack_kernel, [VMEM] * 4, [shaped(ROWS, HALF), shaped(8, 128)], (message, *y_moves(message))
    )

    part = shaped(QUARTER * ROWS + 16, 128, dtype=BF16)
    own, curv, one, two, three = kernel_call(
        hessian_kernel,
        [SMEM, HBM] + [VMEM] * 3,
        [shaped(QUARTER * ROWS, 128), shaped(8, 128), part, part, part],
        (idx, events, scores, core_move(scores), rate),
        [pltpu.VMEM((ROWS + 16, COUNT), BF16), pltpu.VMEM((4, COUNT, 1024), BF16), pltpu.SemaphoreType.DMA((4,))],
        micros=4,
        room=ROOM,
    )
    moved = [
        lax.ppermute(v, "event", [(i, (i + k * ZN) % EN) for i in range(EN)])
        for k, v in ((1, one), (2, two), (3, three))
    ]
    shard = [shaped(ZN, ROWS + 8, 128, dtype=BF16)]
    (message,) = kernel_call(cut_kernel, [VMEM] * 5, shard, (own, curv, *moved))
    message, scalars = kernel_call(
        residual_kernel,
        [SMEM] + [VMEM] * 4,
        shard + [shaped(8, 128)],
        (idx, z_exchange(message), norm, rhs, grad),
    )
    message = z_exchange(message)

    other, mine, first = kernel_call(
        second_kernel,
        [SMEM, HBM] + [VMEM] * 6,
        half + [shaped(TILES, 128)],
        (idx, events, rhs, grad, message, *x_moves(message)),
        [pltpu.VMEM((128, features), BF16), pltpu.VMEM((COUNT, features), BF16), pltpu.SemaphoreType.DMA((4,))],
        micros=4,
        room=ROOM,
    )
    (message,) = kernel_call(pack_kernel, [VMEM] * 2, packed, (mine, core_move(other)))
    tail, lines = kernel_call(
        tail_kernel,
        [SMEM] + [VMEM] * 6,
        [shaped(1, 128), shaped(8, 128)],
        (idx, message, *y_moves(message), scores, rate),
    )
    tail = tail + core_move(tail)
    tails = lax.all_to_all(jnp.broadcast_to(tail[None], (EN, 1, 128)), "event", 0, 0)
    updated, widths = kernel_call(
        end_kernel, [VMEM] * 6, [shaped(TILES, 128), shaped(1, 128)], (tails, scalars, lines, tiled, grad, first)
    )
    return updated.reshape(features), widths[0, : ROWS - 1]


def solution(mesh):
    in_specs = (P("event", "feat"), P("event"), P("feat"), P())
    out_specs = (P("feat"), P())
    return jax.shard_map(on_device, mesh=mesh, in_specs=in_specs, out_specs=out_specs, check_vma=False)
```

```python
import jax
import jax.numpy as jnp
from jax import lax
from jax.experimental import pallas as pl
from jax.experimental.pallas import tpu as pltpu
from jax.sharding import PartitionSpec as P

LAMBDA = 0.5
XN, ZN, YN, CN = 4, 8, 4, 2
EN = XN * ZN
ROWS = 64
TILES = 32
QUARTER = TILES // XN
COUNT = 1280
HALF = COUNT // 2
WINDOW = 4
ROOM = 48
F32, BF16 = jnp.float32, jnp.bfloat16
VMEM = pl.BlockSpec(memory_space=pltpu.VMEM)
SMEM = pl.BlockSpec(memory_space=pltpu.SMEM)
HBM = pl.BlockSpec(memory_space=pltpu.HBM)
ACROSS = (((1,), (1,)), ((), ()))


def shaped(*shape, dtype=F32):
    return jax.ShapeDtypeStruct(shape, dtype)


def kernel_call(body, ins, outs, args, scratch=(), micros=0.5, room=8):
    return pl.pallas_call(
        body,
        out_shape=outs,
        in_specs=ins,
        out_specs=[VMEM] * len(outs),
        scratch_shapes=list(scratch),
        compiler_params=pltpu.CompilerParams(vmem_limit_bytes=room << 20),
        cost_estimate=pl.CostEstimate(flops=0, bytes_accessed=int(micros * 3.6e6), transcendentals=0),
    )(*args)


def x_moves(v):
    n = XN * ZN
    return [lax.ppermute(v, "event", [(i, (i + k * ZN) % n) for i in range(n)]) for k in (1, 2, 3)]


def y_moves(v):
    n = YN * CN
    return [lax.ppermute(v, "feat", [(i, (i + k * CN) % n) for i in range(n)]) for k in (1, 2, 3)]


def core_move(v):
    return lax.ppermute(v, "feat", [(i, i ^ 1) for i in range(YN * CN)])


def z_exchange(v):
    groups = [[x * ZN + z for z in range(ZN)] for x in range(XN)]
    return lax.all_to_all(v, "event", 0, 0, axis_index_groups=groups)


def four(own, one, two, three):
    return (own + two) + (one + three)


def pair_of(v):
    lead = v.astype(BF16)
    return lead, (v - lead.astype(F32)).astype(BF16)


def triple_of(v):
    lead, rest = v.astype(BF16), v
    rest = v - lead.astype(F32)
    mid = rest.astype(BF16)
    return lead, mid, (rest - mid.astype(F32)).astype(BF16)


def row_is(shape, i):
    return lax.broadcasted_iota(jnp.int32, shape, 0) == i


def stacked(lines, rows):
    out = jnp.zeros((rows, lines[0].shape[1]), F32)
    for i, line in enumerate(lines):
        out = jnp.where(row_is(out.shape, i), line.astype(F32), out)
    return out


def joined(v):
    top = v[:ROWS]
    return top + jnp.where(row_is(top.shape, ROWS - 1), v[ROWS : ROWS + 1], 0.0)


def line_sums(top, bottom):
    return jnp.sum(jnp.transpose(jnp.concatenate([top, bottom], axis=0)), axis=0, keepdims=True)


def tile_sums(v):
    total = v[:, :128]
    for t in range(1, v.shape[1] // 128):
        total = total + v[:, t * 128 : (t + 1) * 128]
    return total


class Stream:
    def __init__(self, pieces, sems):
        self.copies = [pltpu.make_async_copy(source, target, sems.at[i]) for i, (source, target) in enumerate(pieces)]
        for copy in self.copies[:WINDOW]:
            copy.start()

    def take(self, i):
        self.copies[i].wait()
        if i + WINDOW < len(self.copies):
            self.copies[i + WINDOW].start()


def row_stream(events_ref, held, sems, starts):
    pieces = [
        (events_ref.at[pl.ds(pl.multiple_of(start, 128), 128), :], held.at[pl.ds(i * 128, 128), :])
        for i, start in enumerate(starts)
    ]
    return Stream(pieces, sems)


def column_stream(events_ref, held, sems, starts):
    pieces = [
        (events_ref.at[:, pl.ds(pl.multiple_of(start, 512), 512)], held.at[i]) for i, start in enumerate(starts)
    ]
    return Stream(pieces, sems)


def place():
    event = lax.axis_index("event")
    return lax.div(event, ZN), lax.rem(event, ZN), lax.rem(lax.axis_index("feat"), CN)


def first_kernel(contexts_ref, w_ref, events_ref, margin_ref, out_ref, rhs, rows, held, sems):
    pieces = row_stream(events_ref, held, sems, [i * 128 for i in range(COUNT // 128)])
    rhs[:16, :] = jnp.broadcast_to(w_ref[...], (16, TILES * 128)).astype(BF16)
    rhs[16:, :] = jnp.zeros((112, TILES * 128), BF16)
    rows[...] = jnp.zeros_like(rows)
    for c in range(0, COUNT // 128, 2):
        pieces.take(c)
        pieces.take(c + 1)
        part = lax.dot_general(
            held[c * 128 : (c + 2) * 128, :], rhs[...], ACROSS, preferred_element_type=F32
        )
        for u in range(2):
            margin_ref[c + u : c + u + 1, :] = jnp.transpose(part[u * 128 : (u + 1) * 128])[:1]

    base = lax.axis_index("event") * COUNT

    @pl.loop(0, ROWS - 1)
    def _(j):
        r = contexts_ref[j] - base

        @pl.when(jnp.logical_and(r >= 0, r < COUNT))
        def _():
            start = pl.multiple_of(lax.div(r, 16) * 16, 16)
            block = held[pl.ds(start, 16), :].astype(F32)
            found = jnp.where(row_is(block.shape, lax.rem(r, 16)), block, 0.0)
            rows[pl.ds(j, 1), :] = jnp.sum(found, axis=0, keepdims=True)

    for t in range(TILES):
        out_ref[t] = rows[:, t * 128 : (t + 1) * 128].astype(BF16)


def gradient_kernel(events_ref, own, one, two, three, labels_ref, rate_ref, grad_ref, errs, held, sems):
    pieces = column_stream(events_ref, held, sems, [c * 512 for c in range(8)])
    margin = four(own[...], one[...], two[...], three[...])
    chance = jax.nn.sigmoid(margin)
    rate = chance * (1.0 - chance)
    errors = chance - labels_ref[...].astype(F32)
    lead, rest = pair_of(errors)
    lead, rest = lead.astype(F32), rest.astype(F32)
    for i in range(COUNT // 128):
        at = slice(i * 128, (i + 1) * 128)
        rate_ref[:, at] = rate[i : i + 1]
        errs[:, at] = stacked([lead[i : i + 1], rest[i : i + 1]], 16).astype(BF16)
    for c in range(8):
        pieces.take(c)
        part = jnp.dot(errs[...], held[c], preferred_element_type=F32)
        line = part[:1] + part[1:2]
        for u in range(4):
            grad_ref[c * 4 + u : c * 4 + u + 1, :] = line[:, u * 128 : (u + 1) * 128]


def spread_kernel(chunks_ref, grad_ref, out_ref):
    total = chunks_ref[0].astype(F32)
    for e in range(1, EN):
        total = total + chunks_ref[e].astype(F32)
    lead, rest = pair_of(grad_ref[...])
    for z in range(ZN):
        out_ref[z, :ROWS, :] = total.astype(BF16)
        out_ref[z, ROWS : ROWS + TILES, :] = lead
        out_ref[z, ROWS + TILES :, :] = rest


def collect_kernel(in_ref, out_ref):
    grad = jnp.zeros((TILES, 128), F32)
    for z in range(ZN):
        out_ref[z * ROWS : (z + 1) * ROWS, :] = in_ref[z, :ROWS, :]
        grad = grad + (in_ref[z, ROWS : ROWS + TILES, :].astype(F32) + in_ref[z, ROWS + TILES :, :].astype(F32))
    lead, rest = pair_of(grad)
    out_ref[QUARTER * ROWS : QUARTER * ROWS + TILES, :] = lead
    out_ref[QUARTER * ROWS + TILES :, :] = rest


def half_stream(events_ref, held, sems, core):
    starts = [half * HALF + i * 128 for half in (1 - core, core) for i in range(HALF // 128)]
    return row_stream(events_ref, held, sems, starts)


def put_scores(pieces, held, rhs, other_ref, own_ref, lines):
    for first, out_ref in ((0, other_ref), (HALF // 128, own_ref)):
        for at, size in ((0, 2), (2, 3)):
            for i in range(size):
                pieces.take(first + at + i)
            events = held[(first + at) * 128 : (first + at + size) * 128, :]
            part = lax.dot_general(events, rhs[...], ACROSS, preferred_element_type=F32)
            for t in range(size):
                columns = slice((at + t) * 128, (at + t + 1) * 128)
                out_ref[:ROWS, columns] = joined(jnp.transpose(part[t * 128 : (t + 1) * 128]))
                out_ref[ROWS:, columns] = lines if at + t == 0 else jnp.zeros_like(lines)


def scores_kernel(
    events_ref, w_ref, own, one, two, three, rhs_ref, grad_ref, other_ref, mine_ref, held, sems
):
    x, _, core = place()
    pieces = half_stream(events_ref, held, sems, core)
    top = QUARTER * ROWS
    grads = [p[top : top + TILES, :].astype(F32) + p[top + TILES :, :].astype(F32) for p in (own, one, two, three)]
    grad_ref[...] = four(*grads) + LAMBDA * w_ref[...]
    norm = jnp.zeros((ROWS, 128), F32)
    rhs_ref[ROWS:, :] = jnp.zeros((128 - ROWS, TILES * 128), BF16)
    for k, part in enumerate((own, one, two, three)):
        quarter = lax.rem(x + XN - k, XN)
        for t in range(QUARTER):
            tile = quarter * QUARTER + t
            grad = grad_ref[pl.ds(tile, 1), :]
            lead, rest = pair_of(grad)
            values = part[t * ROWS : (t + 1) * ROWS, :].astype(F32)
            last = row_is(values.shape, ROWS - 1)
            exact = jnp.where(last, grad, values)
            norm = norm + exact * exact
            at = pl.ds(pl.multiple_of(tile * 128, 128), 128)
            rhs_ref[:ROWS, at] = jnp.where(last, lead.astype(F32), values).astype(BF16)
            rhs_ref[ROWS : ROWS + 16, at] = stacked([rest], 16).astype(BF16)
    line = line_sums(norm, jnp.zeros_like(norm))
    put_scores(pieces, held, rhs_ref, other_ref, mine_ref, stacked([line], 8))


def pack_kernel(own, other, out_ref):
    total = own[...] + other[...]
    scores, lines = total[:ROWS], total[ROWS:]
    lead = scores.astype(BF16)
    rest = scores[ROWS - 1 :] - lead[ROWS - 1 :].astype(F32)
    out_ref[:ROWS, :] = lead
    out_ref[ROWS:, :] = stacked([rest, *triple_of(lines[:1]), *triple_of(lines[1:2])], 16).astype(BF16)


def unpacked(own, one, two, three):
    total = four(*(p[...].astype(F32) for p in (own, one, two, three)))
    first = total[65:66] + total[66:67] + total[67:68]
    second = total[68:69] + total[69:70] + total[70:71]
    return joined(total), first[:, :128], second[:, :128]


def unpack_kernel(own, one, two, three, scores_ref, norm_ref):
    scores, norm, _ = unpacked(own, one, two, three)
    scores_ref[...] = scores
    norm_ref[...] = stacked([norm], 8)


def hessian_kernel(
    events_ref, mine_ref, theirs_ref, rate_ref, own_ref, curv_ref, one_ref, two_ref, three_ref, q, held, sems
):
    x, _, core = place()
    outs = ((2, two_ref), (1, one_ref), (3, three_ref), (0, own_ref))
    starts = [lax.rem(x + k, XN) * QUARTER * 128 + part * 512 for k, _ in outs for part in range(2)]
    pieces = column_stream(events_ref, held, sems, starts)
    curv = jnp.zeros((ROWS, 128), F32)
    for half in range(2):
        scores = jnp.where(core == half, mine_ref[...], theirs_ref[...])
        at = slice(half * HALF, (half + 1) * HALF)
        weighted = rate_ref[:, at] * scores
        curv = curv + tile_sums(weighted * scores)
        lead = weighted.astype(BF16)
        q[:ROWS, at] = lead
        q[ROWS:, at] = stacked([weighted[ROWS - 1 :] - lead[ROWS - 1 :].astype(F32)], 16).astype(BF16)
    triple = [v.astype(F32) for v in triple_of(line_sums(curv, jnp.zeros_like(curv)))]
    curv_ref[...] = stacked(triple, 8)
    for i, (k, out_ref) in enumerate(outs):
        rests = []
        for part in range(2):
            pieces.take(2 * i + part)
            total = joined(jnp.dot(q[...], held[2 * i + part], preferred_element_type=F32))
            for u in range(4):
                t = part * 4 + u
                values = total[:, u * 128 : (u + 1) * 128]
                out_ref[t * ROWS : (t + 1) * ROWS, :] = values.astype(out_ref.dtype)
                rests.append(values[ROWS - 1 :] - values[ROWS - 1 :].astype(BF16).astype(F32))
        if k:
            out_ref[QUARTER * ROWS :, :] = stacked(rests + triple, 16).astype(BF16)


def cut_kernel(own, curv_ref, one, two, three, out_ref):
    top = QUARTER * ROWS
    tails = [p[top:, :].astype(F32) for p in (one, two, three)]
    curvs = [curv_ref[0:1] + curv_ref[1:2] + curv_ref[2:3]]
    curvs += [v[QUARTER : QUARTER + 1] + v[QUARTER + 1 : QUARTER + 2] + v[QUARTER + 2 : QUARTER + 3] for v in tails]
    curv = triple_of(four(*curvs))
    for t in range(QUARTER):
        at = slice(t * ROWS, (t + 1) * ROWS)
        total = four(own[at, :], one[at, :].astype(F32), two[at, :].astype(F32), three[at, :].astype(F32))
        rest = tails[0][t : t + 1] + tails[1][t : t + 1] + tails[2][t : t + 1]
        total = total + jnp.where(row_is(total.shape, ROWS - 1), rest, 0.0)
        lead = total.astype(BF16)
        rest = total[ROWS - 1 :] - lead[ROWS - 1 :].astype(F32)
        out_ref[t, :ROWS, :] = lead
        out_ref[t, ROWS:, :] = stacked([rest, *curv], 8).astype(BF16)


def residual_kernel(in_ref, norm_ref, rhs_ref, grad_ref, out_ref, scalars_ref):
    x, z, _ = place()
    tile = x * QUARTER + z
    total = in_ref[0].astype(F32)
    for z in range(1, ZN):
        total = total + in_ref[z].astype(F32)
    curv = total[65:66] + total[66:67] + total[67:68]
    norm = norm_ref[:1]
    step = norm / (curv + LAMBDA * norm)
    square = (ROWS, 128)
    eye = lax.broadcasted_iota(jnp.int32, square, 0) == lax.broadcasted_iota(jnp.int32, square, 1)
    column = jnp.sum(jnp.where(eye, step, 0.0), axis=1, keepdims=True)
    right = rhs_ref[:ROWS, pl.ds(pl.multiple_of(tile * 128, 128), 128)].astype(F32)
    right = jnp.where(row_is(square, ROWS - 1), grad_ref[pl.ds(tile, 1), :], right)
    residual = right - column * (joined(total) + LAMBDA * right)
    lead = residual.astype(BF16)
    rest = stacked([residual[ROWS - 1 :] - lead[ROWS - 1 :].astype(F32)], 8).astype(BF16)
    for z in range(ZN):
        out_ref[z, :ROWS, :] = lead
        out_ref[z, ROWS:, :] = rest
    scalars_ref[...] = stacked([step, curv, norm], 8)


def second_kernel(
    events_ref, rhs_ref, grad_ref, own, one, two, three, other_ref, mine_ref, first_ref, res, held, sems
):
    x, _, core = place()
    pieces = half_stream(events_ref, held, sems, core)
    norm = jnp.zeros((ROWS, 128), F32)
    cross = jnp.zeros((ROWS, 128), F32)
    res[ROWS:, :] = jnp.zeros((128 - ROWS, TILES * 128), BF16)
    for k, part in enumerate((own, one, two, three)):
        quarter = lax.rem(x + XN - k, XN)
        for t in range(QUARTER):
            tile = quarter * QUARTER + t
            at = pl.ds(pl.multiple_of(tile * 128, 128), 128)
            rows = part[t]
            values = joined(rows.astype(F32))
            right = rhs_ref[:ROWS, at].astype(F32)
            right = jnp.where(row_is(right.shape, ROWS - 1), grad_ref[pl.ds(tile, 1), :], right)
            norm = norm + values * values
            cross = cross + values * right
            first_ref[pl.ds(tile, 1), :] = values[ROWS - 1 :]
            res[:ROWS, at] = rows[:ROWS]
            res[ROWS : ROWS + 16, at] = stacked([rows[ROWS:].astype(F32)[:1]], 16).astype(BF16)
    line = line_sums(norm, cross)
    lines = stacked([line, pltpu.roll(line, ROWS, 1)], 8)
    put_scores(pieces, held, res, other_ref, mine_ref, lines)


def tail_kernel(own, one, two, three, scores_ref, rate_ref, tail_ref, lines_ref):
    scores, norm, cross = unpacked(own, one, two, three)
    rate = jnp.where(place()[2] == 0, rate_ref[:, :HALF], rate_ref[:, HALF:])
    weighted = rate * scores
    tail_ref[...] = line_sums(tile_sums(weighted * scores_ref[...]), tile_sums(weighted * scores))
    lines_ref[...] = stacked([norm, cross], 8)


def end_kernel(tails_ref, scalars_ref, lines_ref, w_ref, grad_ref, first_ref, weights_ref, widths_ref):
    tail = tails_ref[0]
    for e in range(1, EN):
        tail = tail + tails_ref[e]
    mixed, square = tail, pltpu.roll(tail, ROWS, 1)
    step_one, curv, norm = scalars_ref[0:1], scalars_ref[1:2], scalars_ref[2:3]
    norm_next, cross = lines_ref[0:1], lines_ref[1:2]
    ratio = norm_next / norm
    curvature = square + 2.0 * ratio * mixed + ratio * ratio * curv
    curvature = curvature + LAMBDA * (norm_next + 2.0 * ratio * cross + ratio * ratio * norm)
    step_two = norm_next / curvature
    widths_ref[...] = step_one * norm + step_two * (cross + ratio * norm)
    at = slice(ROWS - 1, ROWS)
    grad = grad_ref[...]
    step = step_one[:, at] * grad + step_two[:, at] * (first_ref[...] + ratio[:, at] * grad)
    weights_ref[...] = w_ref[...] - step


def on_device(events, labels, weights, contexts):
    features = TILES * 128
    tiled = weights.reshape(TILES, 128)

    rows = [pltpu.VMEM((COUNT, features), BF16), pltpu.SemaphoreType.DMA((10,))]
    columns = [pltpu.VMEM((8, COUNT, 512), BF16), pltpu.SemaphoreType.DMA((8,))]

    margin, picked = kernel_call(
        first_kernel,
        [SMEM, VMEM, HBM],
        [shaped(COUNT // 128, 128), shaped(TILES, ROWS, 128, dtype=BF16)],
        (contexts, weights.reshape(1, features), events),
        [pltpu.VMEM((128, features), BF16), pltpu.VMEM((ROWS, features), F32), *rows],
        micros=6,
        room=ROOM,
    )
    chunks = lax.all_to_all(picked, "event", 0, 0)

    margin = margin + core_move(margin)
    rate, grad = kernel_call(
        gradient_kernel,
        [HBM] + [VMEM] * 5,
        [shaped(1, COUNT), shaped(TILES, 128)],
        (events, margin, *y_moves(margin), labels.reshape(COUNT // 128, 128)),
        [pltpu.VMEM((16, COUNT), BF16), *columns],
        micros=4,
        room=ROOM,
    )
    (message,) = kernel_call(
        spread_kernel, [VMEM] * 2, [shaped(ZN, ROWS + 2 * TILES, 128, dtype=BF16)], (chunks, grad)
    )
    message = z_exchange(message)
    (message,) = kernel_call(
        collect_kernel, [VMEM], [shaped(QUARTER * ROWS + 2 * TILES, 128, dtype=BF16)], (message,)
    )

    half = [shaped(ROWS + 8, HALF), shaped(ROWS + 8, HALF)]
    rhs, grad, other, mine = kernel_call(
        scores_kernel,
        [HBM] + [VMEM] * 5,
        [shaped(128, features, dtype=BF16), shaped(TILES, 128)] + half,
        (events, tiled, message, *x_moves(message)),
        rows,
        micros=4,
        room=ROOM,
    )
    packed = [shaped(ROWS + 16, HALF, dtype=BF16)]
    (message,) = kernel_call(pack_kernel, [VMEM] * 2, packed, (mine, core_move(other)))
    scores, norm = kernel_call(
        unpack_kernel, [VMEM] * 4, [shaped(ROWS, HALF), shaped(8, 128)], (message, *y_moves(message))
    )

    part = shaped(QUARTER * ROWS + 16, 128, dtype=BF16)
    own, curv, one, two, three = kernel_call(
        hessian_kernel,
        [HBM] + [VMEM] * 3,
        [shaped(QUARTER * ROWS, 128), shaped(8, 128), part, part, part],
        (events, scores, core_move(scores), rate),
        [pltpu.VMEM((ROWS + 16, COUNT), BF16), *columns],
        micros=4,
        room=ROOM,
    )
    moved = [
        lax.ppermute(v, "event", [(i, (i + k * ZN) % EN) for i in range(EN)])
        for k, v in ((1, one), (2, two), (3, three))
    ]
    shard = [shaped(ZN, ROWS + 8, 128, dtype=BF16)]
    (message,) = kernel_call(cut_kernel, [VMEM] * 5, shard, (own, curv, *moved))
    message, scalars = kernel_call(
        residual_kernel,
        [VMEM] * 4,
        shard + [shaped(8, 128)],
        (z_exchange(message), norm, rhs, grad),
    )
    message = z_exchange(message)

    other, mine, first = kernel_call(
        second_kernel,
        [HBM] + [VMEM] * 6,
        half + [shaped(TILES, 128)],
        (events, rhs, grad, message, *x_moves(message)),
        [pltpu.VMEM((128, features), BF16), *rows],
        micros=4,
        room=ROOM,
    )
    (message,) = kernel_call(pack_kernel, [VMEM] * 2, packed, (mine, core_move(other)))
    tail, lines = kernel_call(
        tail_kernel,
        [VMEM] * 6,
        [shaped(1, 128), shaped(8, 128)],
        (message, *y_moves(message), scores, rate),
    )
    tail = tail + core_move(tail)
    tails = lax.all_to_all(jnp.broadcast_to(tail[None], (EN, 1, 128)), "event", 0, 0)
    updated, widths = kernel_call(
        end_kernel, [VMEM] * 6, [shaped(TILES, 128), shaped(1, 128)], (tails, scalars, lines, tiled, grad, first)
    )
    return updated.reshape(features), widths[0, : ROWS - 1]


def solution(mesh):
    in_specs = (P("event", "feat"), P("event"), P("feat"), P())
    out_specs = (P("feat"), P())
    return jax.shard_map(on_device, mesh=mesh, in_specs=in_specs, out_specs=out_specs, check_vma=False)
```

```python
import jax
import jax.numpy as jnp
from jax import lax
from jax.experimental import pallas as pl
from jax.experimental.pallas import tpu as pltpu
from jax.sharding import PartitionSpec as P

LAMBDA = 0.5
XN, ZN, YN, CN = 4, 8, 4, 2
EN = XN * ZN
ROWS = 64
TILES = 32
QUARTER = TILES // XN
COUNT = 1280
HALF = COUNT // 2
WINDOW = 4
ROOM = 48
F32, BF16 = jnp.float32, jnp.bfloat16
VMEM = pl.BlockSpec(memory_space=pltpu.VMEM)
SMEM = pl.BlockSpec(memory_space=pltpu.SMEM)
HBM = pl.BlockSpec(memory_space=pltpu.HBM)
ACROSS = (((1,), (1,)), ((), ()))


def shaped(*shape, dtype=F32):
    return jax.ShapeDtypeStruct(shape, dtype)


def kernel_call(body, ins, outs, args, scratch=(), micros=0.5, room=8):
    return pl.pallas_call(
        body,
        out_shape=outs,
        in_specs=ins,
        out_specs=[VMEM] * len(outs),
        scratch_shapes=list(scratch),
        compiler_params=pltpu.CompilerParams(vmem_limit_bytes=room << 20),
        cost_estimate=pl.CostEstimate(flops=0, bytes_accessed=int(micros * 3.6e6), transcendentals=0),
    )(*args)


def x_moves(v):
    n = XN * ZN
    return [lax.ppermute(v, "event", [(i, (i + k * ZN) % n) for i in range(n)]) for k in (1, 2, 3)]


def y_moves(v):
    n = YN * CN
    return [lax.ppermute(v, "feat", [(i, (i + k * CN) % n) for i in range(n)]) for k in (1, 2, 3)]


def core_move(v):
    return lax.ppermute(v, "feat", [(i, i ^ 1) for i in range(YN * CN)])


def z_exchange(v):
    groups = [[x * ZN + z for z in range(ZN)] for x in range(XN)]
    return lax.all_to_all(v, "event", 0, 0, axis_index_groups=groups)


def four(own, one, two, three):
    return (own + two) + (one + three)


def pair_of(v):
    lead = v.astype(BF16)
    return lead, (v - lead.astype(F32)).astype(BF16)


def triple_of(v):
    lead, rest = v.astype(BF16), v
    rest = v - lead.astype(F32)
    mid = rest.astype(BF16)
    return lead, mid, (rest - mid.astype(F32)).astype(BF16)


def row_is(shape, i):
    return lax.broadcasted_iota(jnp.int32, shape, 0) == i


def stacked(lines, rows):
    out = jnp.zeros((rows, lines[0].shape[1]), F32)
    for i, line in enumerate(lines):
        out = jnp.where(row_is(out.shape, i), line.astype(F32), out)
    return out


def joined(v):
    top = v[:ROWS]
    return top + jnp.where(row_is(top.shape, ROWS - 1), v[ROWS : ROWS + 1], 0.0)


def line_sums(top, bottom):
    return jnp.sum(jnp.transpose(jnp.concatenate([top, bottom], axis=0)), axis=0, keepdims=True)


def tile_sums(v):
    total = v[:, :128]
    for t in range(1, v.shape[1] // 128):
        total = total + v[:, t * 128 : (t + 1) * 128]
    return total


class Stream:
    def __init__(self, pieces, sems):
        self.copies = [pltpu.make_async_copy(source, target, sems.at[i]) for i, (source, target) in enumerate(pieces)]
        for copy in self.copies[:WINDOW]:
            copy.start()

    def take(self, i):
        self.copies[i].wait()
        if i + WINDOW < len(self.copies):
            self.copies[i + WINDOW].start()


class Rows:
    def __init__(self, events_ref, held, sems, starts):
        self.events, self.held = events_ref, held
        self.starts = [pl.multiple_of(start, 128) for start in starts]
        if held is not None:
            pieces = [
                (events_ref.at[pl.ds(start, 128), :], held.at[pl.ds(i * 128, 128), :])
                for i, start in enumerate(self.starts)
            ]
            self.stream = Stream(pieces, sems)

    def take(self, first, count):
        if self.held is None:
            return self.events[pl.ds(self.starts[first], count * 128), :]
        for i in range(count):
            self.stream.take(first + i)
        return self.held[first * 128 : (first + count) * 128, :]


class Columns:
    def __init__(self, events_ref, held, sems, starts):
        self.events, self.held = events_ref, held
        self.starts = [pl.multiple_of(start, 512) for start in starts]
        if held is not None:
            pieces = [(events_ref.at[:, pl.ds(start, 512)], held.at[i]) for i, start in enumerate(self.starts)]
            self.stream = Stream(pieces, sems)

    def take(self, i):
        if self.held is None:
            return self.events[:, pl.ds(self.starts[i], 512)]
        self.stream.take(i)
        return self.held[i]


def place():
    event = lax.axis_index("event")
    return lax.div(event, ZN), lax.rem(event, ZN), lax.rem(lax.axis_index("feat"), CN)


def first_kernel(contexts_ref, w_ref, events_ref, margin_ref, out_ref, w, rows, held, sems, w_sem):
    pieces = Rows(events_ref, held, sems, [i * 128 for i in range(COUNT // 128)])
    w_copy = pltpu.make_async_copy(w_ref, w, w_sem)
    w_copy.start()
    rows[...] = jnp.zeros_like(rows)
    w_copy.wait()
    w[...] = w[...].astype(BF16).astype(F32)
    for c in range(COUNT // 128):
        pieces.take(c, 1)
        sums = []
        for r in range(c * 128, (c + 1) * 128, 16):
            total = jnp.zeros((16, 128), F32)
            for t in range(TILES):
                at = slice(t * 128, (t + 1) * 128)
                total = total + held[r : r + 16, at].astype(F32) * w[:, at]
            sums.append(total)
        turned = jnp.transpose(jnp.concatenate(sums, axis=0))
        margin_ref[c : c + 1, :] = jnp.sum(turned, axis=0, keepdims=True)

    base = lax.axis_index("event") * COUNT

    @pl.loop(0, ROWS - 1)
    def _(j):
        r = contexts_ref[j] - base

        @pl.when(jnp.logical_and(r >= 0, r < COUNT))
        def _():
            start = pl.multiple_of(lax.div(r, 16) * 16, 16)
            block = held[pl.ds(start, 16), :].astype(F32)
            found = jnp.where(row_is(block.shape, lax.rem(r, 16)), block, 0.0)
            rows[pl.ds(j, 1), :] = jnp.sum(found, axis=0, keepdims=True)

    for t in range(TILES):
        out_ref[t] = rows[:, t * 128 : (t + 1) * 128].astype(BF16)


def gradient_kernel(events_ref, own, one, two, three, labels_ref, rate_ref, grad_ref, errs, held=None, sems=None):
    pieces = Columns(events_ref, held, sems, [c * 512 for c in range(8)])
    margin = four(own[...], one[...], two[...], three[...])
    chance = jax.nn.sigmoid(margin)
    rate = chance * (1.0 - chance)
    errors = chance - labels_ref[...].astype(F32)
    lead, rest = pair_of(errors)
    lead, rest = lead.astype(F32), rest.astype(F32)
    for i in range(COUNT // 128):
        at = slice(i * 128, (i + 1) * 128)
        rate_ref[:, at] = rate[i : i + 1]
        errs[:, at] = stacked([lead[i : i + 1], rest[i : i + 1]], 16).astype(BF16)
    for c in range(8):
        part = jnp.dot(errs[...], pieces.take(c), preferred_element_type=F32)
        line = part[:1] + part[1:2]
        for u in range(4):
            grad_ref[c * 4 + u : c * 4 + u + 1, :] = line[:, u * 128 : (u + 1) * 128]


def spread_kernel(chunks_ref, grad_ref, out_ref):
    total = chunks_ref[0].astype(F32)
    for e in range(1, EN):
        total = total + chunks_ref[e].astype(F32)
    lead, rest = pair_of(grad_ref[...])
    for z in range(ZN):
        out_ref[z, :ROWS, :] = total.astype(BF16)
        out_ref[z, ROWS : ROWS + TILES, :] = lead
        out_ref[z, ROWS + TILES :, :] = rest


def collect_kernel(in_ref, out_ref):
    grad = jnp.zeros((TILES, 128), F32)
    for z in range(ZN):
        out_ref[z * ROWS : (z + 1) * ROWS, :] = in_ref[z, :ROWS, :]
        grad = grad + (in_ref[z, ROWS : ROWS + TILES, :].astype(F32) + in_ref[z, ROWS + TILES :, :].astype(F32))
    lead, rest = pair_of(grad)
    out_ref[QUARTER * ROWS : QUARTER * ROWS + TILES, :] = lead
    out_ref[QUARTER * ROWS + TILES :, :] = rest


def half_stream(events_ref, held, sems, core):
    starts = [half * HALF + i * 128 for half in (1 - core, core) for i in range(HALF // 128)]
    return Rows(events_ref, held, sems, starts)


def put_scores(pieces, rhs, other_ref, own_ref, lines):
    for first, out_ref in ((0, other_ref), (HALF // 128, own_ref)):
        for at, size in ((0, 2), (2, 3)):
            part = jnp.dot(pieces.take(first + at, size), rhs[...], preferred_element_type=F32)
            for t in range(size):
                columns = slice((at + t) * 128, (at + t + 1) * 128)
                out_ref[:ROWS, columns] = joined(jnp.transpose(part[t * 128 : (t + 1) * 128]))
                out_ref[ROWS:, columns] = lines if at + t == 0 else jnp.zeros_like(lines)


def turned(top, rest):
    below = jnp.where(row_is(top.shape, 0), rest.astype(F32), 0.0)
    return jnp.transpose(jnp.concatenate([top, below], axis=0)).astype(BF16)


def scores_kernel(
    events_ref, w_ref, own, one, two, three, rhs_ref, grad_ref, other_ref, mine_ref, rhs, held=None, sems=None
):
    x, _, core = place()
    pieces = half_stream(events_ref, held, sems, core)
    tail = QUARTER * ROWS
    grads = [p[tail : tail + TILES, :].astype(F32) + p[tail + TILES :, :].astype(F32) for p in (own, one, two, three)]
    grad_ref[...] = four(*grads) + LAMBDA * w_ref[...]
    norm = jnp.zeros((ROWS, 128), F32)
    for k, part in enumerate((own, one, two, three)):
        quarter = lax.rem(x + XN - k, XN)
        for t in range(QUARTER):
            tile = quarter * QUARTER + t
            grad = grad_ref[pl.ds(tile, 1), :]
            lead, rest = pair_of(grad)
            values = part[t * ROWS : (t + 1) * ROWS, :].astype(F32)
            last = row_is(values.shape, ROWS - 1)
            exact = jnp.where(last, grad, values)
            norm = norm + exact * exact
            at = pl.ds(pl.multiple_of(tile * 128, 128), 128)
            top = jnp.where(last, lead.astype(F32), values)
            rhs_ref[:, at] = top.astype(BF16)
            rhs[at, :] = turned(top, rest)
    line = line_sums(norm, jnp.zeros_like(norm))
    put_scores(pieces, rhs, other_ref, mine_ref, stacked([line], 8))


def pack_kernel(own, other, out_ref):
    total = own[...] + other[...]
    scores, lines = total[:ROWS], total[ROWS:]
    lead = scores.astype(BF16)
    rest = scores[ROWS - 1 :] - lead[ROWS - 1 :].astype(F32)
    out_ref[:ROWS, :] = lead
    out_ref[ROWS:, :] = stacked([rest, *triple_of(lines[:1]), *triple_of(lines[1:2])], 16).astype(BF16)


def unpacked(own, one, two, three):
    total = four(*(p[...].astype(F32) for p in (own, one, two, three)))
    first = total[65:66] + total[66:67] + total[67:68]
    second = total[68:69] + total[69:70] + total[70:71]
    return joined(total), first[:, :128], second[:, :128]


def unpack_kernel(own, one, two, three, scores_ref, norm_ref):
    scores, norm, _ = unpacked(own, one, two, three)
    scores_ref[...] = scores
    norm_ref[...] = stacked([norm], 8)


def hessian_kernel(
    events_ref, mine_ref, theirs_ref, rate_ref, own_ref, curv_ref, one_ref, two_ref, three_ref, q, held=None, sems=None
):
    x, _, core = place()
    outs = ((2, two_ref), (1, one_ref), (3, three_ref), (0, own_ref))
    starts = [lax.rem(x + k, XN) * QUARTER * 128 + part * 512 for k, _ in outs for part in range(2)]
    pieces = Columns(events_ref, held, sems, starts)
    curv = jnp.zeros((ROWS, 128), F32)
    for half in range(2):
        scores = jnp.where(core == half, mine_ref[...], theirs_ref[...])
        at = slice(half * HALF, (half + 1) * HALF)
        weighted = rate_ref[:, at] * scores
        curv = curv + tile_sums(weighted * scores)
        lead = weighted.astype(BF16)
        q[:ROWS, at] = lead
        q[ROWS:, at] = stacked([weighted[ROWS - 1 :] - lead[ROWS - 1 :].astype(F32)], 16).astype(BF16)
    triple = [v.astype(F32) for v in triple_of(line_sums(curv, jnp.zeros_like(curv)))]
    curv_ref[...] = stacked(triple, 8)
    for i, (k, out_ref) in enumerate(outs):
        rests = []
        for part in range(2):
            total = joined(jnp.dot(q[...], pieces.take(2 * i + part), preferred_element_type=F32))
            for u in range(4):
                t = part * 4 + u
                values = total[:, u * 128 : (u + 1) * 128]
                out_ref[t * ROWS : (t + 1) * ROWS, :] = values.astype(out_ref.dtype)
                rests.append(values[ROWS - 1 :] - values[ROWS - 1 :].astype(BF16).astype(F32))
        if k:
            out_ref[QUARTER * ROWS :, :] = stacked(rests + triple, 16).astype(BF16)


def cut_kernel(own, curv_ref, one, two, three, out_ref):
    top = QUARTER * ROWS
    tails = [p[top:, :].astype(F32) for p in (one, two, three)]
    curvs = [curv_ref[0:1] + curv_ref[1:2] + curv_ref[2:3]]
    curvs += [v[QUARTER : QUARTER + 1] + v[QUARTER + 1 : QUARTER + 2] + v[QUARTER + 2 : QUARTER + 3] for v in tails]
    curv = triple_of(four(*curvs))
    for t in range(QUARTER):
        at = slice(t * ROWS, (t + 1) * ROWS)
        total = four(own[at, :], one[at, :].astype(F32), two[at, :].astype(F32), three[at, :].astype(F32))
        rest = tails[0][t : t + 1] + tails[1][t : t + 1] + tails[2][t : t + 1]
        total = total + jnp.where(row_is(total.shape, ROWS - 1), rest, 0.0)
        lead = total.astype(BF16)
        rest = total[ROWS - 1 :] - lead[ROWS - 1 :].astype(F32)
        out_ref[t, :ROWS, :] = lead
        out_ref[t, ROWS:, :] = stacked([rest, *curv], 8).astype(BF16)


def residual_kernel(in_ref, norm_ref, rhs_ref, grad_ref, out_ref, scalars_ref):
    x, z, _ = place()
    tile = x * QUARTER + z
    total = in_ref[0].astype(F32)
    for z in range(1, ZN):
        total = total + in_ref[z].astype(F32)
    curv = total[65:66] + total[66:67] + total[67:68]
    norm = norm_ref[:1]
    step = norm / (curv + LAMBDA * norm)
    square = (ROWS, 128)
    eye = lax.broadcasted_iota(jnp.int32, square, 0) == lax.broadcasted_iota(jnp.int32, square, 1)
    column = jnp.sum(jnp.where(eye, step, 0.0), axis=1, keepdims=True)
    right = rhs_ref[:, pl.ds(pl.multiple_of(tile * 128, 128), 128)].astype(F32)
    right = jnp.where(row_is(square, ROWS - 1), grad_ref[pl.ds(tile, 1), :], right)
    residual = right - column * (joined(total) + LAMBDA * right)
    lead = residual.astype(BF16)
    rest = stacked([residual[ROWS - 1 :] - lead[ROWS - 1 :].astype(F32)], 8).astype(BF16)
    for z in range(ZN):
        out_ref[z, :ROWS, :] = lead
        out_ref[z, ROWS:, :] = rest
    scalars_ref[...] = stacked([step, curv, norm], 8)


def second_kernel(
    events_ref, rhs_ref, grad_ref, own, one, two, three, other_ref, mine_ref, first_ref, res, held=None, sems=None
):
    x, _, core = place()
    pieces = half_stream(events_ref, held, sems, core)
    norm = jnp.zeros((ROWS, 128), F32)
    cross = jnp.zeros((ROWS, 128), F32)
    for k, part in enumerate((own, one, two, three)):
        quarter = lax.rem(x + XN - k, XN)
        for t in range(QUARTER):
            tile = quarter * QUARTER + t
            at = pl.ds(pl.multiple_of(tile * 128, 128), 128)
            rows = part[t]
            values = joined(rows.astype(F32))
            right = rhs_ref[:, at].astype(F32)
            right = jnp.where(row_is(right.shape, ROWS - 1), grad_ref[pl.ds(tile, 1), :], right)
            norm = norm + values * values
            cross = cross + values * right
            first_ref[pl.ds(tile, 1), :] = values[ROWS - 1 :]
            exact = rows.astype(F32)
            res[at, :] = turned(exact[:ROWS], exact[ROWS : ROWS + 1])
    line = line_sums(norm, cross)
    lines = stacked([line, pltpu.roll(line, ROWS, 1)], 8)
    put_scores(pieces, res, other_ref, mine_ref, lines)


def tail_kernel(own, one, two, three, scores_ref, rate_ref, tail_ref, lines_ref):
    scores, norm, cross = unpacked(own, one, two, three)
    rate = jnp.where(place()[2] == 0, rate_ref[:, :HALF], rate_ref[:, HALF:])
    weighted = rate * scores
    tail_ref[...] = line_sums(tile_sums(weighted * scores_ref[...]), tile_sums(weighted * scores))
    lines_ref[...] = stacked([norm, cross], 8)


def end_kernel(tails_ref, scalars_ref, lines_ref, w_ref, grad_ref, first_ref, weights_ref, widths_ref):
    tail = tails_ref[0]
    for e in range(1, EN):
        tail = tail + tails_ref[e]
    mixed, square = tail, pltpu.roll(tail, ROWS, 1)
    step_one, curv, norm = scalars_ref[0:1], scalars_ref[1:2], scalars_ref[2:3]
    norm_next, cross = lines_ref[0:1], lines_ref[1:2]
    ratio = norm_next / norm
    curvature = square + 2.0 * ratio * mixed + ratio * ratio * curv
    curvature = curvature + LAMBDA * (norm_next + 2.0 * ratio * cross + ratio * ratio * norm)
    step_two = norm_next / curvature
    widths = step_one * norm + step_two * (cross + ratio * norm)
    widths_ref[...] = widths[:, : ROWS - 1]
    at = slice(ROWS - 1, ROWS)
    grad = grad_ref[...]
    step = step_one[:, at] * grad + step_two[:, at] * (first_ref[...] + ratio[:, at] * grad)
    weights_ref[...] = w_ref[...] - step


def on_device(events, labels, weights, contexts):
    features = TILES * 128
    tiled = weights.reshape(TILES, 128)

    rows = [pltpu.VMEM((COUNT, features), BF16), pltpu.SemaphoreType.DMA((10,))]
    columns = [pltpu.VMEM((8, COUNT, 512), BF16), pltpu.SemaphoreType.DMA((8,))]

    margin, picked = kernel_call(
        first_kernel,
        [SMEM, HBM, HBM],
        [shaped(COUNT // 128, 128), shaped(TILES, ROWS, 128, dtype=BF16)],
        (contexts, weights.reshape(1, features), events),
        [pltpu.VMEM((1, features), F32), pltpu.VMEM((ROWS, features), F32), *rows, pltpu.SemaphoreType.DMA],
        micros=6,
        room=ROOM,
    )
    chunks = lax.all_to_all(picked, "event", 0, 0)

    margin = margin + core_move(margin)
    rate, grad = kernel_call(
        gradient_kernel,
        [HBM] + [VMEM] * 5,
        [shaped(1, COUNT), shaped(TILES, 128)],
        (events, margin, *y_moves(margin), labels.reshape(COUNT // 128, 128)),
        [pltpu.VMEM((16, COUNT), BF16), *columns],
        micros=4,
        room=ROOM,
    )
    (message,) = kernel_call(
        spread_kernel, [VMEM] * 2, [shaped(ZN, ROWS + 2 * TILES, 128, dtype=BF16)], (chunks, grad)
    )
    message = z_exchange(message)
    (message,) = kernel_call(
        collect_kernel, [VMEM], [shaped(QUARTER * ROWS + 2 * TILES, 128, dtype=BF16)], (message,)
    )

    half = [shaped(ROWS + 8, HALF), shaped(ROWS + 8, HALF)]
    rhs, grad, other, mine = kernel_call(
        scores_kernel,
        [HBM] + [VMEM] * 5,
        [shaped(ROWS, features, dtype=BF16), shaped(TILES, 128)] + half,
        (events, tiled, message, *x_moves(message)),
        [pltpu.VMEM((features, 128), BF16), *rows],
        micros=4,
        room=ROOM,
    )
    packed = [shaped(ROWS + 16, HALF, dtype=BF16)]
    (message,) = kernel_call(pack_kernel, [VMEM] * 2, packed, (mine, core_move(other)))
    scores, norm = kernel_call(
        unpack_kernel, [VMEM] * 4, [shaped(ROWS, HALF), shaped(8, 128)], (message, *y_moves(message))
    )

    part = shaped(QUARTER * ROWS + 16, 128, dtype=BF16)
    own, curv, one, two, three = kernel_call(
        hessian_kernel,
        [HBM] + [VMEM] * 3,
        [shaped(QUARTER * ROWS, 128), shaped(8, 128), part, part, part],
        (events, scores, core_move(scores), rate),
        [pltpu.VMEM((ROWS + 16, COUNT), BF16), *columns],
        micros=4,
        room=ROOM,
    )
    moved = [
        lax.ppermute(v, "event", [(i, (i + k * ZN) % EN) for i in range(EN)])
        for k, v in ((1, one), (2, two), (3, three))
    ]
    shard = [shaped(ZN, ROWS + 8, 128, dtype=BF16)]
    (message,) = kernel_call(cut_kernel, [VMEM] * 5, shard, (own, curv, *moved))
    message, scalars = kernel_call(
        residual_kernel,
        [VMEM] * 4,
        shard + [shaped(8, 128)],
        (z_exchange(message), norm, rhs, grad),
    )
    message = z_exchange(message)

    other, mine, first = kernel_call(
        second_kernel,
        [VMEM] + [VMEM] * 6,
        half + [shaped(TILES, 128)],
        (events, rhs, grad, message, *x_moves(message)),
        [pltpu.VMEM((features, 128), BF16)],
        micros=4,
        room=8,
    )
    (message,) = kernel_call(pack_kernel, [VMEM] * 2, packed, (mine, core_move(other)))
    tail, lines = kernel_call(
        tail_kernel,
        [VMEM] * 6,
        [shaped(1, 128), shaped(8, 128)],
        (message, *y_moves(message), scores, rate),
    )
    tail = tail + core_move(tail)
    tails = lax.all_to_all(jnp.broadcast_to(tail[None], (EN, 1, 128)), "event", 0, 0)
    updated, widths = kernel_call(
        end_kernel, [VMEM] * 6, [shaped(TILES, 128), shaped(1, ROWS - 1)], (tails, scalars, lines, tiled, grad, first)
    )
    return updated.reshape(features), widths.reshape(ROWS - 1)


def solution(mesh):
    in_specs = (P("event", "feat"), P("event"), P("feat"), P())
    out_specs = (P("feat"), P())
    return jax.shard_map(on_device, mesh=mesh, in_specs=in_specs, out_specs=out_specs, check_vma=False)
```

```python
import jax
import jax.numpy as jnp
from jax import lax
from jax.experimental import pallas as pl
from jax.experimental.pallas import tpu as pltpu
from jax.sharding import PartitionSpec as P

LAMBDA = 0.5
XN, ZN, YN, CN = 4, 8, 4, 2
EN = XN * ZN
ROWS = 64
TILES = 32
QUARTER = TILES // XN
COUNT = 1280
HALF = COUNT // 2
WINDOW = 4
ROOM = 48
F32, BF16 = jnp.float32, jnp.bfloat16
VMEM = pl.BlockSpec(memory_space=pltpu.VMEM)
SMEM = pl.BlockSpec(memory_space=pltpu.SMEM)
HBM = pl.BlockSpec(memory_space=pltpu.HBM)
ACROSS = (((1,), (1,)), ((), ()))


def shaped(*shape, dtype=F32):
    return jax.ShapeDtypeStruct(shape, dtype)


def kernel_call(body, ins, outs, args, scratch=(), micros=0.5, room=8):
    return pl.pallas_call(
        body,
        out_shape=outs,
        in_specs=ins,
        out_specs=[VMEM] * len(outs),
        scratch_shapes=list(scratch),
        compiler_params=pltpu.CompilerParams(vmem_limit_bytes=room << 20),
        cost_estimate=pl.CostEstimate(flops=0, bytes_accessed=int(micros * 3.6e6), transcendentals=0),
    )(*args)


def x_moves(v):
    n = XN * ZN
    return [lax.ppermute(v, "event", [(i, (i + k * ZN) % n) for i in range(n)]) for k in (1, 2, 3)]


def y_moves(v):
    n = YN * CN
    return [lax.ppermute(v, "feat", [(i, (i + k * CN) % n) for i in range(n)]) for k in (1, 2, 3)]


def core_move(v):
    return lax.ppermute(v, "feat", [(i, i ^ 1) for i in range(YN * CN)])


def z_exchange(v):
    groups = [[x * ZN + z for z in range(ZN)] for x in range(XN)]
    return lax.all_to_all(v, "event", 0, 0, axis_index_groups=groups)


def four(own, one, two, three):
    return (own + two) + (one + three)


def pair_of(v):
    lead = v.astype(BF16)
    return lead, (v - lead.astype(F32)).astype(BF16)


def triple_of(v):
    lead, rest = v.astype(BF16), v
    rest = v - lead.astype(F32)
    mid = rest.astype(BF16)
    return lead, mid, (rest - mid.astype(F32)).astype(BF16)


def row_is(shape, i):
    return lax.broadcasted_iota(jnp.int32, shape, 0) == i


def stacked(lines, rows):
    out = jnp.zeros((rows, lines[0].shape[1]), F32)
    for i, line in enumerate(lines):
        out = jnp.where(row_is(out.shape, i), line.astype(F32), out)
    return out


def joined(v):
    top = v[:ROWS]
    return top + jnp.where(row_is(top.shape, ROWS - 1), v[ROWS : ROWS + 1], 0.0)


def line_sums(top, bottom):
    return jnp.sum(jnp.transpose(jnp.concatenate([top, bottom], axis=0)), axis=0, keepdims=True)


def tile_sums(v):
    total = v[:, :128]
    for t in range(1, v.shape[1] // 128):
        total = total + v[:, t * 128 : (t + 1) * 128]
    return total


class Stream:
    def __init__(self, pieces, sems):
        self.copies = [pltpu.make_async_copy(source, target, sems.at[i]) for i, (source, target) in enumerate(pieces)]
        for copy in self.copies[:WINDOW]:
            copy.start()

    def take(self, i):
        self.copies[i].wait()
        if i + WINDOW < len(self.copies):
            self.copies[i + WINDOW].start()


class Rows:
    def __init__(self, events_ref, held, sems, starts):
        self.events, self.held = events_ref, held
        self.starts = [pl.multiple_of(start, 128) for start in starts]
        if held is not None:
            pieces = [
                (events_ref.at[pl.ds(start, 128), :], held.at[pl.ds(i * 128, 128), :])
                for i, start in enumerate(self.starts)
            ]
            self.stream = Stream(pieces, sems)

    def take(self, first, count):
        if self.held is None:
            return self.events[pl.ds(self.starts[first], count * 128), :]
        for i in range(count):
            self.stream.take(first + i)
        return self.held[first * 128 : (first + count) * 128, :]


def place():
    event = lax.axis_index("event")
    return lax.div(event, ZN), lax.rem(event, ZN), lax.rem(lax.axis_index("feat"), CN)


def pick_kernel(contexts_ref, events_ref, out_ref, blocks, rows, sems):
    base = lax.axis_index("event") * COUNT

    def owned(j):
        return jnp.logical_and(contexts_ref[j] >= base, contexts_ref[j] < base + COUNT)

    def fetch(j):
        start = pl.multiple_of(lax.div(contexts_ref[j] - base, 16) * 16, 16)
        return pltpu.make_async_copy(events_ref.at[pl.ds(start, 16), :], blocks.at[j], sems.at[j])

    @pl.loop(0, ROWS - 1, unroll=9)
    def _(j):
        @pl.when(owned(j))
        def _():
            fetch(j).start()

    rows[...] = jnp.zeros_like(rows)

    @pl.loop(0, ROWS - 1, unroll=9)
    def _(j):
        @pl.when(owned(j))
        def _():
            fetch(j).wait()
            block = blocks[j].astype(F32)
            found = jnp.where(row_is(block.shape, lax.rem(contexts_ref[j] - base, 16)), block, 0.0)
            rows[pl.ds(j, 1), :] = jnp.sum(found, axis=0, keepdims=True)

    for t in range(TILES):
        out_ref[t] = rows[:, t * 128 : (t + 1) * 128].astype(BF16)


def margin_kernel(w_ref, events_ref, _after, margin_ref, held, w, sems):
    pieces = Rows(events_ref, held, sems, [i * 128 for i in range(COUNT // 128)])
    w[...] = w_ref[...].astype(BF16).astype(F32)
    for c in range(COUNT // 128):
        pieces.take(c, 1)
        sums = []
        for r in range(c * 128, (c + 1) * 128, 16):
            total = jnp.zeros((16, 128), F32)
            for t in range(TILES):
                at = slice(t * 128, (t + 1) * 128)
                total = total + held[r : r + 16, at].astype(F32) * w[:, at]
            sums.append(total)
        turned = jnp.transpose(jnp.concatenate(sums, axis=0))
        margin_ref[c : c + 1, :] = jnp.sum(turned, axis=0, keepdims=True)


def gradient_kernel(events_ref, own, one, two, three, labels_ref, rate_ref, grad_ref, errs):
    margin = four(own[...], one[...], two[...], three[...])
    chance = jax.nn.sigmoid(margin)
    rate = chance * (1.0 - chance)
    errors = chance - labels_ref[...].astype(F32)
    lead, rest = pair_of(errors)
    lead, rest = lead.astype(F32), rest.astype(F32)
    for i in range(COUNT // 128):
        at = slice(i * 128, (i + 1) * 128)
        rate_ref[:, at] = rate[i : i + 1]
        errs[:, at] = stacked([lead[i : i + 1], rest[i : i + 1]], 16).astype(BF16)
    for c in range(8):
        part = jnp.dot(errs[...], events_ref[:, c * 512 : (c + 1) * 512], preferred_element_type=F32)
        line = part[:1] + part[1:2]
        for u in range(4):
            grad_ref[c * 4 + u : c * 4 + u + 1, :] = line[:, u * 128 : (u + 1) * 128]


def spread_kernel(chunks_ref, grad_ref, out_ref):
    total = chunks_ref[0].astype(F32)
    for e in range(1, EN):
        total = total + chunks_ref[e].astype(F32)
    lead, rest = pair_of(grad_ref[...])
    for z in range(ZN):
        out_ref[z, :ROWS, :] = total.astype(BF16)
        out_ref[z, ROWS : ROWS + TILES, :] = lead
        out_ref[z, ROWS + TILES :, :] = rest


def collect_kernel(in_ref, out_ref):
    grad = jnp.zeros((TILES, 128), F32)
    for z in range(ZN):
        out_ref[z * ROWS : (z + 1) * ROWS, :] = in_ref[z, :ROWS, :]
        grad = grad + (in_ref[z, ROWS : ROWS + TILES, :].astype(F32) + in_ref[z, ROWS + TILES :, :].astype(F32))
    lead, rest = pair_of(grad)
    out_ref[QUARTER * ROWS : QUARTER * ROWS + TILES, :] = lead
    out_ref[QUARTER * ROWS + TILES :, :] = rest


def half_stream(events_ref, held, sems, core):
    starts = [half * HALF + i * 128 for half in (1 - core, core) for i in range(HALF // 128)]
    return Rows(events_ref, held, sems, starts)


def put_scores(pieces, rhs, other_ref, own_ref, lines):
    for first, out_ref in ((0, other_ref), (HALF // 128, own_ref)):
        for at, size in ((0, 2), (2, 3)):
            part = jnp.dot(pieces.take(first + at, size), rhs[...], preferred_element_type=F32)
            for t in range(size):
                columns = slice((at + t) * 128, (at + t + 1) * 128)
                out_ref[:ROWS, columns] = joined(jnp.transpose(part[t * 128 : (t + 1) * 128]))
                out_ref[ROWS:, columns] = lines if at + t == 0 else jnp.zeros_like(lines)


def turned(top, rest):
    below = jnp.where(row_is(top.shape, 0), rest.astype(F32), 0.0)
    return jnp.transpose(jnp.concatenate([top, below], axis=0)).astype(BF16)


def scores_kernel(
    events_ref, w_ref, own, one, two, three, rhs_ref, grad_ref, other_ref, mine_ref, held, rhs, sems
):
    x, _, core = place()
    pieces = half_stream(events_ref, held, sems, core)
    tail = QUARTER * ROWS
    grads = [p[tail : tail + TILES, :].astype(F32) + p[tail + TILES :, :].astype(F32) for p in (own, one, two, three)]
    grad_ref[...] = four(*grads) + LAMBDA * w_ref[...]
    norm = jnp.zeros((ROWS, 128), F32)
    for k, part in enumerate((own, one, two, three)):
        quarter = lax.rem(x + XN - k, XN)
        for t in range(QUARTER):
            tile = quarter * QUARTER + t
            grad = grad_ref[pl.ds(tile, 1), :]
            lead, rest = pair_of(grad)
            values = part[t * ROWS : (t + 1) * ROWS, :].astype(F32)
            last = row_is(values.shape, ROWS - 1)
            exact = jnp.where(last, grad, values)
            norm = norm + exact * exact
            at = pl.ds(pl.multiple_of(tile * 128, 128), 128)
            top = jnp.where(last, lead.astype(F32), values)
            rhs_ref[:, at] = top.astype(BF16)
            rhs[at, :] = turned(top, rest)
    line = line_sums(norm, jnp.zeros_like(norm))
    put_scores(pieces, rhs, other_ref, mine_ref, stacked([line], 8))


def pack_kernel(own, other, out_ref):
    total = own[...] + other[...]
    scores, lines = total[:ROWS], total[ROWS:]
    lead = scores.astype(BF16)
    rest = scores[ROWS - 1 :] - lead[ROWS - 1 :].astype(F32)
    out_ref[:ROWS, :] = lead
    out_ref[ROWS:, :] = stacked([rest, *triple_of(lines[:1]), *triple_of(lines[1:2])], 8).astype(BF16)


def unpacked(own, one, two, three):
    total = four(*(p[...].astype(F32) for p in (own, one, two, three)))
    first = total[65:66] + total[66:67] + total[67:68]
    second = total[68:69] + total[69:70] + total[70:71]
    return joined(total), first[:, :128], second[:, :128]


def unpack_kernel(own, one, two, three, scores_ref, norm_ref):
    scores, norm, _ = unpacked(own, one, two, three)
    scores_ref[...] = scores
    norm_ref[...] = stacked([norm], 8)


def hessian_kernel(
    events_ref, mine_ref, theirs_ref, rate_ref, own_ref, curv_ref, one_ref, two_ref, three_ref, q
):
    x, _, core = place()
    outs = ((2, two_ref), (1, one_ref), (3, three_ref), (0, own_ref))
    curv = jnp.zeros((ROWS, 128), F32)
    first, second = rate_ref[:, :HALF], rate_ref[:, HALF:]
    mine = core == 0
    halves = ((theirs_ref, jnp.where(mine, second, first)), (mine_ref, jnp.where(mine, first, second)))
    for half, (scores_ref, rate) in enumerate(halves):
        scores = scores_ref[...]
        at = slice(half * HALF, (half + 1) * HALF)
        weighted = rate * scores
        curv = curv + tile_sums(weighted * scores)
        lead = weighted.astype(BF16)
        q[:ROWS, at] = lead
        q[ROWS:, at] = stacked([weighted[ROWS - 1 :] - lead[ROWS - 1 :].astype(F32)], 16).astype(BF16)
    triple = [v.astype(F32) for v in triple_of(line_sums(curv, jnp.zeros_like(curv)))]
    curv_ref[...] = stacked(triple, 8)
    for k, out_ref in outs:
        rests = []
        for part in range(2):
            start = pl.multiple_of(lax.rem(x + k, XN) * QUARTER * 128 + part * 512, 512)
            total = joined(jnp.dot(q[...], events_ref[:, pl.ds(start, 512)], preferred_element_type=F32))
            for u in range(4):
                t = part * 4 + u
                values = total[:, u * 128 : (u + 1) * 128]
                out_ref[t * ROWS : (t + 1) * ROWS, :] = values.astype(out_ref.dtype)
                rests.append(values[ROWS - 1 :] - values[ROWS - 1 :].astype(BF16).astype(F32))
        if k:
            out_ref[QUARTER * ROWS :, :] = stacked(rests + triple, 16).astype(BF16)


def cut_kernel(own, curv_ref, one, two, three, out_ref):
    top = QUARTER * ROWS
    tails = [p[top:, :].astype(F32) for p in (one, two, three)]
    curvs = [curv_ref[0:1] + curv_ref[1:2] + curv_ref[2:3]]
    curvs += [v[QUARTER : QUARTER + 1] + v[QUARTER + 1 : QUARTER + 2] + v[QUARTER + 2 : QUARTER + 3] for v in tails]
    curv = triple_of(four(*curvs))
    for t in range(QUARTER):
        at = slice(t * ROWS, (t + 1) * ROWS)
        total = four(own[at, :], one[at, :].astype(F32), two[at, :].astype(F32), three[at, :].astype(F32))
        rest = tails[0][t : t + 1] + tails[1][t : t + 1] + tails[2][t : t + 1]
        total = total + jnp.where(row_is(total.shape, ROWS - 1), rest, 0.0)
        lead = total.astype(BF16)
        rest = total[ROWS - 1 :] - lead[ROWS - 1 :].astype(F32)
        out_ref[t, :ROWS, :] = lead
        out_ref[t, ROWS:, :] = stacked([rest, *curv], 8).astype(BF16)


def residual_kernel(in_ref, norm_ref, rhs_ref, grad_ref, out_ref, scalars_ref):
    x, z, _ = place()
    tile = x * QUARTER + z
    total = in_ref[0].astype(F32)
    for z in range(1, ZN):
        total = total + in_ref[z].astype(F32)
    curv = total[65:66] + total[66:67] + total[67:68]
    norm = norm_ref[:1]
    step = norm / (curv + LAMBDA * norm)
    square = (ROWS, 128)
    eye = lax.broadcasted_iota(jnp.int32, square, 0) == lax.broadcasted_iota(jnp.int32, square, 1)
    column = jnp.sum(jnp.where(eye, step, 0.0), axis=1, keepdims=True)
    right = rhs_ref[:, pl.ds(pl.multiple_of(tile * 128, 128), 128)].astype(F32)
    right = jnp.where(row_is(square, ROWS - 1), grad_ref[pl.ds(tile, 1), :], right)
    residual = right - column * (joined(total) + LAMBDA * right)
    lead = residual.astype(BF16)
    rest = stacked([residual[ROWS - 1 :] - lead[ROWS - 1 :].astype(F32)], 8).astype(BF16)
    for z in range(ZN):
        out_ref[z, :ROWS, :] = lead
        out_ref[z, ROWS:, :] = rest
    scalars_ref[...] = stacked([step, curv, norm], 8)


def second_kernel(
    events_ref, rhs_ref, grad_ref, own, one, two, three, other_ref, mine_ref, first_ref, res
):
    x, _, _ = place()
    pieces = Rows(events_ref, None, None, [i * 128 for i in range(COUNT // 128)])
    norm = jnp.zeros((ROWS, 128), F32)
    cross = jnp.zeros((ROWS, 128), F32)
    for k, part in enumerate((own, one, two, three)):
        quarter = lax.rem(x + XN - k, XN)
        for t in range(QUARTER):
            tile = quarter * QUARTER + t
            at = pl.ds(pl.multiple_of(tile * 128, 128), 128)
            rows = part[t]
            values = joined(rows.astype(F32))
            right = rhs_ref[:, at].astype(F32)
            right = jnp.where(row_is(right.shape, ROWS - 1), grad_ref[pl.ds(tile, 1), :], right)
            norm = norm + values * values
            cross = cross + values * right
            first_ref[pl.ds(tile, 1), :] = values[ROWS - 1 :]
            exact = rows.astype(F32)
            res[at, :] = turned(exact[:ROWS], exact[ROWS : ROWS + 1])
    line = line_sums(norm, cross)
    lines = stacked([line, pltpu.roll(line, ROWS, 1)], 8)
    put_scores(pieces, res, other_ref, mine_ref, lines)


def tail_kernel(own, one, two, three, scores_ref, rate_ref, tail_ref, lines_ref):
    scores, norm, cross = unpacked(own, one, two, three)
    rate = jnp.where(place()[2] == 0, rate_ref[:, :HALF], rate_ref[:, HALF:])
    weighted = rate * scores
    tail_ref[...] = line_sums(tile_sums(weighted * scores_ref[...]), tile_sums(weighted * scores))
    lines_ref[...] = stacked([norm, cross], 8)


def end_kernel(tails_ref, scalars_ref, lines_ref, w_ref, grad_ref, first_ref, weights_ref, widths_ref):
    tail = tails_ref[0]
    for e in range(1, EN):
        tail = tail + tails_ref[e]
    mixed, square = tail, pltpu.roll(tail, ROWS, 1)
    step_one, curv, norm = scalars_ref[0:1], scalars_ref[1:2], scalars_ref[2:3]
    norm_next, cross = lines_ref[0:1], lines_ref[1:2]
    ratio = norm_next / norm
    curvature = square + 2.0 * ratio * mixed + ratio * ratio * curv
    curvature = curvature + LAMBDA * (norm_next + 2.0 * ratio * cross + ratio * ratio * norm)
    step_two = norm_next / curvature
    widths = step_one * norm + step_two * (cross + ratio * norm)
    widths_ref[...] = widths[:, : ROWS - 1]
    at = slice(ROWS - 1, ROWS)
    grad = grad_ref[...]
    step = step_one[:, at] * grad + step_two[:, at] * (first_ref[...] + ratio[:, at] * grad)
    weights_ref[...] = w_ref[...] - step


def on_device(events, labels, weights, contexts):
    features = TILES * 128
    tiled = weights.reshape(TILES, 128)

    whole = shaped(COUNT, features, dtype=BF16)
    sems = pltpu.SemaphoreType.DMA((10,))

    (picked,) = kernel_call(
        pick_kernel,
        [SMEM, HBM],
        [shaped(TILES, ROWS, 128, dtype=BF16)],
        (contexts, events),
        [
            pltpu.VMEM((ROWS - 1, 16, features), BF16),
            pltpu.VMEM((ROWS, features), F32),
            pltpu.SemaphoreType.DMA((ROWS - 1,)),
        ],
        micros=2,
        room=ROOM,
    )
    chunks = lax.all_to_all(picked, "event", 0, 0)
    margin, held = kernel_call(
        margin_kernel,
        [VMEM, HBM, HBM],
        [shaped(COUNT // 128, 128), whole],
        (weights.reshape(1, features), events, picked),
        [pltpu.VMEM((1, features), F32), sems],
        micros=4,
        room=40,
    )

    margin = margin + core_move(margin)
    rate, grad = kernel_call(
        gradient_kernel,
        [VMEM] * 6,
        [shaped(1, COUNT), shaped(TILES, 128)],
        (held, margin, *y_moves(margin), labels.reshape(COUNT // 128, 128)),
        [pltpu.VMEM((16, COUNT), BF16)],
        micros=4,
        room=8,
    )
    (message,) = kernel_call(
        spread_kernel, [VMEM] * 2, [shaped(ZN, ROWS + 2 * TILES, 128, dtype=BF16)], (chunks, grad)
    )
    message = z_exchange(message)
    (message,) = kernel_call(
        collect_kernel, [VMEM], [shaped(QUARTER * ROWS + 2 * TILES, 128, dtype=BF16)], (message,)
    )

    half = [shaped(ROWS + 8, HALF), shaped(ROWS + 8, HALF)]
    rhs, grad, other, mine, held = kernel_call(
        scores_kernel,
        [HBM] + [VMEM] * 5,
        [shaped(ROWS, features, dtype=BF16), shaped(TILES, 128)] + half + [whole],
        (events, tiled, message, *x_moves(message)),
        [pltpu.VMEM((features, 128), BF16), sems],
        micros=4,
        room=40,
    )
    packed = [shaped(ROWS + 8, HALF, dtype=BF16)]
    (message,) = kernel_call(pack_kernel, [VMEM] * 2, packed, (mine, core_move(other)))
    scores, norm = kernel_call(
        unpack_kernel, [VMEM] * 4, [shaped(ROWS, HALF), shaped(8, 128)], (message, *y_moves(message))
    )

    part = shaped(QUARTER * ROWS + 16, 128, dtype=BF16)
    own, curv, one, two, three = kernel_call(
        hessian_kernel,
        [VMEM] * 4,
        [shaped(QUARTER * ROWS, 128), shaped(8, 128), part, part, part],
        (held, scores, core_move(scores), rate),
        [pltpu.VMEM((ROWS + 16, COUNT), BF16)],
        micros=4,
        room=8,
    )
    moved = [
        lax.ppermute(v, "event", [(i, (i + k * ZN) % EN) for i in range(EN)])
        for k, v in ((1, one), (2, two), (3, three))
    ]
    shard = [shaped(ZN, ROWS + 8, 128, dtype=BF16)]
    (message,) = kernel_call(cut_kernel, [VMEM] * 5, shard, (own, curv, *moved))
    message, scalars = kernel_call(
        residual_kernel,
        [VMEM] * 4,
        shard + [shaped(8, 128)],
        (z_exchange(message), norm, rhs, grad),
    )
    message = z_exchange(message)

    other, mine, first = kernel_call(
        second_kernel,
        [VMEM] * 7,
        half + [shaped(TILES, 128)],
        (held, rhs, grad, message, *x_moves(message)),
        [pltpu.VMEM((features, 128), BF16)],
        micros=4,
        room=8,
    )
    (message,) = kernel_call(pack_kernel, [VMEM] * 2, packed, (mine, core_move(other)))
    tail, lines = kernel_call(
        tail_kernel,
        [VMEM] * 6,
        [shaped(1, 128), shaped(8, 128)],
        (message, *y_moves(message), scores, rate),
    )
    tail = tail + core_move(tail)
    tails = lax.all_to_all(jnp.broadcast_to(tail[None], (EN, 1, 128)), "event", 0, 0)
    updated, widths = kernel_call(
        end_kernel, [VMEM] * 6, [shaped(TILES, 128), shaped(1, ROWS - 1)], (tails, scalars, lines, tiled, grad, first)
    )
    return updated.reshape(features), widths.reshape(ROWS - 1)


def solution(mesh):
    in_specs = (P("event", "feat"), P("event"), P("feat"), P())
    out_specs = (P("feat"), P())
    return jax.shard_map(on_device, mesh=mesh, in_specs=in_specs, out_specs=out_specs, check_vma=False)
```

```python
import jax
import jax.numpy as jnp
from jax import lax
from jax.experimental import pallas as pl
from jax.experimental.pallas import tpu as pltpu
from jax.sharding import PartitionSpec as P

LAMBDA = 0.5
XN, ZN, YN, CN = 4, 8, 4, 2
EN = XN * ZN
ROWS = 64
TILES = 32
QUARTER = TILES // XN
COUNT = 1280
HALF = COUNT // 2
WINDOW = 10
ROOM = 48
F32, BF16 = jnp.float32, jnp.bfloat16
VMEM = pl.BlockSpec(memory_space=pltpu.VMEM)
SMEM = pl.BlockSpec(memory_space=pltpu.SMEM)
HBM = pl.BlockSpec(memory_space=pltpu.HBM)
ACROSS = (((1,), (1,)), ((), ()))


def shaped(*shape, dtype=F32):
    return jax.ShapeDtypeStruct(shape, dtype)


def kernel_call(body, ins, outs, args, scratch=(), micros=0.5, room=8):
    return pl.pallas_call(
        body,
        out_shape=outs,
        in_specs=ins,
        out_specs=[VMEM] * len(outs),
        scratch_shapes=list(scratch),
        compiler_params=pltpu.CompilerParams(vmem_limit_bytes=room << 20),
        cost_estimate=pl.CostEstimate(flops=0, bytes_accessed=int(micros * 3.6e6), transcendentals=0),
    )(*args)


def x_moves(v):
    n = XN * ZN
    return [lax.ppermute(v, "event", [(i, (i + k * ZN) % n) for i in range(n)]) for k in (1, 2, 3)]


def y_moves(v):
    n = YN * CN
    return [lax.ppermute(v, "feat", [(i, (i + k * CN) % n) for i in range(n)]) for k in (1, 2, 3)]


def core_move(v):
    return lax.ppermute(v, "feat", [(i, i ^ 1) for i in range(YN * CN)])


def z_exchange(v):
    groups = [[x * ZN + z for z in range(ZN)] for x in range(XN)]
    return lax.all_to_all(v, "event", 0, 0, axis_index_groups=groups)


def four(own, one, two, three):
    return (own + two) + (one + three)


def pair_of(v):
    lead = v.astype(BF16)
    return lead, (v - lead.astype(F32)).astype(BF16)


def triple_of(v):
    lead, rest = v.astype(BF16), v
    rest = v - lead.astype(F32)
    mid = rest.astype(BF16)
    return lead, mid, (rest - mid.astype(F32)).astype(BF16)


def row_is(shape, i):
    return lax.broadcasted_iota(jnp.int32, shape, 0) == i


def stacked(lines, rows):
    out = jnp.zeros((rows, lines[0].shape[1]), F32)
    for i, line in enumerate(lines):
        out = jnp.where(row_is(out.shape, i), line.astype(F32), out)
    return out


def joined(v):
    top = v[:ROWS]
    return top + jnp.where(row_is(top.shape, ROWS - 1), v[ROWS : ROWS + 1], 0.0)


def line_sums(top, bottom):
    return jnp.sum(jnp.transpose(jnp.concatenate([top, bottom], axis=0)), axis=0, keepdims=True)


def tile_sums(v):
    total = v[:, :128]
    for t in range(1, v.shape[1] // 128):
        total = total + v[:, t * 128 : (t + 1) * 128]
    return total


class Stream:
    def __init__(self, pieces, sems):
        self.copies = [pltpu.make_async_copy(source, target, sems.at[i]) for i, (source, target) in enumerate(pieces)]
        for copy in self.copies[:WINDOW]:
            copy.start()

    def take(self, i):
        self.copies[i].wait()
        if i + WINDOW < len(self.copies):
            self.copies[i + WINDOW].start()


class Rows:
    def __init__(self, events_ref, held, sems, starts):
        self.events, self.held = events_ref, held
        self.starts = [pl.multiple_of(start, 128) for start in starts]
        if held is not None:
            pieces = [
                (events_ref.at[pl.ds(start, 128), :], held.at[pl.ds(i * 128, 128), :])
                for i, start in enumerate(self.starts)
            ]
            self.stream = Stream(pieces, sems)

    def take(self, first, count):
        if self.held is None:
            return self.events[pl.ds(self.starts[first], count * 128), :]
        for i in range(count):
            self.stream.take(first + i)
        return self.held[first * 128 : (first + count) * 128, :]


def place():
    event = lax.axis_index("event")
    return lax.div(event, ZN), lax.rem(event, ZN), lax.rem(lax.axis_index("feat"), CN)


def pick_kernel(contexts_ref, events_ref, out_ref, blocks, rows, sems):
    base = lax.axis_index("event") * COUNT

    def owned(j):
        return jnp.logical_and(contexts_ref[j] >= base, contexts_ref[j] < base + COUNT)

    def fetch(j):
        start = pl.multiple_of(lax.div(contexts_ref[j] - base, 16) * 16, 16)
        return pltpu.make_async_copy(events_ref.at[pl.ds(start, 16), :], blocks.at[j], sems.at[j])

    @pl.loop(0, ROWS - 1, unroll=9)
    def _(j):
        @pl.when(owned(j))
        def _():
            fetch(j).start()

    rows[...] = jnp.zeros_like(rows)

    @pl.loop(0, ROWS - 1, unroll=9)
    def _(j):
        @pl.when(owned(j))
        def _():
            fetch(j).wait()
            block = blocks[j].astype(F32)
            found = jnp.where(row_is(block.shape, lax.rem(contexts_ref[j] - base, 16)), block, 0.0)
            rows[pl.ds(j, 1), :] = jnp.sum(found, axis=0, keepdims=True)

    for t in range(TILES):
        out_ref[t] = rows[:, t * 128 : (t + 1) * 128].astype(BF16)


def margin_kernel(w_ref, events_ref, _after, margin_ref, held, w, sems):
    pieces = Rows(events_ref, held, sems, [i * 128 for i in range(COUNT // 128)])
    w[...] = w_ref[...].astype(BF16).astype(F32)
    for c in range(COUNT // 128):
        pieces.take(c, 1)
        sums = []
        for r in range(c * 128, (c + 1) * 128, 16):
            total = jnp.zeros((16, 128), F32)
            for t in range(TILES):
                at = slice(t * 128, (t + 1) * 128)
                total = total + held[r : r + 16, at].astype(F32) * w[:, at]
            sums.append(total)
        turned = jnp.transpose(jnp.concatenate(sums, axis=0))
        margin_ref[c : c + 1, :] = jnp.sum(turned, axis=0, keepdims=True)


def load_kernel(events_ref, _after, held, sems):
    pieces = Rows(events_ref, held, sems, [i * 128 for i in range(COUNT // 128)])
    for i in range(COUNT // 128):
        pieces.stream.take(i)


def gradient_kernel(events_ref, own, one, two, three, labels_ref, rate_ref, grad_ref, errs):
    margin = four(own[...], one[...], two[...], three[...])
    chance = jax.nn.sigmoid(margin)
    rate = chance * (1.0 - chance)
    errors = chance - labels_ref[...].astype(F32)
    lead, rest = pair_of(errors)
    lead, rest = lead.astype(F32), rest.astype(F32)
    for i in range(COUNT // 128):
        at = slice(i * 128, (i + 1) * 128)
        rate_ref[:, at] = rate[i : i + 1]
        errs[:, at] = stacked([lead[i : i + 1], rest[i : i + 1]], 16).astype(BF16)
    for c in range(8):
        part = jnp.dot(errs[...], events_ref[:, c * 512 : (c + 1) * 512], preferred_element_type=F32)
        line = part[:1] + part[1:2]
        for u in range(4):
            grad_ref[c * 4 + u : c * 4 + u + 1, :] = line[:, u * 128 : (u + 1) * 128]


def spread_kernel(chunks_ref, grad_ref, out_ref):
    total = chunks_ref[0].astype(F32)
    for e in range(1, EN):
        total = total + chunks_ref[e].astype(F32)
    lead, rest = pair_of(grad_ref[...])
    for z in range(ZN):
        out_ref[z, :ROWS, :] = total.astype(BF16)
        out_ref[z, ROWS : ROWS + TILES, :] = lead
        out_ref[z, ROWS + TILES :, :] = rest


def collect_kernel(in_ref, out_ref):
    grad = jnp.zeros((TILES, 128), F32)
    for z in range(ZN):
        out_ref[z * ROWS : (z + 1) * ROWS, :] = in_ref[z, :ROWS, :]
        grad = grad + (in_ref[z, ROWS : ROWS + TILES, :].astype(F32) + in_ref[z, ROWS + TILES :, :].astype(F32))
    lead, rest = pair_of(grad)
    out_ref[QUARTER * ROWS : QUARTER * ROWS + TILES, :] = lead
    out_ref[QUARTER * ROWS + TILES :, :] = rest


def halves(events_ref, core):
    starts = [half * HALF + i * 128 for half in (1 - core, core) for i in range(HALF // 128)]
    return Rows(events_ref, None, None, starts)


def put_scores(pieces, rhs, other_ref, own_ref, lines):
    for first, out_ref in ((0, other_ref), (HALF // 128, own_ref)):
        for at, size in ((0, 2), (2, 3)):
            part = jnp.dot(pieces.take(first + at, size), rhs[...], preferred_element_type=F32)
            for t in range(size):
                columns = slice((at + t) * 128, (at + t + 1) * 128)
                out_ref[:ROWS, columns] = joined(jnp.transpose(part[t * 128 : (t + 1) * 128]))
                out_ref[ROWS:, columns] = lines if at + t == 0 else jnp.zeros_like(lines)


def turned(top, rest):
    below = jnp.where(row_is(top.shape, 0), rest.astype(F32), 0.0)
    return jnp.transpose(jnp.concatenate([top, below], axis=0)).astype(BF16)


def scores_kernel(
    events_ref, w_ref, own, one, two, three, rhs_ref, grad_ref, other_ref, mine_ref, rhs
):
    x, _, core = place()
    pieces = halves(events_ref, core)
    tail = QUARTER * ROWS
    grads = [p[tail : tail + TILES, :].astype(F32) + p[tail + TILES :, :].astype(F32) for p in (own, one, two, three)]
    grad_ref[...] = four(*grads) + LAMBDA * w_ref[...]
    norm = jnp.zeros((ROWS, 128), F32)
    for k, part in enumerate((own, one, two, three)):
        quarter = lax.rem(x + XN - k, XN)
        for t in range(QUARTER):
            tile = quarter * QUARTER + t
            grad = grad_ref[pl.ds(tile, 1), :]
            lead, rest = pair_of(grad)
            values = part[t * ROWS : (t + 1) * ROWS, :].astype(F32)
            last = row_is(values.shape, ROWS - 1)
            exact = jnp.where(last, grad, values)
            norm = norm + exact * exact
            at = pl.ds(pl.multiple_of(tile * 128, 128), 128)
            top = jnp.where(last, lead.astype(F32), values)
            rhs_ref[:, at] = top.astype(BF16)
            rhs[at, :] = turned(top, rest)
    line = line_sums(norm, jnp.zeros_like(norm))
    put_scores(pieces, rhs, other_ref, mine_ref, stacked([line], 8))


def pack_kernel(own, other, out_ref):
    total = own[...] + other[...]
    scores, lines = total[:ROWS], total[ROWS:]
    lead = scores.astype(BF16)
    rest = scores[ROWS - 1 :] - lead[ROWS - 1 :].astype(F32)
    out_ref[:ROWS, :] = lead
    out_ref[ROWS:, :] = stacked([rest, *triple_of(lines[:1]), *triple_of(lines[1:2])], 8).astype(BF16)


def unpacked(own, one, two, three):
    total = four(*(p[...].astype(F32) for p in (own, one, two, three)))
    first = total[65:66] + total[66:67] + total[67:68]
    second = total[68:69] + total[69:70] + total[70:71]
    return joined(total), first[:, :128], second[:, :128]


def unpack_kernel(own, one, two, three, scores_ref, norm_ref):
    scores, norm, _ = unpacked(own, one, two, three)
    scores_ref[...] = scores
    norm_ref[...] = stacked([norm], 8)


def hessian_kernel(
    events_ref, mine_ref, theirs_ref, rate_ref, own_ref, curv_ref, one_ref, two_ref, three_ref, q
):
    x, _, core = place()
    outs = ((2, two_ref), (1, one_ref), (3, three_ref), (0, own_ref))
    curv = jnp.zeros((ROWS, 128), F32)
    for half in range(2):
        at = slice(half * HALF, (half + 1) * HALF)
        scores, rate = jnp.where(core == half, mine_ref[...], theirs_ref[...]), rate_ref[:, at]
        weighted = rate * scores
        curv = curv + tile_sums(weighted * scores)
        lead = weighted.astype(BF16)
        q[:ROWS, at] = lead
        q[ROWS:, at] = stacked([weighted[ROWS - 1 :] - lead[ROWS - 1 :].astype(F32)], 16).astype(BF16)
    triple = [v.astype(F32) for v in triple_of(line_sums(curv, jnp.zeros_like(curv)))]
    curv_ref[...] = stacked(triple, 8)
    for k, out_ref in outs:
        rests = []
        for part in range(2):
            start = pl.multiple_of(lax.rem(x + k, XN) * QUARTER * 128 + part * 512, 512)
            total = joined(jnp.dot(q[...], events_ref[:, pl.ds(start, 512)], preferred_element_type=F32))
            for u in range(4):
                t = part * 4 + u
                values = total[:, u * 128 : (u + 1) * 128]
                out_ref[t * ROWS : (t + 1) * ROWS, :] = values.astype(out_ref.dtype)
                rests.append(values[ROWS - 1 :] - values[ROWS - 1 :].astype(BF16).astype(F32))
        if k:
            out_ref[QUARTER * ROWS :, :] = stacked(rests + triple, 16).astype(BF16)


def cut_kernel(own, curv_ref, one, two, three, out_ref):
    top = QUARTER * ROWS
    tails = [p[top:, :].astype(F32) for p in (one, two, three)]
    curvs = [curv_ref[0:1] + curv_ref[1:2] + curv_ref[2:3]]
    curvs += [v[QUARTER : QUARTER + 1] + v[QUARTER + 1 : QUARTER + 2] + v[QUARTER + 2 : QUARTER + 3] for v in tails]
    curv = triple_of(four(*curvs))
    for t in range(QUARTER):
        at = slice(t * ROWS, (t + 1) * ROWS)
        total = four(own[at, :], one[at, :].astype(F32), two[at, :].astype(F32), three[at, :].astype(F32))
        rest = tails[0][t : t + 1] + tails[1][t : t + 1] + tails[2][t : t + 1]
        total = total + jnp.where(row_is(total.shape, ROWS - 1), rest, 0.0)
        lead = total.astype(BF16)
        rest = total[ROWS - 1 :] - lead[ROWS - 1 :].astype(F32)
        out_ref[t, :ROWS, :] = lead
        out_ref[t, ROWS:, :] = stacked([rest, *curv], 8).astype(BF16)


def residual_kernel(in_ref, norm_ref, rhs_ref, grad_ref, out_ref, scalars_ref):
    x, z, _ = place()
    tile = x * QUARTER + z
    total = in_ref[0].astype(F32)
    for z in range(1, ZN):
        total = total + in_ref[z].astype(F32)
    curv = total[65:66] + total[66:67] + total[67:68]
    norm = norm_ref[:1]
    step = norm / (curv + LAMBDA * norm)
    square = (ROWS, 128)
    eye = lax.broadcasted_iota(jnp.int32, square, 0) == lax.broadcasted_iota(jnp.int32, square, 1)
    column = jnp.sum(jnp.where(eye, step, 0.0), axis=1, keepdims=True)
    right = rhs_ref[:, pl.ds(pl.multiple_of(tile * 128, 128), 128)].astype(F32)
    right = jnp.where(row_is(square, ROWS - 1), grad_ref[pl.ds(tile, 1), :], right)
    residual = right - column * (joined(total) + LAMBDA * right)
    lead = residual.astype(BF16)
    rest = stacked([residual[ROWS - 1 :] - lead[ROWS - 1 :].astype(F32)], 8).astype(BF16)
    for z in range(ZN):
        out_ref[z, :ROWS, :] = lead
        out_ref[z, ROWS:, :] = rest
    scalars_ref[...] = stacked([step, curv, norm], 8)


def second_kernel(
    events_ref, rhs_ref, grad_ref, own, one, two, three, other_ref, mine_ref, first_ref, res
):
    x, _, core = place()
    pieces = halves(events_ref, core)
    norm = jnp.zeros((ROWS, 128), F32)
    cross = jnp.zeros((ROWS, 128), F32)
    for k, part in enumerate((own, one, two, three)):
        quarter = lax.rem(x + XN - k, XN)
        for t in range(QUARTER):
            tile = quarter * QUARTER + t
            at = pl.ds(pl.multiple_of(tile * 128, 128), 128)
            rows = part[t]
            values = joined(rows.astype(F32))
            right = rhs_ref[:, at].astype(F32)
            right = jnp.where(row_is(right.shape, ROWS - 1), grad_ref[pl.ds(tile, 1), :], right)
            norm = norm + values * values
            cross = cross + values * right
            first_ref[pl.ds(tile, 1), :] = values[ROWS - 1 :]
            exact = rows.astype(F32)
            res[at, :] = turned(exact[:ROWS], exact[ROWS : ROWS + 1])
    line = line_sums(norm, cross)
    lines = stacked([line, pltpu.roll(line, ROWS, 1)], 8)
    put_scores(pieces, res, other_ref, mine_ref, lines)


def tail_kernel(own, one, two, three, scores_ref, rate_ref, tail_ref, lines_ref):
    scores, norm, cross = unpacked(own, one, two, three)
    rate = jnp.where(place()[2] == 0, rate_ref[:, :HALF], rate_ref[:, HALF:])
    weighted = rate * scores
    tail_ref[...] = line_sums(tile_sums(weighted * scores_ref[...]), tile_sums(weighted * scores))
    lines_ref[...] = stacked([norm, cross], 8)


def end_kernel(tails_ref, scalars_ref, lines_ref, w_ref, grad_ref, first_ref, weights_ref, widths_ref):
    tail = tails_ref[0]
    for e in range(1, EN):
        tail = tail + tails_ref[e]
    mixed, square = tail, pltpu.roll(tail, ROWS, 1)
    step_one, curv, norm = scalars_ref[0:1], scalars_ref[1:2], scalars_ref[2:3]
    norm_next, cross = lines_ref[0:1], lines_ref[1:2]
    ratio = norm_next / norm
    curvature = square + 2.0 * ratio * mixed + ratio * ratio * curv
    curvature = curvature + LAMBDA * (norm_next + 2.0 * ratio * cross + ratio * ratio * norm)
    step_two = norm_next / curvature
    widths = step_one * norm + step_two * (cross + ratio * norm)
    widths_ref[...] = widths[:, : ROWS - 1]
    at = slice(ROWS - 1, ROWS)
    grad = grad_ref[...]
    step = step_one[:, at] * grad + step_two[:, at] * (first_ref[...] + ratio[:, at] * grad)
    weights_ref[...] = w_ref[...] - step


def on_device(events, labels, weights, contexts):
    features = TILES * 128
    tiled = weights.reshape(TILES, 128)

    whole = shaped(COUNT, features, dtype=BF16)
    sems = pltpu.SemaphoreType.DMA((10,))

    (picked,) = kernel_call(
        pick_kernel,
        [SMEM, HBM],
        [shaped(TILES, ROWS, 128, dtype=BF16)],
        (contexts, events),
        [
            pltpu.VMEM((ROWS - 1, 16, features), BF16),
            pltpu.VMEM((ROWS, features), F32),
            pltpu.SemaphoreType.DMA((ROWS - 1,)),
        ],
        micros=2,
        room=ROOM,
    )
    chunks = lax.all_to_all(picked, "event", 0, 0)
    margin, held = kernel_call(
        margin_kernel,
        [VMEM, HBM, HBM],
        [shaped(COUNT // 128, 128), whole],
        (weights.reshape(1, features), events, picked),
        [pltpu.VMEM((1, features), F32), sems],
        micros=4,
        room=40,
    )

    margin = margin + core_move(margin)
    rate, grad = kernel_call(
        gradient_kernel,
        [VMEM] * 6,
        [shaped(1, COUNT), shaped(TILES, 128)],
        (held, margin, *y_moves(margin), labels.reshape(COUNT // 128, 128)),
        [pltpu.VMEM((16, COUNT), BF16)],
        micros=4,
        room=8,
    )
    (message,) = kernel_call(
        spread_kernel, [VMEM] * 2, [shaped(ZN, ROWS + 2 * TILES, 128, dtype=BF16)], (chunks, grad)
    )
    message = z_exchange(message)
    (message,) = kernel_call(
        collect_kernel, [VMEM], [shaped(QUARTER * ROWS + 2 * TILES, 128, dtype=BF16)], (message,)
    )

    moved = x_moves(message)
    (held,) = kernel_call(load_kernel, [HBM, HBM], [whole], (events, message), [sems], micros=5, room=40)

    half = [shaped(ROWS + 8, HALF), shaped(ROWS + 8, HALF)]
    rhs, grad, other, mine = kernel_call(
        scores_kernel,
        [VMEM] * 6,
        [shaped(ROWS, features, dtype=BF16), shaped(TILES, 128)] + half,
        (held, tiled, message, *moved),
        [pltpu.VMEM((features, 128), BF16)],
        micros=3,
        room=8,
    )
    packed = [shaped(ROWS + 8, HALF, dtype=BF16)]
    (message,) = kernel_call(pack_kernel, [VMEM] * 2, packed, (mine, core_move(other)))
    scores, norm = kernel_call(
        unpack_kernel, [VMEM] * 4, [shaped(ROWS, HALF), shaped(8, 128)], (message, *y_moves(message))
    )

    part = shaped(QUARTER * ROWS + 16, 128, dtype=BF16)
    own, curv, one, two, three = kernel_call(
        hessian_kernel,
        [VMEM] * 4,
        [shaped(QUARTER * ROWS, 128), shaped(8, 128), part, part, part],
        (held, scores, core_move(scores), rate),
        [pltpu.VMEM((ROWS + 16, COUNT), BF16)],
        micros=4,
        room=8,
    )
    moved = [
        lax.ppermute(v, "event", [(i, (i + k * ZN) % EN) for i in range(EN)])
        for k, v in ((1, one), (2, two), (3, three))
    ]
    shard = [shaped(ZN, ROWS + 8, 128, dtype=BF16)]
    (message,) = kernel_call(cut_kernel, [VMEM] * 5, shard, (own, curv, *moved))
    message, scalars = kernel_call(
        residual_kernel,
        [VMEM] * 4,
        shard + [shaped(8, 128)],
        (z_exchange(message), norm, rhs, grad),
    )
    message = z_exchange(message)

    other, mine, first = kernel_call(
        second_kernel,
        [VMEM] * 7,
        half + [shaped(TILES, 128)],
        (held, rhs, grad, message, *x_moves(message)),
        [pltpu.VMEM((features, 128), BF16)],
        micros=4,
        room=8,
    )
    (message,) = kernel_call(pack_kernel, [VMEM] * 2, packed, (mine, core_move(other)))
    tail, lines = kernel_call(
        tail_kernel,
        [VMEM] * 6,
        [shaped(1, 128), shaped(8, 128)],
        (message, *y_moves(message), scores, rate),
    )
    tail = tail + core_move(tail)
    tails = lax.all_to_all(jnp.broadcast_to(tail[None], (EN, 1, 128)), "event", 0, 0)
    updated, widths = kernel_call(
        end_kernel, [VMEM] * 6, [shaped(TILES, 128), shaped(1, ROWS - 1)], (tails, scalars, lines, tiled, grad, first)
    )
    return updated.reshape(features), widths.reshape(ROWS - 1)


def solution(mesh):
    in_specs = (P("event", "feat"), P("event"), P("feat"), P())
    out_specs = (P("feat"), P())
    return jax.shard_map(on_device, mesh=mesh, in_specs=in_specs, out_specs=out_specs, check_vma=False)
```

```python
import functools

import jax
import jax.numpy as jnp
from jax import lax
from jax.experimental import pallas as pl
from jax.experimental.pallas import tpu as pltpu
from jax.sharding import PartitionSpec as P

LAMBDA = 0.5
XN, ZN, YN, CN = 4, 8, 4, 2
EN = XN * ZN
ROWS = 64
TILES = 32
QUARTER = TILES // XN
COUNT = 1280
HALF = COUNT // 2
WINDOW = 10
ROOM = 48
F32, BF16 = jnp.float32, jnp.bfloat16
VMEM = pl.BlockSpec(memory_space=pltpu.VMEM)
SMEM = pl.BlockSpec(memory_space=pltpu.SMEM)
HBM = pl.BlockSpec(memory_space=pltpu.HBM)
ACROSS = (((1,), (1,)), ((), ()))


def shaped(*shape, dtype=F32):
    return jax.ShapeDtypeStruct(shape, dtype)


def kernel_call(body, ins, outs, args, scratch=(), micros=0.5, room=8):
    return pl.pallas_call(
        body,
        out_shape=outs,
        in_specs=ins,
        out_specs=[VMEM] * len(outs),
        scratch_shapes=list(scratch),
        compiler_params=pltpu.CompilerParams(vmem_limit_bytes=room << 20),
        cost_estimate=pl.CostEstimate(flops=0, bytes_accessed=int(micros * 3.6e6), transcendentals=0),
    )(*args)


def x_moves(v):
    n = XN * ZN
    return [lax.ppermute(v, "event", [(i, (i + k * ZN) % n) for i in range(n)]) for k in (1, 2, 3)]


def y_moves(v):
    n = YN * CN
    return [lax.ppermute(v, "feat", [(i, (i + k * CN) % n) for i in range(n)]) for k in (1, 2, 3)]


def core_move(v):
    return lax.ppermute(v, "feat", [(i, i ^ 1) for i in range(YN * CN)])


def z_exchange(v):
    groups = [[x * ZN + z for z in range(ZN)] for x in range(XN)]
    return lax.all_to_all(v, "event", 0, 0, axis_index_groups=groups)


def four(own, one, two, three):
    return (own + two) + (one + three)


def pair_of(v):
    lead = v.astype(BF16)
    return lead, (v - lead.astype(F32)).astype(BF16)


def triple_of(v):
    lead, rest = v.astype(BF16), v
    rest = v - lead.astype(F32)
    mid = rest.astype(BF16)
    return lead, mid, (rest - mid.astype(F32)).astype(BF16)


def row_is(shape, i):
    return lax.broadcasted_iota(jnp.int32, shape, 0) == i


def stacked(lines, rows):
    out = jnp.zeros((rows, lines[0].shape[1]), F32)
    for i, line in enumerate(lines):
        out = jnp.where(row_is(out.shape, i), line.astype(F32), out)
    return out


def joined(v):
    top = v[:ROWS]
    return top + jnp.where(row_is(top.shape, ROWS - 1), v[ROWS : ROWS + 1], 0.0)


def line_sums(top, bottom):
    return jnp.sum(jnp.transpose(jnp.concatenate([top, bottom], axis=0)), axis=0, keepdims=True)


def tile_sums(v):
    total = v[:, :128]
    for t in range(1, v.shape[1] // 128):
        total = total + v[:, t * 128 : (t + 1) * 128]
    return total


class Stream:
    def __init__(self, pieces, sems):
        self.copies = [pltpu.make_async_copy(source, target, sems.at[i]) for i, (source, target) in enumerate(pieces)]
        for copy in self.copies[:WINDOW]:
            copy.start()

    def take(self, i):
        self.copies[i].wait()
        if i + WINDOW < len(self.copies):
            self.copies[i + WINDOW].start()


class Rows:
    def __init__(self, events_ref, held, sems, starts):
        self.events, self.held = events_ref, held
        self.starts = [pl.multiple_of(start, 128) for start in starts]
        if held is not None:
            pieces = [
                (events_ref.at[pl.ds(start, 128), :], held.at[pl.ds(i * 128, 128), :])
                for i, start in enumerate(self.starts)
            ]
            self.stream = Stream(pieces, sems)

    def take(self, first, count):
        if self.held is None:
            return self.events[pl.ds(self.starts[first], count * 128), :]
        for i in range(count):
            self.stream.take(first + i)
        return self.held[first * 128 : (first + count) * 128, :]


def place():
    event = lax.axis_index("event")
    return lax.div(event, ZN), lax.rem(event, ZN), lax.rem(lax.axis_index("feat"), CN)


def pick_kernel(contexts_ref, events_ref, out_ref, blocks, rows, sems):
    base = lax.axis_index("event") * COUNT

    def owned(j):
        return jnp.logical_and(contexts_ref[j] >= base, contexts_ref[j] < base + COUNT)

    def fetch(j):
        start = pl.multiple_of(lax.div(contexts_ref[j] - base, 16) * 16, 16)
        return pltpu.make_async_copy(events_ref.at[pl.ds(start, 16), :], blocks.at[j], sems.at[j])

    @pl.loop(0, ROWS - 1, unroll=9)
    def _(j):
        @pl.when(owned(j))
        def _():
            fetch(j).start()

    rows[...] = jnp.zeros_like(rows)

    @pl.loop(0, ROWS - 1, unroll=9)
    def _(j):
        @pl.when(owned(j))
        def _():
            fetch(j).wait()
            block = blocks[j].astype(F32)
            found = jnp.where(row_is(block.shape, lax.rem(contexts_ref[j] - base, 16)), block, 0.0)
            rows[pl.ds(j, 1), :] = jnp.sum(found, axis=0, keepdims=True)

    for t in range(TILES):
        out_ref[t] = rows[:, t * 128 : (t + 1) * 128].astype(BF16)


def margin_kernel(w_ref, events_ref, _after, margin_ref, held, w, sems):
    pieces = Rows(events_ref, held, sems, [i * 128 for i in range(COUNT // 128)])
    w[...] = w_ref[...].astype(BF16).astype(F32)
    for c in range(COUNT // 128):
        pieces.take(c, 1)
        sums = []
        for r in range(c * 128, (c + 1) * 128, 16):
            total = jnp.zeros((16, 128), F32)
            for t in range(TILES):
                at = slice(t * 128, (t + 1) * 128)
                total = total + held[r : r + 16, at].astype(F32) * w[:, at]
            sums.append(total)
        turned = jnp.transpose(jnp.concatenate(sums, axis=0))
        margin_ref[c : c + 1, :] = jnp.sum(turned, axis=0, keepdims=True)


def load_kernel(events_ref, _after, held, sems):
    pieces = Rows(events_ref, held, sems, [i * 128 for i in range(COUNT // 128)])
    for i in range(COUNT // 128):
        pieces.stream.take(i)


def gradient_kernel(events_ref, own, one, two, three, labels_ref, rate_ref, grad_ref, errs):
    margin = four(own[...], one[...], two[...], three[...])
    chance = jax.nn.sigmoid(margin)
    rate = chance * (1.0 - chance)
    errors = chance - labels_ref[...].astype(F32)
    lead, rest = pair_of(errors)
    lead, rest = lead.astype(F32), rest.astype(F32)
    for i in range(COUNT // 128):
        at = slice(i * 128, (i + 1) * 128)
        rate_ref[:, at] = rate[i : i + 1]
        errs[:, at] = stacked([lead[i : i + 1], rest[i : i + 1]], 16).astype(BF16)
    for c in range(8):
        part = jnp.dot(errs[...], events_ref[:, c * 512 : (c + 1) * 512], preferred_element_type=F32)
        line = part[:1] + part[1:2]
        for u in range(4):
            grad_ref[c * 4 + u : c * 4 + u + 1, :] = line[:, u * 128 : (u + 1) * 128]


def spread_kernel(chunks_ref, grad_ref, out_ref):
    total = chunks_ref[0].astype(F32)
    for e in range(1, EN):
        total = total + chunks_ref[e].astype(F32)
    lead, rest = pair_of(grad_ref[...])
    for z in range(ZN):
        out_ref[z, :ROWS, :] = total.astype(BF16)
        out_ref[z, ROWS : ROWS + TILES, :] = lead
        out_ref[z, ROWS + TILES :, :] = rest


def collect_kernel(in_ref, out_ref):
    grad = jnp.zeros((TILES, 128), F32)
    for z in range(ZN):
        out_ref[z * ROWS : (z + 1) * ROWS, :] = in_ref[z, :ROWS, :]
        grad = grad + (in_ref[z, ROWS : ROWS + TILES, :].astype(F32) + in_ref[z, ROWS + TILES :, :].astype(F32))
    lead, rest = pair_of(grad)
    out_ref[QUARTER * ROWS : QUARTER * ROWS + TILES, :] = lead
    out_ref[QUARTER * ROWS + TILES :, :] = rest


def halves(events_ref, core):
    starts = [half * HALF + i * 128 for half in (1 - core, core) for i in range(HALF // 128)]
    return Rows(events_ref, None, None, starts)


def put_scores(pieces, rhs, other_ref, own_ref, lines):
    for first, out_ref in ((0, other_ref), (HALF // 128, own_ref)):
        for at, size in ((0, 2), (2, 3)):
            part = jnp.dot(pieces.take(first + at, size), rhs[...], preferred_element_type=F32)
            for t in range(size):
                columns = slice((at + t) * 128, (at + t + 1) * 128)
                out_ref[:ROWS, columns] = joined(jnp.transpose(part[t * 128 : (t + 1) * 128]))
                out_ref[ROWS:, columns] = lines if at + t == 0 else jnp.zeros_like(lines)


def turned(top, rest):
    below = jnp.where(row_is(top.shape, 0), rest.astype(F32), 0.0)
    return jnp.transpose(jnp.concatenate([top, below], axis=0)).astype(BF16)


def scores_kernel(
    events_ref, w_ref, own, one, two, three, rhs_ref, grad_ref, other_ref, mine_ref, rhs
):
    x, _, core = place()
    pieces = halves(events_ref, core)
    tail = QUARTER * ROWS
    grads = [p[tail : tail + TILES, :].astype(F32) + p[tail + TILES :, :].astype(F32) for p in (own, one, two, three)]
    grad_ref[...] = four(*grads) + LAMBDA * w_ref[...]
    norms = []
    for k, part in enumerate((own, one, two, three)):
        quarter = lax.rem(x + XN - k, XN)
        norm = jnp.zeros((ROWS, 128), F32)
        for t in range(QUARTER):
            tile = quarter * QUARTER + t
            grad = grad_ref[pl.ds(tile, 1), :]
            lead, rest = pair_of(grad)
            values = part[t * ROWS : (t + 1) * ROWS, :].astype(F32)
            last = row_is(values.shape, ROWS - 1)
            exact = jnp.where(last, grad, values)
            norm = norm + exact * exact
            at = pl.ds(pl.multiple_of(tile * 128, 128), 128)
            top = jnp.where(last, lead.astype(F32), values)
            rhs_ref[:, at] = top.astype(BF16)
            rhs[at, :] = turned(top, rest)
        norms.append(norm)
    line = line_sums(four(*norms), jnp.zeros_like(norm))
    put_scores(pieces, rhs, other_ref, mine_ref, stacked([line], 8))


def pack_kernel(own, other, out_ref):
    total = own[...] + other[...]
    scores, lines = total[:ROWS], total[ROWS:]
    lead = scores.astype(BF16)
    rest = scores[ROWS - 1 :] - lead[ROWS - 1 :].astype(F32)
    out_ref[:ROWS, :] = lead
    out_ref[ROWS:, :] = stacked([rest, *triple_of(lines[:1]), *triple_of(lines[1:2])], 8).astype(BF16)


def unpacked(own, one, two, three):
    total = four(*(p[...].astype(F32) for p in (own, one, two, three)))
    first = total[65:66] + total[66:67] + total[67:68]
    second = total[68:69] + total[69:70] + total[70:71]
    return joined(total), first[:, :128], second[:, :128]


def unpack_kernel(own, one, two, three, scores_ref, norm_ref):
    scores, norm, _ = unpacked(own, one, two, three)
    scores_ref[...] = scores
    norm_ref[...] = stacked([norm], 8)


def hessian_kernel(
    events_ref, mine_ref, theirs_ref, rate_ref, own_ref, curv_ref, one_ref, two_ref, three_ref, q
):
    x, _, core = place()
    outs = ((2, two_ref), (1, one_ref), (3, three_ref), (0, own_ref))
    curv = jnp.zeros((ROWS, 128), F32)
    for half in range(2):
        at = slice(half * HALF, (half + 1) * HALF)
        scores, rate = jnp.where(core == half, mine_ref[...], theirs_ref[...]), rate_ref[:, at]
        weighted = rate * scores
        curv = curv + tile_sums(weighted * scores)
        lead = weighted.astype(BF16)
        q[:ROWS, at] = lead
        q[ROWS:, at] = stacked([weighted[ROWS - 1 :] - lead[ROWS - 1 :].astype(F32)], 16).astype(BF16)
    triple = [v.astype(F32) for v in triple_of(line_sums(curv, jnp.zeros_like(curv)))]
    curv_ref[...] = stacked(triple, 8)
    for k, out_ref in outs:
        rests = []
        for part in range(2):
            start = pl.multiple_of(lax.rem(x + k, XN) * QUARTER * 128 + part * 512, 512)
            total = joined(jnp.dot(q[...], events_ref[:, pl.ds(start, 512)], preferred_element_type=F32))
            for u in range(4):
                t = part * 4 + u
                values = total[:, u * 128 : (u + 1) * 128]
                out_ref[t * ROWS : (t + 1) * ROWS, :] = values.astype(out_ref.dtype)
                rests.append(values[ROWS - 1 :] - values[ROWS - 1 :].astype(BF16).astype(F32))
        if k:
            out_ref[QUARTER * ROWS :, :] = stacked(rests + triple, 16).astype(BF16)


def cut_kernel(own, curv_ref, one, two, three, out_ref):
    top = QUARTER * ROWS
    tails = [p[top:, :].astype(F32) for p in (one, two, three)]
    curvs = [curv_ref[0:1] + curv_ref[1:2] + curv_ref[2:3]]
    curvs += [v[QUARTER : QUARTER + 1] + v[QUARTER + 1 : QUARTER + 2] + v[QUARTER + 2 : QUARTER + 3] for v in tails]
    curv = triple_of(four(*curvs))
    for t in range(QUARTER):
        at = slice(t * ROWS, (t + 1) * ROWS)
        total = four(own[at, :], one[at, :].astype(F32), two[at, :].astype(F32), three[at, :].astype(F32))
        rest = tails[0][t : t + 1] + tails[1][t : t + 1] + tails[2][t : t + 1]
        total = total + jnp.where(row_is(total.shape, ROWS - 1), rest, 0.0)
        lead = total.astype(BF16)
        rest = total[ROWS - 1 :] - lead[ROWS - 1 :].astype(F32)
        out_ref[t, :ROWS, :] = lead
        out_ref[t, ROWS:, :] = stacked([rest, *curv], 8).astype(BF16)


def residual_kernel(in_ref, norm_ref, rhs_ref, grad_ref, out_ref, scalars_ref):
    x, z, _ = place()
    tile = x * QUARTER + z
    total = in_ref[0].astype(F32)
    for z in range(1, ZN):
        total = total + in_ref[z].astype(F32)
    curv = total[65:66] + total[66:67] + total[67:68]
    norm = norm_ref[:1]
    step = norm / (curv + LAMBDA * norm)
    square = (ROWS, 128)
    eye = lax.broadcasted_iota(jnp.int32, square, 0) == lax.broadcasted_iota(jnp.int32, square, 1)
    column = jnp.sum(jnp.where(eye, step, 0.0), axis=1, keepdims=True)
    right = rhs_ref[:, pl.ds(pl.multiple_of(tile * 128, 128), 128)].astype(F32)
    right = jnp.where(row_is(square, ROWS - 1), grad_ref[pl.ds(tile, 1), :], right)
    residual = right - column * (joined(total) + LAMBDA * right)
    lead = residual.astype(BF16)
    rest = stacked([residual[ROWS - 1 :] - lead[ROWS - 1 :].astype(F32)], 8).astype(BF16)
    for z in range(ZN):
        out_ref[z, :ROWS, :] = lead
        out_ref[z, ROWS:, :] = rest
    scalars_ref[...] = stacked([step, curv, norm], 8)


def repack_kernel(in_ref, out_ref):
    rests = []
    for t in range(QUARTER):
        rows = in_ref[t]
        out_ref[t * ROWS : (t + 1) * ROWS, :] = rows[:ROWS]
        rests.append(rows[ROWS:].astype(F32)[:1])
    out_ref[QUARTER * ROWS :, :] = stacked(rests, 16).astype(BF16)


def quarter_work(k, events_ref, rhs_ref, grad_ref, part, first_ref, res):
    x, _, _ = place()
    quarter = lax.rem(x + XN - k, XN)
    norm = jnp.zeros((ROWS, 128), F32)
    cross = jnp.zeros((ROWS, 128), F32)
    rests = part[QUARTER * ROWS :, :].astype(F32)
    for t in range(QUARTER):
        tile = quarter * QUARTER + t
        at = pl.ds(pl.multiple_of(tile * 128, 128), 128)
        top, rest = part[t * ROWS : (t + 1) * ROWS, :].astype(F32), rests[t : t + 1]
        last = row_is(top.shape, ROWS - 1)
        values = top + jnp.where(last, rest, 0.0)
        right = jnp.where(last, grad_ref[pl.ds(tile, 1), :], rhs_ref[:, at].astype(F32))
        norm = norm + values * values
        cross = cross + values * right
        first_ref[t : t + 1, :] = values[ROWS - 1 :]
        res[t * 128 : (t + 1) * 128, :] = turned(top, rest)
    columns = pl.ds(pl.multiple_of(quarter * QUARTER * 128, 1024), QUARTER * 128)
    scores = jnp.dot(events_ref[:, columns], res[...], preferred_element_type=F32)
    return scores, jnp.concatenate([norm, cross], axis=0)


def open_kernel(events_ref, rhs_ref, grad_ref, part, total_ref, sums_ref, first_ref, res):
    total_ref[...], sums_ref[...] = quarter_work(0, events_ref, rhs_ref, grad_ref, part, first_ref, res)


def add_kernel(k, events_ref, rhs_ref, grad_ref, part, total, total_ref, sums_ref, first_ref, res):
    scores, sums_ref[...] = quarter_work(k, events_ref, rhs_ref, grad_ref, part, first_ref, res)
    total_ref[...] = total[...] + scores


def close_kernel(
    events_ref, rhs_ref, grad_ref, part, total, own, two, three, other_ref, mine_ref, first_ref, res, scores_ref
):
    scores, one = quarter_work(1, events_ref, rhs_ref, grad_ref, part, first_ref, res)
    scores_ref[...] = total[...] + scores
    sums = four(own[...], one, two[...], three[...])
    line = line_sums(sums[:ROWS], sums[ROWS:])
    lines = stacked([line, pltpu.roll(line, ROWS, 1)], 8)
    core = place()[2]
    for half, out_ref in ((1 - core, other_ref), (core, mine_ref)):
        for t in range(HALF // 128):
            rows = scores_ref[pl.ds(pl.multiple_of(half * HALF + t * 128, 128), 128), :]
            columns = slice(t * 128, (t + 1) * 128)
            out_ref[:ROWS, columns] = joined(jnp.transpose(rows))
            out_ref[ROWS:, columns] = lines if t == 0 else jnp.zeros_like(lines)


def tail_kernel(own, one, two, three, scores_ref, rate_ref, tail_ref, lines_ref):
    scores, norm, cross = unpacked(own, one, two, three)
    rate = jnp.where(place()[2] == 0, rate_ref[:, :HALF], rate_ref[:, HALF:])
    weighted = rate * scores
    tail_ref[...] = line_sums(tile_sums(weighted * scores_ref[...]), tile_sums(weighted * scores))
    lines_ref[...] = stacked([norm, cross], 8)


def end_kernel(
    tails_ref, scalars_ref, lines_ref, w_ref, grad_ref, own, one, two, three, weights_ref, widths_ref
):
    tail = tails_ref[0]
    for e in range(1, EN):
        tail = tail + tails_ref[e]
    mixed, square = tail, pltpu.roll(tail, ROWS, 1)
    step_one, curv, norm = scalars_ref[0:1], scalars_ref[1:2], scalars_ref[2:3]
    norm_next, cross = lines_ref[0:1], lines_ref[1:2]
    ratio = norm_next / norm
    curvature = square + 2.0 * ratio * mixed + ratio * ratio * curv
    curvature = curvature + LAMBDA * (norm_next + 2.0 * ratio * cross + ratio * ratio * norm)
    step_two = norm_next / curvature
    widths = step_one * norm + step_two * (cross + ratio * norm)
    widths_ref[...] = widths[:, : ROWS - 1]
    at = slice(ROWS - 1, ROWS)
    x, _, _ = place()
    for k, first in enumerate((own, one, two, three)):
        rows = pl.ds(pl.multiple_of(lax.rem(x + XN - k, XN) * QUARTER, QUARTER), QUARTER)
        grad = grad_ref[rows, :]
        step = step_one[:, at] * grad + step_two[:, at] * (first[...] + ratio[:, at] * grad)
        weights_ref[rows, :] = w_ref[rows, :] - step


def on_device(events, labels, weights, contexts):
    features = TILES * 128
    tiled = weights.reshape(TILES, 128)

    whole = shaped(COUNT, features, dtype=BF16)
    sems = pltpu.SemaphoreType.DMA((10,))

    (picked,) = kernel_call(
        pick_kernel,
        [SMEM, HBM],
        [shaped(TILES, ROWS, 128, dtype=BF16)],
        (contexts, events),
        [
            pltpu.VMEM((ROWS - 1, 16, features), BF16),
            pltpu.VMEM((ROWS, features), F32),
            pltpu.SemaphoreType.DMA((ROWS - 1,)),
        ],
        micros=2,
        room=ROOM,
    )
    chunks = lax.all_to_all(picked, "event", 0, 0)
    margin, held = kernel_call(
        margin_kernel,
        [VMEM, HBM, HBM],
        [shaped(COUNT // 128, 128), whole],
        (weights.reshape(1, features), events, picked),
        [pltpu.VMEM((1, features), F32), sems],
        micros=4,
        room=40,
    )

    margin = margin + core_move(margin)
    rate, grad = kernel_call(
        gradient_kernel,
        [VMEM] * 6,
        [shaped(1, COUNT), shaped(TILES, 128)],
        (held, margin, *y_moves(margin), labels.reshape(COUNT // 128, 128)),
        [pltpu.VMEM((16, COUNT), BF16)],
        micros=4,
        room=8,
    )
    (message,) = kernel_call(
        spread_kernel, [VMEM] * 2, [shaped(ZN, ROWS + 2 * TILES, 128, dtype=BF16)], (chunks, grad)
    )
    message = z_exchange(message)
    (message,) = kernel_call(
        collect_kernel, [VMEM], [shaped(QUARTER * ROWS + 2 * TILES, 128, dtype=BF16)], (message,)
    )

    moved = x_moves(message)
    (held,) = kernel_call(load_kernel, [HBM, HBM], [whole], (events, message), [sems], micros=5, room=40)

    half = [shaped(ROWS + 8, HALF), shaped(ROWS + 8, HALF)]
    rhs, grad, other, mine = kernel_call(
        scores_kernel,
        [VMEM] * 6,
        [shaped(ROWS, features, dtype=BF16), shaped(TILES, 128)] + half,
        (held, tiled, message, *moved),
        [pltpu.VMEM((features, 128), BF16)],
        micros=3,
        room=8,
    )
    packed = [shaped(ROWS + 8, HALF, dtype=BF16)]
    (message,) = kernel_call(pack_kernel, [VMEM] * 2, packed, (mine, core_move(other)))
    scores, norm = kernel_call(
        unpack_kernel, [VMEM] * 4, [shaped(ROWS, HALF), shaped(8, 128)], (message, *y_moves(message))
    )

    part = shaped(QUARTER * ROWS + 16, 128, dtype=BF16)
    own, curv, one, two, three = kernel_call(
        hessian_kernel,
        [VMEM] * 4,
        [shaped(QUARTER * ROWS, 128), shaped(8, 128), part, part, part],
        (held, scores, core_move(scores), rate),
        [pltpu.VMEM((ROWS + 16, COUNT), BF16)],
        micros=4,
        room=8,
    )
    moved = [
        lax.ppermute(v, "event", [(i, (i + k * ZN) % EN) for i in range(EN)])
        for k, v in ((1, one), (2, two), (3, three))
    ]
    shard = [shaped(ZN, ROWS + 8, 128, dtype=BF16)]
    (message,) = kernel_call(cut_kernel, [VMEM] * 5, shard, (own, curv, *moved))
    message, scalars = kernel_call(
        residual_kernel,
        [VMEM] * 4,
        shard + [shaped(8, 128)],
        (z_exchange(message), norm, rhs, grad),
    )
    message = z_exchange(message)

    (message,) = kernel_call(repack_kernel, [VMEM], [part], (message,))
    one, two, three = x_moves(message)
    sums = [shaped(COUNT, 128), shaped(128, 128)]
    first = [shaped(QUARTER, 128)]
    scratch = [pltpu.VMEM((QUARTER * 128, 128), BF16)]
    total, sum_own, first_own = kernel_call(
        open_kernel, [VMEM] * 4, sums + first, (held, rhs, grad, message), scratch, micros=1, room=8
    )
    total, sum_three, first_three = kernel_call(
        functools.partial(add_kernel, 3),
        [VMEM] * 5,
        sums + first,
        (held, rhs, grad, three, total),
        scratch,
        micros=1,
        room=8,
    )
    total, sum_two, first_two = kernel_call(
        functools.partial(add_kernel, 2),
        [VMEM] * 5,
        sums + first,
        (held, rhs, grad, two, total),
        scratch,
        micros=1,
        room=8,
    )
    other, mine, first_one = kernel_call(
        close_kernel,
        [VMEM] * 8,
        half + first,
        (held, rhs, grad, one, total, sum_own, sum_two, sum_three),
        scratch + [pltpu.VMEM((COUNT, 128), F32)],
        micros=1,
        room=8,
    )
    (message,) = kernel_call(pack_kernel, [VMEM] * 2, packed, (mine, core_move(other)))
    tail, lines = kernel_call(
        tail_kernel,
        [VMEM] * 6,
        [shaped(1, 128), shaped(8, 128)],
        (message, *y_moves(message), scores, rate),
    )
    tail = tail + core_move(tail)
    tails = lax.all_to_all(jnp.broadcast_to(tail[None], (EN, 1, 128)), "event", 0, 0)
    updated, widths = kernel_call(
        end_kernel, [VMEM] * 9, [shaped(TILES, 128), shaped(1, ROWS - 1)], (tails, scalars, lines, tiled, grad, first_own, first_one, first_two, first_three)
    )
    return updated.reshape(features), widths.reshape(ROWS - 1)


def solution(mesh):
    in_specs = (P("event", "feat"), P("event"), P("feat"), P())
    out_specs = (P("feat"), P())
    return jax.shard_map(on_device, mesh=mesh, in_specs=in_specs, out_specs=out_specs, check_vma=False)
```

```python
import functools

import jax
import jax.numpy as jnp
from jax import lax
from jax.experimental import pallas as pl
from jax.experimental.pallas import tpu as pltpu
from jax.sharding import PartitionSpec as P

LAMBDA = 0.5
XN, ZN, YN, CN = 4, 8, 4, 2
EN = XN * ZN
ROWS = 64
TILES = 32
QUARTER = TILES // XN
COUNT = 1280
HALF = COUNT // 2
WINDOW = 10
ROOM = 48
F32, BF16 = jnp.float32, jnp.bfloat16
VMEM = pl.BlockSpec(memory_space=pltpu.VMEM)
SMEM = pl.BlockSpec(memory_space=pltpu.SMEM)
HBM = pl.BlockSpec(memory_space=pltpu.HBM)
ACROSS = (((1,), (1,)), ((), ()))


def shaped(*shape, dtype=F32):
    return jax.ShapeDtypeStruct(shape, dtype)


def kernel_call(body, ins, outs, args, scratch=(), micros=0.5, room=8):
    return pl.pallas_call(
        body,
        out_shape=outs,
        in_specs=ins,
        out_specs=[VMEM] * len(outs),
        scratch_shapes=list(scratch),
        compiler_params=pltpu.CompilerParams(vmem_limit_bytes=room << 20),
        cost_estimate=pl.CostEstimate(flops=0, bytes_accessed=int(micros * 3.6e6), transcendentals=0),
    )(*args)


def x_moves(v):
    n = XN * ZN
    return [lax.ppermute(v, "event", [(i, (i + k * ZN) % n) for i in range(n)]) for k in (1, 2, 3)]


def x_scatter(one, two, three):
    n = XN * ZN
    return [
        lax.ppermute(v, "event", [(i, (i + k * ZN) % n) for i in range(n)])
        for k, v in ((1, one), (2, two), (3, three))
    ]


def y_moves(v):
    n = YN * CN
    return [lax.ppermute(v, "feat", [(i, (i + k * CN) % n) for i in range(n)]) for k in (1, 2, 3)]


def core_move(v):
    return lax.ppermute(v, "feat", [(i, i ^ 1) for i in range(YN * CN)])


def z_exchange(v):
    groups = [[x * ZN + z for z in range(ZN)] for x in range(XN)]
    return lax.all_to_all(v, "event", 0, 0, axis_index_groups=groups)


def four(own, one, two, three):
    return (own + two) + (one + three)


def pair_of(v):
    lead = v.astype(BF16)
    return lead, (v - lead.astype(F32)).astype(BF16)


def triple_of(v):
    lead, rest = v.astype(BF16), v
    rest = v - lead.astype(F32)
    mid = rest.astype(BF16)
    return lead, mid, (rest - mid.astype(F32)).astype(BF16)


def row_is(shape, i):
    return lax.broadcasted_iota(jnp.int32, shape, 0) == i


def stacked(lines, rows):
    out = jnp.zeros((rows, lines[0].shape[1]), F32)
    for i, line in enumerate(lines):
        out = jnp.where(row_is(out.shape, i), line.astype(F32), out)
    return out


def joined(v):
    top = v[:ROWS]
    return top + jnp.where(row_is(top.shape, ROWS - 1), v[ROWS : ROWS + 1], 0.0)


def line_sums(top, bottom):
    return jnp.sum(jnp.transpose(jnp.concatenate([top, bottom], axis=0)), axis=0, keepdims=True)


def tile_sums(v):
    total = v[:, :128]
    for t in range(1, v.shape[1] // 128):
        total = total + v[:, t * 128 : (t + 1) * 128]
    return total


class Stream:
    def __init__(self, pieces, sems):
        self.copies = [pltpu.make_async_copy(source, target, sems.at[i]) for i, (source, target) in enumerate(pieces)]
        for copy in self.copies[:WINDOW]:
            copy.start()

    def take(self, i):
        self.copies[i].wait()
        if i + WINDOW < len(self.copies):
            self.copies[i + WINDOW].start()


class Rows:
    def __init__(self, events_ref, held, sems, starts):
        self.events, self.held = events_ref, held
        self.starts = [pl.multiple_of(start, 128) for start in starts]
        if held is not None:
            pieces = [
                (events_ref.at[pl.ds(start, 128), :], held.at[pl.ds(i * 128, 128), :])
                for i, start in enumerate(self.starts)
            ]
            self.stream = Stream(pieces, sems)

    def take(self, first, count):
        if self.held is None:
            return self.events[pl.ds(self.starts[first], count * 128), :]
        for i in range(count):
            self.stream.take(first + i)
        return self.held[first * 128 : (first + count) * 128, :]


def place():
    event = lax.axis_index("event")
    return lax.div(event, ZN), lax.rem(event, ZN), lax.rem(lax.axis_index("feat"), CN)


def pick_kernel(contexts_ref, events_ref, own_ref, one_ref, two_ref, three_ref, blocks, rows, sems):
    base = lax.axis_index("event") * COUNT

    def owned(j):
        return jnp.logical_and(contexts_ref[j] >= base, contexts_ref[j] < base + COUNT)

    def fetch(j):
        start = pl.multiple_of(lax.div(contexts_ref[j] - base, 16) * 16, 16)
        return pltpu.make_async_copy(events_ref.at[pl.ds(start, 16), :], blocks.at[j], sems.at[j])

    @pl.loop(0, ROWS - 1, unroll=9)
    def _(j):
        @pl.when(owned(j))
        def _():
            fetch(j).start()

    rows[...] = jnp.zeros_like(rows)

    @pl.loop(0, ROWS - 1, unroll=9)
    def _(j):
        @pl.when(owned(j))
        def _():
            fetch(j).wait()
            block = blocks[j].astype(F32)
            found = jnp.where(row_is(block.shape, lax.rem(contexts_ref[j] - base, 16)), block, 0.0)
            rows[pl.ds(j, 1), :] = jnp.sum(found, axis=0, keepdims=True)

    x, _, _ = place()
    for k, out_ref in enumerate((own_ref, one_ref, two_ref, three_ref)):
        quarter = lax.rem(x + k, XN)
        for t in range(QUARTER):
            at = pl.ds(pl.multiple_of((quarter * QUARTER + t) * 128, 128), 128)
            out_ref[t * ROWS : (t + 1) * ROWS, :] = rows[:, at].astype(BF16)


def join_kernel(own, one, two, three, _after, out_ref):
    for t in range(QUARTER):
        at = slice(t * ROWS, (t + 1) * ROWS)
        out_ref[t] = four(*(p[at, :].astype(F32) for p in (own, one, two, three))).astype(BF16)


def margin_kernel(w_ref, events_ref, _after, margin_ref, w, held, sems):
    pieces = Rows(events_ref, held, sems, [i * 128 for i in range(COUNT // 128)])
    w[...] = w_ref[...].astype(BF16).astype(F32)
    for c in range(COUNT // 128):
        pieces.take(c, 1)
        sums = []
        for r in range(c * 128, (c + 1) * 128, 16):
            total = jnp.zeros((16, 128), F32)
            for t in range(TILES):
                at = slice(t * 128, (t + 1) * 128)
                total = total + held[r : r + 16, at].astype(F32) * w[:, at]
            sums.append(total)
        turned = jnp.transpose(jnp.concatenate(sums, axis=0))
        margin_ref[c : c + 1, :] = jnp.sum(turned, axis=0, keepdims=True)


def load_kernel(events_ref, _after, held, sems):
    pieces = Rows(events_ref, held, sems, [i * 128 for i in range(COUNT // 128)])
    for i in range(COUNT // 128):
        pieces.stream.take(i)


def gradient_kernel(events_ref, own, one, two, three, labels_ref, rate_ref, grad_ref, errs):
    margin = four(own[...], one[...], two[...], three[...])
    chance = jax.nn.sigmoid(margin)
    rate = chance * (1.0 - chance)
    errors = chance - labels_ref[...].astype(F32)
    lead, rest = pair_of(errors)
    lead, rest = lead.astype(F32), rest.astype(F32)
    for i in range(COUNT // 128):
        at = slice(i * 128, (i + 1) * 128)
        rate_ref[:, at] = rate[i : i + 1]
        errs[:, at] = stacked([lead[i : i + 1], rest[i : i + 1]], 16).astype(BF16)
    for c in range(8):
        part = jnp.dot(errs[...], events_ref[:, c * 512 : (c + 1) * 512], preferred_element_type=F32)
        line = part[:1] + part[1:2]
        for u in range(4):
            grad_ref[c * 4 + u : c * 4 + u + 1, :] = line[:, u * 128 : (u + 1) * 128]


def spread_kernel(chunks_ref, grad_ref, out_ref):
    total = chunks_ref[0].astype(F32)
    for z in range(1, ZN):
        total = total + chunks_ref[z].astype(F32)
    lead, rest = pair_of(grad_ref[...])
    for z in range(ZN):
        out_ref[z, :ROWS, :] = total.astype(BF16)
        out_ref[z, ROWS : ROWS + TILES, :] = lead
        out_ref[z, ROWS + TILES :, :] = rest


def collect_kernel(in_ref, out_ref):
    grad = jnp.zeros((TILES, 128), F32)
    for z in range(ZN):
        out_ref[z * ROWS : (z + 1) * ROWS, :] = in_ref[z, :ROWS, :]
        grad = grad + (in_ref[z, ROWS : ROWS + TILES, :].astype(F32) + in_ref[z, ROWS + TILES :, :].astype(F32))
    lead, rest = pair_of(grad)
    out_ref[QUARTER * ROWS : QUARTER * ROWS + TILES, :] = lead
    out_ref[QUARTER * ROWS + TILES :, :] = rest


def halves(events_ref, core):
    starts = [half * HALF + i * 128 for half in (1 - core, core) for i in range(HALF // 128)]
    return Rows(events_ref, None, None, starts)


def put_scores(pieces, rhs, other_ref, own_ref, lines):
    for first, out_ref in ((0, other_ref), (HALF // 128, own_ref)):
        for at, size in ((0, 2), (2, 3)):
            part = jnp.dot(pieces.take(first + at, size), rhs[...], preferred_element_type=F32)
            for t in range(size):
                columns = slice((at + t) * 128, (at + t + 1) * 128)
                out_ref[:ROWS, columns] = joined(jnp.transpose(part[t * 128 : (t + 1) * 128]))
                out_ref[ROWS:, columns] = lines if at + t == 0 else jnp.zeros_like(lines)


def turned(top, rest):
    below = jnp.where(row_is(top.shape, 0), rest.astype(F32), 0.0)
    return jnp.transpose(jnp.concatenate([top, below], axis=0)).astype(BF16)


def scores_kernel(
    events_ref, w_ref, own, one, two, three, rhs_ref, grad_ref, other_ref, mine_ref, rhs
):
    x, _, core = place()
    pieces = halves(events_ref, core)
    tail = QUARTER * ROWS
    grads = [p[tail : tail + TILES, :].astype(F32) + p[tail + TILES :, :].astype(F32) for p in (own, one, two, three)]
    grad_ref[...] = four(*grads) + LAMBDA * w_ref[...]
    norms = []
    for k, part in enumerate((own, one, two, three)):
        quarter = lax.rem(x + XN - k, XN)
        norm = jnp.zeros((ROWS, 128), F32)
        for t in range(QUARTER):
            tile = quarter * QUARTER + t
            grad = grad_ref[pl.ds(tile, 1), :]
            lead, rest = pair_of(grad)
            values = part[t * ROWS : (t + 1) * ROWS, :].astype(F32)
            last = row_is(values.shape, ROWS - 1)
            exact = jnp.where(last, grad, values)
            norm = norm + exact * exact
            at = pl.ds(pl.multiple_of(tile * 128, 128), 128)
            top = jnp.where(last, lead.astype(F32), values)
            rhs_ref[:, at] = top.astype(BF16)
            rhs[at, :] = turned(top, rest)
        norms.append(norm)
    line = line_sums(four(*norms), jnp.zeros_like(norm))
    put_scores(pieces, rhs, other_ref, mine_ref, stacked([line], 8))


def pack_kernel(own, other, out_ref):
    total = own[...] + other[...]
    scores, lines = total[:ROWS], total[ROWS:]
    lead = scores.astype(BF16)
    rest = scores[ROWS - 1 :] - lead[ROWS - 1 :].astype(F32)
    out_ref[:ROWS, :] = lead
    out_ref[ROWS:, :] = stacked([rest, *triple_of(lines[:1]), *triple_of(lines[1:2])], 8).astype(BF16)


def unpacked(own, one, two, three):
    total = four(*(p[...].astype(F32) for p in (own, one, two, three)))
    first = total[65:66] + total[66:67] + total[67:68]
    second = total[68:69] + total[69:70] + total[70:71]
    return joined(total), first[:, :128], second[:, :128]


def unpack_kernel(own, one, two, three, scores_ref, norm_ref):
    scores, norm, _ = unpacked(own, one, two, three)
    scores_ref[...] = scores
    norm_ref[...] = stacked([norm], 8)


def hessian_kernel(
    events_ref, mine_ref, theirs_ref, rate_ref, own_ref, curv_ref, one_ref, two_ref, three_ref, q
):
    x, _, core = place()
    outs = ((2, two_ref), (1, one_ref), (3, three_ref), (0, own_ref))
    curv = jnp.zeros((ROWS, 128), F32)
    for half in range(2):
        at = slice(half * HALF, (half + 1) * HALF)
        scores, rate = jnp.where(core == half, mine_ref[...], theirs_ref[...]), rate_ref[:, at]
        weighted = rate * scores
        curv = curv + tile_sums(weighted * scores)
        lead = weighted.astype(BF16)
        q[:ROWS, at] = lead
        q[ROWS:, at] = stacked([weighted[ROWS - 1 :] - lead[ROWS - 1 :].astype(F32)], 16).astype(BF16)
    triple = [v.astype(F32) for v in triple_of(line_sums(curv, jnp.zeros_like(curv)))]
    curv_ref[...] = stacked(triple, 8)
    for k, out_ref in outs:
        rests = []
        for part in range(2):
            start = pl.multiple_of(lax.rem(x + k, XN) * QUARTER * 128 + part * 512, 512)
            total = joined(jnp.dot(q[...], events_ref[:, pl.ds(start, 512)], preferred_element_type=F32))
            for u in range(4):
                t = part * 4 + u
                values = total[:, u * 128 : (u + 1) * 128]
                out_ref[t * ROWS : (t + 1) * ROWS, :] = values.astype(out_ref.dtype)
                rests.append(values[ROWS - 1 :] - values[ROWS - 1 :].astype(BF16).astype(F32))
        if k:
            out_ref[QUARTER * ROWS :, :] = stacked(rests + triple, 16).astype(BF16)


def cut_kernel(own, curv_ref, one, two, three, out_ref):
    top = QUARTER * ROWS
    tails = [p[top:, :].astype(F32) for p in (one, two, three)]
    curvs = [curv_ref[0:1] + curv_ref[1:2] + curv_ref[2:3]]
    curvs += [v[QUARTER : QUARTER + 1] + v[QUARTER + 1 : QUARTER + 2] + v[QUARTER + 2 : QUARTER + 3] for v in tails]
    curv = triple_of(four(*curvs))
    for t in range(QUARTER):
        at = slice(t * ROWS, (t + 1) * ROWS)
        total = four(own[at, :], one[at, :].astype(F32), two[at, :].astype(F32), three[at, :].astype(F32))
        rest = tails[0][t : t + 1] + tails[1][t : t + 1] + tails[2][t : t + 1]
        total = total + jnp.where(row_is(total.shape, ROWS - 1), rest, 0.0)
        lead = total.astype(BF16)
        rest = total[ROWS - 1 :] - lead[ROWS - 1 :].astype(F32)
        out_ref[t, :ROWS, :] = lead
        out_ref[t, ROWS:, :] = stacked([rest, *curv], 8).astype(BF16)


def residual_kernel(in_ref, norm_ref, rhs_ref, grad_ref, out_ref, scalars_ref):
    x, z, _ = place()
    tile = x * QUARTER + z
    total = in_ref[0].astype(F32)
    for z in range(1, ZN):
        total = total + in_ref[z].astype(F32)
    curv = total[65:66] + total[66:67] + total[67:68]
    norm = norm_ref[:1]
    step = norm / (curv + LAMBDA * norm)
    square = (ROWS, 128)
    eye = lax.broadcasted_iota(jnp.int32, square, 0) == lax.broadcasted_iota(jnp.int32, square, 1)
    column = jnp.sum(jnp.where(eye, step, 0.0), axis=1, keepdims=True)
    right = rhs_ref[:, pl.ds(pl.multiple_of(tile * 128, 128), 128)].astype(F32)
    right = jnp.where(row_is(square, ROWS - 1), grad_ref[pl.ds(tile, 1), :], right)
    residual = right - column * (joined(total) + LAMBDA * right)
    lead = residual.astype(BF16)
    rest = stacked([residual[ROWS - 1 :] - lead[ROWS - 1 :].astype(F32)], 8).astype(BF16)
    for z in range(ZN):
        out_ref[z, :ROWS, :] = lead
        out_ref[z, ROWS:, :] = rest
    scalars_ref[...] = stacked([step, curv, norm], 8)


def repack_kernel(in_ref, out_ref):
    rests = []
    for t in range(QUARTER):
        rows = in_ref[t]
        out_ref[t * ROWS : (t + 1) * ROWS, :] = rows[:ROWS]
        rests.append(rows[ROWS:].astype(F32)[:1])
    out_ref[QUARTER * ROWS :, :] = stacked(rests, 16).astype(BF16)


def quarter_work(k, events_ref, rhs_ref, grad_ref, part, first_ref, res):
    x, _, _ = place()
    quarter = lax.rem(x + XN - k, XN)
    norm = jnp.zeros((ROWS, 128), F32)
    cross = jnp.zeros((ROWS, 128), F32)
    rests = part[QUARTER * ROWS :, :].astype(F32)
    for t in range(QUARTER):
        tile = quarter * QUARTER + t
        at = pl.ds(pl.multiple_of(tile * 128, 128), 128)
        top, rest = part[t * ROWS : (t + 1) * ROWS, :].astype(F32), rests[t : t + 1]
        last = row_is(top.shape, ROWS - 1)
        values = top + jnp.where(last, rest, 0.0)
        right = jnp.where(last, grad_ref[pl.ds(tile, 1), :], rhs_ref[:, at].astype(F32))
        norm = norm + values * values
        cross = cross + values * right
        first_ref[t : t + 1, :] = values[ROWS - 1 :]
        res[t * 128 : (t + 1) * 128, :] = turned(top, rest)
    columns = pl.ds(pl.multiple_of(quarter * QUARTER * 128, 1024), QUARTER * 128)
    scores = jnp.dot(events_ref[:, columns], res[...], preferred_element_type=F32)
    return scores, jnp.concatenate([norm, cross], axis=0)


def open_kernel(events_ref, rhs_ref, grad_ref, part, total_ref, sums_ref, first_ref, res):
    total_ref[...], sums_ref[...] = quarter_work(0, events_ref, rhs_ref, grad_ref, part, first_ref, res)


def add_kernel(k, events_ref, rhs_ref, grad_ref, part, total, total_ref, sums_ref, first_ref, res):
    scores, sums_ref[...] = quarter_work(k, events_ref, rhs_ref, grad_ref, part, first_ref, res)
    total_ref[...] = total[...] + scores


def close_kernel(
    events_ref, rhs_ref, grad_ref, part, total, own, two, three, other_ref, mine_ref, first_ref, res, scores_ref
):
    scores, one = quarter_work(1, events_ref, rhs_ref, grad_ref, part, first_ref, res)
    scores_ref[...] = total[...] + scores
    sums = four(own[...], one, two[...], three[...])
    line = line_sums(sums[:ROWS], sums[ROWS:])
    lines = stacked([line, pltpu.roll(line, ROWS, 1)], 8)
    core = place()[2]
    for half, out_ref in ((1 - core, other_ref), (core, mine_ref)):
        for t in range(HALF // 128):
            rows = scores_ref[pl.ds(pl.multiple_of(half * HALF + t * 128, 128), 128), :]
            columns = slice(t * 128, (t + 1) * 128)
            out_ref[:ROWS, columns] = joined(jnp.transpose(rows))
            out_ref[ROWS:, columns] = lines if t == 0 else jnp.zeros_like(lines)


def tail_kernel(own, one, two, three, scores_ref, rate_ref, tail_ref, lines_ref):
    scores, norm, cross = unpacked(own, one, two, three)
    rate = jnp.where(place()[2] == 0, rate_ref[:, :HALF], rate_ref[:, HALF:])
    weighted = rate * scores
    tail_ref[...] = line_sums(tile_sums(weighted * scores_ref[...]), tile_sums(weighted * scores))
    lines_ref[...] = stacked([norm, cross], 8)


def end_kernel(
    tails_ref, scalars_ref, lines_ref, w_ref, grad_ref, own, one, two, three, weights_ref, widths_ref
):
    tail = tails_ref[0]
    for e in range(1, EN):
        tail = tail + tails_ref[e]
    mixed, square = tail, pltpu.roll(tail, ROWS, 1)
    step_one, curv, norm = scalars_ref[0:1], scalars_ref[1:2], scalars_ref[2:3]
    norm_next, cross = lines_ref[0:1], lines_ref[1:2]
    ratio = norm_next / norm
    curvature = square + 2.0 * ratio * mixed + ratio * ratio * curv
    curvature = curvature + LAMBDA * (norm_next + 2.0 * ratio * cross + ratio * ratio * norm)
    step_two = norm_next / curvature
    widths = step_one * norm + step_two * (cross + ratio * norm)
    widths_ref[...] = widths[:, : ROWS - 1]
    at = slice(ROWS - 1, ROWS)
    x, _, _ = place()
    for k, first in enumerate((own, one, two, three)):
        rows = pl.ds(pl.multiple_of(lax.rem(x + XN - k, XN) * QUARTER, QUARTER), QUARTER)
        grad = grad_ref[rows, :]
        step = step_one[:, at] * grad + step_two[:, at] * (first[...] + ratio[:, at] * grad)
        weights_ref[rows, :] = w_ref[rows, :] - step


def on_device(events, labels, weights, contexts):
    features = TILES * 128
    tiled = weights.reshape(TILES, 128)

    whole = shaped(COUNT, features, dtype=BF16)
    sems = pltpu.SemaphoreType.DMA((10,))

    own, *picked = kernel_call(
        pick_kernel,
        [SMEM, HBM],
        [shaped(QUARTER * ROWS, 128, dtype=BF16)] * 4,
        (contexts, events),
        [
            pltpu.VMEM((ROWS - 1, 16, features), BF16),
            pltpu.VMEM((ROWS, features), F32),
            pltpu.SemaphoreType.DMA((ROWS - 1,)),
        ],
        micros=2,
        room=ROOM,
    )
    picked = x_scatter(*picked)
    (margin,) = kernel_call(
        margin_kernel,
        [VMEM, HBM, HBM],
        [shaped(COUNT // 128, 128)],
        (weights.reshape(1, features), events, own),
        [pltpu.VMEM((1, features), F32), pltpu.VMEM((COUNT, features), BF16), sems],
        micros=4,
        room=ROOM,
    )

    margin = margin + core_move(margin)
    (chunks,) = kernel_call(
        join_kernel, [VMEM] * 4 + [HBM], [shaped(ZN, ROWS, 128, dtype=BF16)], (own, *picked, margin)
    )
    (held,) = kernel_call(load_kernel, [HBM, HBM], [whole], (events, chunks), [sems], micros=5, room=40)
    chunks = z_exchange(chunks)
    rate, grad = kernel_call(
        gradient_kernel,
        [VMEM] * 6,
        [shaped(1, COUNT), shaped(TILES, 128)],
        (held, margin, *y_moves(margin), labels.reshape(COUNT // 128, 128)),
        [pltpu.VMEM((16, COUNT), BF16)],
        micros=4,
        room=8,
    )
    (message,) = kernel_call(
        spread_kernel, [VMEM] * 2, [shaped(ZN, ROWS + 2 * TILES, 128, dtype=BF16)], (chunks, grad)
    )
    message = z_exchange(message)
    (message,) = kernel_call(
        collect_kernel, [VMEM], [shaped(QUARTER * ROWS + 2 * TILES, 128, dtype=BF16)], (message,)
    )

    moved = x_moves(message)
    (held,) = kernel_call(load_kernel, [HBM, HBM], [whole], (events, message), [sems], micros=5, room=40)

    half = [shaped(ROWS + 8, HALF), shaped(ROWS + 8, HALF)]
    rhs, grad, other, mine = kernel_call(
        scores_kernel,
        [VMEM] * 6,
        [shaped(ROWS, features, dtype=BF16), shaped(TILES, 128)] + half,
        (held, tiled, message, *moved),
        [pltpu.VMEM((features, 128), BF16)],
        micros=3,
        room=8,
    )
    packed = [shaped(ROWS + 8, HALF, dtype=BF16)]
    (message,) = kernel_call(pack_kernel, [VMEM] * 2, packed, (mine, core_move(other)))
    scores, norm = kernel_call(
        unpack_kernel, [VMEM] * 4, [shaped(ROWS, HALF), shaped(8, 128)], (message, *y_moves(message))
    )

    part = shaped(QUARTER * ROWS + 16, 128, dtype=BF16)
    own, curv, one, two, three = kernel_call(
        hessian_kernel,
        [VMEM] * 4,
        [shaped(QUARTER * ROWS, 128), shaped(8, 128), part, part, part],
        (held, scores, core_move(scores), rate),
        [pltpu.VMEM((ROWS + 16, COUNT), BF16)],
        micros=4,
        room=8,
    )
    moved = x_scatter(one, two, three)
    shard = [shaped(ZN, ROWS + 8, 128, dtype=BF16)]
    (message,) = kernel_call(cut_kernel, [VMEM] * 5, shard, (own, curv, *moved))
    message, scalars = kernel_call(
        residual_kernel,
        [VMEM] * 4,
        shard + [shaped(8, 128)],
        (z_exchange(message), norm, rhs, grad),
    )
    message = z_exchange(message)

    (message,) = kernel_call(repack_kernel, [VMEM], [part], (message,))
    one, two, three = x_moves(message)
    sums = [shaped(COUNT, 128), shaped(128, 128)]
    first = [shaped(QUARTER, 128)]
    scratch = [pltpu.VMEM((QUARTER * 128, 128), BF16)]
    total, sum_own, first_own = kernel_call(
        open_kernel, [VMEM] * 4, sums + first, (held, rhs, grad, message), scratch, micros=1, room=8
    )
    total, sum_three, first_three = kernel_call(
        functools.partial(add_kernel, 3),
        [VMEM] * 5,
        sums + first,
        (held, rhs, grad, three, total),
        scratch,
        micros=1,
        room=8,
    )
    total, sum_two, first_two = kernel_call(
        functools.partial(add_kernel, 2),
        [VMEM] * 5,
        sums + first,
        (held, rhs, grad, two, total),
        scratch,
        micros=1,
        room=8,
    )
    other, mine, first_one = kernel_call(
        close_kernel,
        [VMEM] * 8,
        half + first,
        (held, rhs, grad, one, total, sum_own, sum_two, sum_three),
        scratch + [pltpu.VMEM((COUNT, 128), F32)],
        micros=1,
        room=8,
    )
    (message,) = kernel_call(pack_kernel, [VMEM] * 2, packed, (mine, core_move(other)))
    tail, lines = kernel_call(
        tail_kernel,
        [VMEM] * 6,
        [shaped(1, 128), shaped(8, 128)],
        (message, *y_moves(message), scores, rate),
    )
    tail = tail + core_move(tail)
    tails = lax.all_to_all(jnp.broadcast_to(tail[None], (EN, 1, 128)), "event", 0, 0)
    updated, widths = kernel_call(
        end_kernel, [VMEM] * 9, [shaped(TILES, 128), shaped(1, ROWS - 1)], (tails, scalars, lines, tiled, grad, first_own, first_one, first_two, first_three)
    )
    return updated.reshape(features), widths.reshape(ROWS - 1)


def solution(mesh):
    in_specs = (P("event", "feat"), P("event"), P("feat"), P())
    out_specs = (P("feat"), P())
    return jax.shard_map(on_device, mesh=mesh, in_specs=in_specs, out_specs=out_specs, check_vma=False)
```

```python
import jax
import jax.numpy as jnp
from jax import lax
from jax.experimental import pallas as pl
from jax.experimental.pallas import tpu as pltpu
from jax.sharding import PartitionSpec as P

LAMBDA = 0.5
XN, ZN, YN, CN = 4, 8, 4, 2
EN = XN * ZN
ROWS = 64
TILES = 32
QUARTER = TILES // XN
COUNT = 1280
HALF = COUNT // 2
WINDOW = 10
ROOM = 48
F32, BF16 = jnp.float32, jnp.bfloat16
VMEM = pl.BlockSpec(memory_space=pltpu.VMEM)
SMEM = pl.BlockSpec(memory_space=pltpu.SMEM)
HBM = pl.BlockSpec(memory_space=pltpu.HBM)
ACROSS = (((1,), (1,)), ((), ()))


def shaped(*shape, dtype=F32):
    return jax.ShapeDtypeStruct(shape, dtype)


def kernel_call(body, ins, outs, args, scratch=(), micros=0.5, room=8):
    return pl.pallas_call(
        body,
        out_shape=outs,
        in_specs=ins,
        out_specs=[VMEM] * len(outs),
        scratch_shapes=list(scratch),
        compiler_params=pltpu.CompilerParams(vmem_limit_bytes=room << 20),
        cost_estimate=pl.CostEstimate(flops=0, bytes_accessed=int(micros * 3.6e6), transcendentals=0),
    )(*args)


def x_moves(v):
    n = XN * ZN
    return [lax.ppermute(v, "event", [(i, (i + k * ZN) % n) for i in range(n)]) for k in (1, 2, 3)]


def y_moves(v):
    n = YN * CN
    return [lax.ppermute(v, "feat", [(i, (i + k * CN) % n) for i in range(n)]) for k in (1, 2, 3)]


def core_move(v):
    return lax.ppermute(v, "feat", [(i, i ^ 1) for i in range(YN * CN)])


def z_exchange(v):
    groups = [[x * ZN + z for z in range(ZN)] for x in range(XN)]
    return lax.all_to_all(v, "event", 0, 0, axis_index_groups=groups)


def four(own, one, two, three):
    return (own + two) + (one + three)


def pair_of(v):
    lead = v.astype(BF16)
    return lead, (v - lead.astype(F32)).astype(BF16)


def triple_of(v):
    lead, rest = v.astype(BF16), v
    rest = v - lead.astype(F32)
    mid = rest.astype(BF16)
    return lead, mid, (rest - mid.astype(F32)).astype(BF16)


def row_is(shape, i):
    return lax.broadcasted_iota(jnp.int32, shape, 0) == i


def stacked(lines, rows):
    out = jnp.zeros((rows, lines[0].shape[1]), F32)
    for i, line in enumerate(lines):
        out = jnp.where(row_is(out.shape, i), line.astype(F32), out)
    return out


def joined(v):
    top = v[:ROWS]
    return top + jnp.where(row_is(top.shape, ROWS - 1), v[ROWS : ROWS + 1], 0.0)


def line_sums(top, bottom):
    return jnp.sum(jnp.transpose(jnp.concatenate([top, bottom], axis=0)), axis=0, keepdims=True)


def tile_sums(v):
    total = v[:, :128]
    for t in range(1, v.shape[1] // 128):
        total = total + v[:, t * 128 : (t + 1) * 128]
    return total


class Stream:
    def __init__(self, pieces, sems):
        self.copies = [pltpu.make_async_copy(source, target, sems.at[i]) for i, (source, target) in enumerate(pieces)]
        for copy in self.copies[:WINDOW]:
            copy.start()

    def take(self, i):
        self.copies[i].wait()
        if i + WINDOW < len(self.copies):
            self.copies[i + WINDOW].start()


class Rows:
    def __init__(self, events_ref, held, sems, starts):
        self.events, self.held = events_ref, held
        self.starts = [pl.multiple_of(start, 128) for start in starts]
        if held is not None:
            pieces = [
                (events_ref.at[pl.ds(start, 128), :], held.at[pl.ds(i * 128, 128), :])
                for i, start in enumerate(self.starts)
            ]
            self.stream = Stream(pieces, sems)

    def take(self, first, count):
        if self.held is None:
            return self.events[pl.ds(self.starts[first], count * 128), :]
        for i in range(count):
            self.stream.take(first + i)
        return self.held[first * 128 : (first + count) * 128, :]


def place():
    event = lax.axis_index("event")
    return lax.div(event, ZN), lax.rem(event, ZN), lax.rem(lax.axis_index("feat"), CN)


def pick_kernel(contexts_ref, events_ref, out_ref, blocks, rows, sems):
    base = lax.axis_index("event") * COUNT

    def owned(j):
        return jnp.logical_and(contexts_ref[j] >= base, contexts_ref[j] < base + COUNT)

    def fetch(j):
        start = pl.multiple_of(lax.div(contexts_ref[j] - base, 16) * 16, 16)
        return pltpu.make_async_copy(events_ref.at[pl.ds(start, 16), :], blocks.at[j], sems.at[j])

    @pl.loop(0, ROWS - 1, unroll=9)
    def _(j):
        @pl.when(owned(j))
        def _():
            fetch(j).start()

    rows[...] = jnp.zeros_like(rows)

    @pl.loop(0, ROWS - 1, unroll=9)
    def _(j):
        @pl.when(owned(j))
        def _():
            fetch(j).wait()
            block = blocks[j].astype(F32)
            found = jnp.where(row_is(block.shape, lax.rem(contexts_ref[j] - base, 16)), block, 0.0)
            rows[pl.ds(j, 1), :] = jnp.sum(found, axis=0, keepdims=True)

    for t in range(TILES):
        out_ref[t] = rows[:, t * 128 : (t + 1) * 128].astype(BF16)


def margin_kernel(w_ref, events_ref, _after, margin_ref, held, w, sems):
    pieces = Rows(events_ref, held, sems, [i * 128 for i in range(COUNT // 128)])
    w[...] = w_ref[...].astype(BF16).astype(F32)
    for c in range(COUNT // 128):
        pieces.take(c, 1)
        sums = []
        for r in range(c * 128, (c + 1) * 128, 16):
            total = jnp.zeros((16, 128), F32)
            for t in range(TILES):
                at = slice(t * 128, (t + 1) * 128)
                total = total + held[r : r + 16, at].astype(F32) * w[:, at]
            sums.append(total)
        turned = jnp.transpose(jnp.concatenate(sums, axis=0))
        margin_ref[c : c + 1, :] = jnp.sum(turned, axis=0, keepdims=True)


def load_kernel(events_ref, _after, held, sems):
    pieces = Rows(events_ref, held, sems, [i * 128 for i in range(COUNT // 128)])
    for i in range(COUNT // 128):
        pieces.stream.take(i)


def gradient_kernel(events_ref, own, one, two, three, labels_ref, rate_ref, grad_ref, errs):
    margin = four(own[...], one[...], two[...], three[...])
    chance = jax.nn.sigmoid(margin)
    rate = chance * (1.0 - chance)
    errors = chance - labels_ref[...].astype(F32)
    lead, rest = pair_of(errors)
    lead, rest = lead.astype(F32), rest.astype(F32)
    for i in range(COUNT // 128):
        at = slice(i * 128, (i + 1) * 128)
        rate_ref[:, at] = rate[i : i + 1]
        errs[:, at] = stacked([lead[i : i + 1], rest[i : i + 1]], 16).astype(BF16)
    for c in range(8):
        part = jnp.dot(errs[...], events_ref[:, c * 512 : (c + 1) * 512], preferred_element_type=F32)
        line = part[:1] + part[1:2]
        for u in range(4):
            grad_ref[c * 4 + u : c * 4 + u + 1, :] = line[:, u * 128 : (u + 1) * 128]


def spread_kernel(chunks_ref, grad_ref, out_ref):
    total = chunks_ref[0].astype(F32)
    for e in range(1, EN):
        total = total + chunks_ref[e].astype(F32)
    lead, rest = pair_of(grad_ref[...])
    for z in range(ZN):
        out_ref[z, :ROWS, :] = total.astype(BF16)
        out_ref[z, ROWS : ROWS + TILES, :] = lead
        out_ref[z, ROWS + TILES :, :] = rest


def collect_kernel(in_ref, out_ref):
    grad = jnp.zeros((TILES, 128), F32)
    for z in range(ZN):
        out_ref[z * ROWS : (z + 1) * ROWS, :] = in_ref[z, :ROWS, :]
        grad = grad + (in_ref[z, ROWS : ROWS + TILES, :].astype(F32) + in_ref[z, ROWS + TILES :, :].astype(F32))
    lead, rest = pair_of(grad)
    out_ref[QUARTER * ROWS : QUARTER * ROWS + TILES, :] = lead
    out_ref[QUARTER * ROWS + TILES :, :] = rest


def halves(events_ref, core):
    starts = [half * HALF + i * 128 for half in (1 - core, core) for i in range(HALF // 128)]
    return Rows(events_ref, None, None, starts)


def put_scores(pieces, rhs, other_ref, own_ref, lines):
    for first, out_ref in ((0, other_ref), (HALF // 128, own_ref)):
        for at, size in ((0, 2), (2, 3)):
            part = jnp.dot(pieces.take(first + at, size), rhs[...], preferred_element_type=F32)
            for t in range(size):
                columns = slice((at + t) * 128, (at + t + 1) * 128)
                out_ref[:ROWS, columns] = joined(jnp.transpose(part[t * 128 : (t + 1) * 128]))
                out_ref[ROWS:, columns] = lines if at + t == 0 else jnp.zeros_like(lines)


def turned(top, rest):
    below = jnp.where(row_is(top.shape, 0), rest.astype(F32), 0.0)
    return jnp.transpose(jnp.concatenate([top, below], axis=0)).astype(BF16)


def scores_kernel(
    events_ref, w_ref, own, one, two, three, rhs_ref, grad_ref, other_ref, mine_ref, rhs
):
    x, _, core = place()
    pieces = halves(events_ref, core)
    tail = QUARTER * ROWS
    grads = [p[tail : tail + TILES, :].astype(F32) + p[tail + TILES :, :].astype(F32) for p in (own, one, two, three)]
    grad_ref[...] = four(*grads) + LAMBDA * w_ref[...]
    norms = []
    for k, part in enumerate((own, one, two, three)):
        quarter = lax.rem(x + XN - k, XN)
        norm = jnp.zeros((ROWS, 128), F32)
        for t in range(QUARTER):
            tile = quarter * QUARTER + t
            grad = grad_ref[pl.ds(tile, 1), :]
            lead, rest = pair_of(grad)
            values = part[t * ROWS : (t + 1) * ROWS, :].astype(F32)
            last = row_is(values.shape, ROWS - 1)
            exact = jnp.where(last, grad, values)
            norm = norm + exact * exact
            at = pl.ds(pl.multiple_of(tile * 128, 128), 128)
            top = jnp.where(last, lead.astype(F32), values)
            rhs_ref[:, at] = top.astype(BF16)
            rhs[at, :] = turned(top, rest)
        norms.append(norm)
    line = line_sums(four(*norms), jnp.zeros_like(norm))
    put_scores(pieces, rhs, other_ref, mine_ref, stacked([line], 8))


def pack_kernel(own, other, out_ref):
    total = own[...] + other[...]
    scores, lines = total[:ROWS], total[ROWS:]
    lead = scores.astype(BF16)
    rest = scores[ROWS - 1 :] - lead[ROWS - 1 :].astype(F32)
    out_ref[:ROWS, :] = lead
    out_ref[ROWS:, :] = stacked([rest, *triple_of(lines[:1]), *triple_of(lines[1:2])], 8).astype(BF16)


def unpacked(own, one, two, three):
    total = four(*(p[...].astype(F32) for p in (own, one, two, three)))
    first = total[65:66] + total[66:67] + total[67:68]
    second = total[68:69] + total[69:70] + total[70:71]
    return joined(total), first[:, :128], second[:, :128]


def unpack_kernel(own, one, two, three, scores_ref, norm_ref):
    scores, norm, _ = unpacked(own, one, two, three)
    scores_ref[...] = scores
    norm_ref[...] = stacked([norm], 8)


def hessian_kernel(
    events_ref, mine_ref, theirs_ref, rate_ref, own_ref, curv_ref, one_ref, two_ref, three_ref, q
):
    x, _, core = place()
    outs = ((2, two_ref), (1, one_ref), (3, three_ref), (0, own_ref))
    curv = jnp.zeros((ROWS, 128), F32)
    for half in range(2):
        at = slice(half * HALF, (half + 1) * HALF)
        scores, rate = jnp.where(core == half, mine_ref[...], theirs_ref[...]), rate_ref[:, at]
        weighted = rate * scores
        curv = curv + tile_sums(weighted * scores)
        lead = weighted.astype(BF16)
        q[:ROWS, at] = lead
        q[ROWS:, at] = stacked([weighted[ROWS - 1 :] - lead[ROWS - 1 :].astype(F32)], 16).astype(BF16)
    triple = [v.astype(F32) for v in triple_of(line_sums(curv, jnp.zeros_like(curv)))]
    curv_ref[...] = stacked(triple, 8)
    for k, out_ref in outs:
        rests = []
        for part in range(2):
            start = pl.multiple_of(lax.rem(x + k, XN) * QUARTER * 128 + part * 512, 512)
            total = joined(jnp.dot(q[...], events_ref[:, pl.ds(start, 512)], preferred_element_type=F32))
            for u in range(4):
                t = part * 4 + u
                values = total[:, u * 128 : (u + 1) * 128]
                out_ref[t * ROWS : (t + 1) * ROWS, :] = values.astype(out_ref.dtype)
                rests.append(values[ROWS - 1 :] - values[ROWS - 1 :].astype(BF16).astype(F32))
        if k:
            out_ref[QUARTER * ROWS :, :] = stacked(rests + triple, 16).astype(BF16)


def cut_kernel(own, curv_ref, one, two, three, out_ref):
    top = QUARTER * ROWS
    tails = [p[top:, :].astype(F32) for p in (one, two, three)]
    curvs = [curv_ref[0:1] + curv_ref[1:2] + curv_ref[2:3]]
    curvs += [v[QUARTER : QUARTER + 1] + v[QUARTER + 1 : QUARTER + 2] + v[QUARTER + 2 : QUARTER + 3] for v in tails]
    curv = triple_of(four(*curvs))
    for t in range(QUARTER):
        at = slice(t * ROWS, (t + 1) * ROWS)
        total = four(own[at, :], one[at, :].astype(F32), two[at, :].astype(F32), three[at, :].astype(F32))
        rest = tails[0][t : t + 1] + tails[1][t : t + 1] + tails[2][t : t + 1]
        total = total + jnp.where(row_is(total.shape, ROWS - 1), rest, 0.0)
        lead = total.astype(BF16)
        rest = total[ROWS - 1 :] - lead[ROWS - 1 :].astype(F32)
        out_ref[t, :ROWS, :] = lead
        out_ref[t, ROWS:, :] = stacked([rest, *curv], 8).astype(BF16)


def residual_kernel(in_ref, norm_ref, rhs_ref, grad_ref, out_ref, scalars_ref):
    x, z, _ = place()
    tile = x * QUARTER + z
    total = in_ref[0].astype(F32)
    for z in range(1, ZN):
        total = total + in_ref[z].astype(F32)
    curv = total[65:66] + total[66:67] + total[67:68]
    norm = norm_ref[:1]
    step = norm / (curv + LAMBDA * norm)
    square = (ROWS, 128)
    eye = lax.broadcasted_iota(jnp.int32, square, 0) == lax.broadcasted_iota(jnp.int32, square, 1)
    column = jnp.sum(jnp.where(eye, step, 0.0), axis=1, keepdims=True)
    right = rhs_ref[:, pl.ds(pl.multiple_of(tile * 128, 128), 128)].astype(F32)
    right = jnp.where(row_is(square, ROWS - 1), grad_ref[pl.ds(tile, 1), :], right)
    residual = right - column * (joined(total) + LAMBDA * right)
    lead = residual.astype(BF16)
    rest = stacked([residual[ROWS - 1 :] - lead[ROWS - 1 :].astype(F32)], 8).astype(BF16)
    for z in range(ZN):
        out_ref[z, :ROWS, :] = lead
        out_ref[z, ROWS:, :] = rest
    scalars_ref[...] = stacked([step, curv, norm], 8)


def repack_kernel(in_ref, out_ref):
    rests = []
    for t in range(QUARTER):
        rows = in_ref[t]
        out_ref[t * ROWS : (t + 1) * ROWS, :] = rows[:ROWS]
        rests.append(rows[ROWS:].astype(F32)[:1])
    out_ref[QUARTER * ROWS :, :] = stacked(rests, 16).astype(BF16)


def quarter_work(k, events_ref, rhs_ref, grad_ref, part, first_ref, res):
    x, _, _ = place()
    quarter = lax.rem(x + XN - k, XN)
    norm = jnp.zeros((ROWS, 128), F32)
    cross = jnp.zeros((ROWS, 128), F32)
    rests = part[QUARTER * ROWS :, :].astype(F32)
    for t in range(QUARTER):
        tile = quarter * QUARTER + t
        at = pl.ds(pl.multiple_of(tile * 128, 128), 128)
        top, rest = part[t * ROWS : (t + 1) * ROWS, :].astype(F32), rests[t : t + 1]
        last = row_is(top.shape, ROWS - 1)
        values = top + jnp.where(last, rest, 0.0)
        right = jnp.where(last, grad_ref[pl.ds(tile, 1), :], rhs_ref[:, at].astype(F32))
        norm = norm + values * values
        cross = cross + values * right
        first_ref[t : t + 1, :] = values[ROWS - 1 :]
        res[t * 128 : (t + 1) * 128, :] = turned(top, rest)
    columns = pl.ds(pl.multiple_of(quarter * QUARTER * 128, 1024), QUARTER * 128)
    scores = jnp.dot(events_ref[:, columns], res[...], preferred_element_type=F32)
    return scores, jnp.concatenate([norm, cross], axis=0)


def open_kernel(events_ref, rhs_ref, grad_ref, part, total_ref, sums_ref, first_ref, res):
    total_ref[...], sums_ref[...] = quarter_work(0, events_ref, rhs_ref, grad_ref, part, first_ref, res)


def close_kernel(
    events_ref, rhs_ref, grad_ref, one, two, three, total, own, other_ref, mine_ref, f1, f2, f3, res, scores_ref
):
    scores, sums = total[...], [own[...]]
    for k, part, first_ref in ((1, one, f1), (2, two, f2), (3, three, f3)):
        more, sum_k = quarter_work(k, events_ref, rhs_ref, grad_ref, part, first_ref, res.at[k - 1])
        scores = scores + more
        sums.append(sum_k)
    scores_ref[...] = scores
    sums = four(*sums)
    line = line_sums(sums[:ROWS], sums[ROWS:])
    lines = stacked([line, pltpu.roll(line, ROWS, 1)], 8)
    core = place()[2]
    for half, out_ref in ((1 - core, other_ref), (core, mine_ref)):
        for t in range(HALF // 128):
            rows = scores_ref[pl.ds(pl.multiple_of(half * HALF + t * 128, 128), 128), :]
            columns = slice(t * 128, (t + 1) * 128)
            out_ref[:ROWS, columns] = joined(jnp.transpose(rows))
            out_ref[ROWS:, columns] = lines if t == 0 else jnp.zeros_like(lines)


def tail_kernel(own, one, two, three, scores_ref, rate_ref, tail_ref, lines_ref):
    scores, norm, cross = unpacked(own, one, two, three)
    rate = jnp.where(place()[2] == 0, rate_ref[:, :HALF], rate_ref[:, HALF:])
    weighted = rate * scores
    tail_ref[...] = line_sums(tile_sums(weighted * scores_ref[...]), tile_sums(weighted * scores))
    lines_ref[...] = stacked([norm, cross], 8)


def end_kernel(
    tails_ref, scalars_ref, lines_ref, w_ref, grad_ref, own, one, two, three, weights_ref, widths_ref
):
    tail = tails_ref[0]
    for e in range(1, EN):
        tail = tail + tails_ref[e]
    mixed, square = tail, pltpu.roll(tail, ROWS, 1)
    step_one, curv, norm = scalars_ref[0:1], scalars_ref[1:2], scalars_ref[2:3]
    norm_next, cross = lines_ref[0:1], lines_ref[1:2]
    ratio = norm_next / norm
    curvature = square + 2.0 * ratio * mixed + ratio * ratio * curv
    curvature = curvature + LAMBDA * (norm_next + 2.0 * ratio * cross + ratio * ratio * norm)
    step_two = norm_next / curvature
    widths = step_one * norm + step_two * (cross + ratio * norm)
    widths_ref[...] = widths[:, : ROWS - 1]
    at = slice(ROWS - 1, ROWS)
    x, _, _ = place()
    for k, first in enumerate((own, one, two, three)):
        rows = pl.ds(pl.multiple_of(lax.rem(x + XN - k, XN) * QUARTER, QUARTER), QUARTER)
        grad = grad_ref[rows, :]
        step = step_one[:, at] * grad + step_two[:, at] * (first[...] + ratio[:, at] * grad)
        weights_ref[rows, :] = w_ref[rows, :] - step


def on_device(events, labels, weights, contexts):
    features = TILES * 128
    tiled = weights.reshape(TILES, 128)

    whole = shaped(COUNT, features, dtype=BF16)
    sems = pltpu.SemaphoreType.DMA((10,))

    (picked,) = kernel_call(
        pick_kernel,
        [SMEM, HBM],
        [shaped(TILES, ROWS, 128, dtype=BF16)],
        (contexts, events),
        [
            pltpu.VMEM((ROWS - 1, 16, features), BF16),
            pltpu.VMEM((ROWS, features), F32),
            pltpu.SemaphoreType.DMA((ROWS - 1,)),
        ],
        micros=2,
        room=ROOM,
    )
    chunks = lax.all_to_all(picked, "event", 0, 0)
    margin, held = kernel_call(
        margin_kernel,
        [VMEM, HBM, HBM],
        [shaped(COUNT // 128, 128), whole],
        (weights.reshape(1, features), events, picked),
        [pltpu.VMEM((1, features), F32), sems],
        micros=4,
        room=40,
    )

    margin = margin + core_move(margin)
    rate, grad = kernel_call(
        gradient_kernel,
        [VMEM] * 6,
        [shaped(1, COUNT), shaped(TILES, 128)],
        (held, margin, *y_moves(margin), labels.reshape(COUNT // 128, 128)),
        [pltpu.VMEM((16, COUNT), BF16)],
        micros=4,
        room=8,
    )
    (message,) = kernel_call(
        spread_kernel, [VMEM] * 2, [shaped(ZN, ROWS + 2 * TILES, 128, dtype=BF16)], (chunks, grad)
    )
    message = z_exchange(message)
    (message,) = kernel_call(
        collect_kernel, [VMEM], [shaped(QUARTER * ROWS + 2 * TILES, 128, dtype=BF16)], (message,)
    )

    moved = x_moves(message)
    (held,) = kernel_call(load_kernel, [HBM, HBM], [whole], (events, message), [sems], micros=5, room=40)

    half = [shaped(ROWS + 8, HALF), shaped(ROWS + 8, HALF)]
    rhs, grad, other, mine = kernel_call(
        scores_kernel,
        [VMEM] * 6,
        [shaped(ROWS, features, dtype=BF16), shaped(TILES, 128)] + half,
        (held, tiled, message, *moved),
        [pltpu.VMEM((features, 128), BF16)],
        micros=3,
        room=8,
    )
    packed = [shaped(ROWS + 8, HALF, dtype=BF16)]
    (message,) = kernel_call(pack_kernel, [VMEM] * 2, packed, (mine, core_move(other)))
    scores, norm = kernel_call(
        unpack_kernel, [VMEM] * 4, [shaped(ROWS, HALF), shaped(8, 128)], (message, *y_moves(message))
    )

    part = shaped(QUARTER * ROWS + 16, 128, dtype=BF16)
    own, curv, one, two, three = kernel_call(
        hessian_kernel,
        [VMEM] * 4,
        [shaped(QUARTER * ROWS, 128), shaped(8, 128), part, part, part],
        (held, scores, core_move(scores), rate),
        [pltpu.VMEM((ROWS + 16, COUNT), BF16)],
        micros=4,
        room=8,
    )
    moved = [
        lax.ppermute(v, "event", [(i, (i + k * ZN) % EN) for i in range(EN)])
        for k, v in ((1, one), (2, two), (3, three))
    ]
    shard = [shaped(ZN, ROWS + 8, 128, dtype=BF16)]
    (message,) = kernel_call(cut_kernel, [VMEM] * 5, shard, (own, curv, *moved))
    message, scalars = kernel_call(
        residual_kernel,
        [VMEM] * 4,
        shard + [shaped(8, 128)],
        (z_exchange(message), norm, rhs, grad),
    )
    message = z_exchange(message)

    (message,) = kernel_call(repack_kernel, [VMEM], [part], (message,))
    one, two, three = x_moves(message)
    sums = [shaped(COUNT, 128), shaped(128, 128)]
    first = [shaped(QUARTER, 128)]
    scratch = [pltpu.VMEM((QUARTER * 128, 128), BF16)]
    total, sum_own, first_own = kernel_call(
        open_kernel, [VMEM] * 4, sums + first, (held, rhs, grad, message), scratch, micros=1, room=8
    )
    other, mine, first_one, first_two, first_three = kernel_call(
        close_kernel,
        [VMEM] * 8,
        half + first * 3,
        (held, rhs, grad, one, two, three, total, sum_own),
        [pltpu.VMEM((3, QUARTER * 128, 128), BF16), pltpu.VMEM((COUNT, 128), F32)],
        micros=2,
        room=8,
    )
    (message,) = kernel_call(pack_kernel, [VMEM] * 2, packed, (mine, core_move(other)))
    tail, lines = kernel_call(
        tail_kernel,
        [VMEM] * 6,
        [shaped(1, 128), shaped(8, 128)],
        (message, *y_moves(message), scores, rate),
    )
    tail = tail + core_move(tail)
    tails = lax.all_to_all(jnp.broadcast_to(tail[None], (EN, 1, 128)), "event", 0, 0)
    updated, widths = kernel_call(
        end_kernel, [VMEM] * 9, [shaped(TILES, 128), shaped(1, ROWS - 1)], (tails, scalars, lines, tiled, grad, first_own, first_one, first_two, first_three)
    )
    return updated.reshape(features), widths.reshape(ROWS - 1)


def solution(mesh):
    in_specs = (P("event", "feat"), P("event"), P("feat"), P())
    out_specs = (P("feat"), P())
    return jax.shard_map(on_device, mesh=mesh, in_specs=in_specs, out_specs=out_specs, check_vma=False)
```
